256 devices in a mesh: gx: 16 (over y_hi, z), gy: 16 (over y_lo, x, core).
Axes of the slice: x: 4, y: 4 (y_hi: 2, y_lo: 2; y = y_hi * 2 + y_lo), z: 8, core: 2. Of those that a mesh axis runs over, the one named last changes fastest.
Arguments:
- velocity: float32 [3, 6, 512, 2048], P(None, None, 'gx', 'gy'), may hold values from -6 to 6
- stress: float32 [6, 6, 512, 2048], P(None, None, 'gx', 'gy'), may hold values from -6 to 6
- lame_first: float32 [6, 512, 2048], P(None, 'gx', 'gy'), may hold values from 0.3 to 1
- shear: float32 [6, 512, 2048], P(None, 'gx', 'gy'), may hold values from 0.2 to 0.6
- buoyancy: float32 [6, 512, 2048], P(None, 'gx', 'gy'), may hold values from 0.5 to 1.5
- fwd_strain: bfloat16 [6, 6, 512, 2048], P(None, None, 'gx', 'gy'), may hold values from -6 to 6
- fwd_accel: bfloat16 [3, 6, 512, 2048], P(None, None, 'gx', 'gy'), may hold values from -6 to 6
- kernels: float32 [3, 6, 512, 2048], P(None, None, 'gx', 'gy'), may hold values from -6 to 6
- station_trace: float32 [131072, 6], P(('gx', 'gy')), may hold values from -6 to 6
- station_tile: int32 [131072, 1], P(('gx', 'gy')), may hold values from 0 to 255; in each aligned block of 512 rows (0 to 511, 512 to 1023, ...) at most 4 rows name the same one
- station_cell: int32 [131072], P(('gx', 'gy')), may hold values from 0 to 24575
- station_count: int32 [256], P(('gx', 'gy')), may hold values from 1 to 512, 98304 in all
Outputs:
- velocity_out: float32 [3, 6, 512, 2048], P(None, None, 'gx', 'gy')
- stress_out: float32 [6, 6, 512, 2048], P(None, None, 'gx', 'gy')
- kernels_out: float32 [3, 6, 512, 2048], P(None, None, 'gx', 'gy')
The draws below stay inside these ranges and needn't reach their ends.
Inputs may be any that keep to these rules, and one draw needn't show every extreme that they name: `station_tile`: in each device's block of 512 rows no tile is named by more than 4 rows, and every tile is named somewhere.
All inputs are finite; a program needn't handle non-finite values. No bound on the sum of `station_count` on one device may be relied on, other than what follows from the above.
Results may differ from the reference program's by a relative error of at most 0.0003.
Values sent between devices are 32-bit elements; how exact they have to be, the bound alone decides.
A program may use at most 192 MiB of HBM per device.

```python
import math
import jax
import jax.numpy as jnp
import numpy as np
from jax import lax

CZ = 6
CX = 32
CY = 128
STEPS = 2
CAP = 4
STA_DEV = 512
NX = 512
NY = 2048
STATIONS = 131072
N_GX = 16
N_GY = 16


def touch_ends(result, key, least, top_value):
    longest = result.shape.index(max(result.shape))
    spots = []
    for shift in (0, 1):
        where = [jax.random.randint(jax.random.fold_in(key, axis), (), 0, length) for axis, length in enumerate(result.shape)]
        where[longest] = (where[longest] + shift) % result.shape[longest]
        spots.append(tuple(where))
    return result.at[spots[0]].set(least).at[spots[1]].set(top_value)


def block_scale(rng, shape, cuts, least, top_value):
    factor_of = 1.0
    for axis_at, shards_of in cuts:
        heights = jax.random.uniform(jax.random.fold_in(jax.random.fold_in(rng, 6), axis_at), (shards_of,), jnp.float32, least / len(cuts), top_value / len(cuts))
        factor_of = factor_of * jnp.repeat(jnp.exp(heights), shape[axis_at] // shards_of).reshape((-1,) + (1,) * (len(shape) - 1 - axis_at))
    return factor_of


def length_profile(number_of, total, most, skew):
    loads = [(1 << 20) // math.isqrt(standing ** skew) + 1 for standing in range(2, number_of + 1)]
    spare, given = total - most - (number_of - 1), [1] * (number_of - 1)
    while spare > 0:
        free = [i for i in range(number_of - 1) if given[i] < most]
        pool, left = sum([loads[i] for i in free]), spare
        for i in free:
            addition = min(most - given[i], max(1, left * loads[i] // pool), spare)
            given[i] = given[i] + addition
            spare = spare - addition
    return np.array([most] + given)


def ragged_sizes(stream_key, amount, total, limit, skew):
    if amount == 2:
        one = jax.random.randint(stream_key, (), max(1, total - limit), min(limit, total - 1) + 1)
        return jnp.stack([one, total - one])
    lengths = jnp.asarray(length_profile(amount, total, limit, skew), jnp.int32)
    couples = (amount - 1) // 2
    source_of, receiver = lengths[1:1 + 2 * couples:2], lengths[2:2 + 2 * couples:2]
    slack = jnp.minimum(source_of - 1, limit - receiver)
    moved = jax.random.randint(jax.random.fold_in(stream_key, 1), (couples,), 0, 1 << 20) % (slack + 1)
    lengths = lengths.at[1:1 + 2 * couples:2].set(source_of - moved).at[2:2 + 2 * couples:2].set(receiver + moved)
    return lengths[jax.random.permutation(jax.random.fold_in(stream_key, 2), amount)]


def deal_out(key, own, number, rows, number_of, top, limit, lean):
    ranking = jax.random.permutation(key, number_of)
    crowded, usual = portions_of(number_of, rows * top, limit, lean, True), portions_of(number_of, rows * top, limit, lean, False)
    places = jnp.arange(number_of)

    def named(lengths, rotation):
        used = int((lengths > 0).sum())
        fixed = max(1, used // 4)
        passed = fixed + (places - fixed + rotation * (used - fixed)) % max(1, number_of - fixed)
        return jnp.zeros((number_of,), jnp.int32).at[ranking[jnp.where(places < fixed, places, passed)]].set(jnp.asarray(lengths, jnp.int32))

    lengths = jnp.where(number % 4 == 0, named(crowded, number // 4), named(usual, number - number // 4 - 1))
    mixed = jax.random.permutation(jax.random.fold_in(own, 3), number_of)
    giver, receiver = mixed[0:number_of // 2 * 2:2], mixed[1:number_of // 2 * 2:2]
    slack = jnp.minimum(lengths[giver] - 1, limit - lengths[receiver]) // 2
    slack = jnp.where((giver == ranking[0]) | (receiver == ranking[0]) | (lengths[receiver] == 0), 0, jnp.maximum(slack, 0))
    passed = jax.random.randint(jax.random.fold_in(own, 4), (number_of // 2,), 0, 1 << 20) % (slack + 1)
    lengths = lengths.at[giver].add(-passed).at[receiver].add(passed)
    items = jnp.searchsorted(jnp.cumsum(lengths), jnp.arange(rows * top), side="right").astype(jnp.int32)
    listing = items.reshape(top, rows).T
    listing = listing[jax.random.permutation(jax.random.fold_in(own, 1), rows)]
    rotation = jax.random.randint(jax.random.fold_in(own, 2), (rows, 1), 0, top)
    return jnp.take_along_axis(listing, (jnp.arange(top)[None, :] + rotation) % top, axis=1)


def portions_of(amount, total, most, skew, full):
    loads = [(1 << 20) // math.isqrt(rank ** skew) + 1 for rank in range(1, amount + 1)]
    largest = most if full else min(most, max(-(-total // amount), total * loads[0] // sum(loads)))
    least = 1 if total - largest >= amount - 1 else 0
    given, surplus = [largest] + [least] * (amount - 1), total - largest - least * (amount - 1)
    while surplus > 0:
        movable = [i for i in range(1, amount) if given[i] < largest] or [i for i in range(1, amount) if given[i] < most]
        mass, budget = sum([loads[i] for i in movable]), surplus
        for i in movable:
            extra = min(most - given[i], max(1, budget * loads[i] // mass), surplus)
            given[i] = given[i] + extra
            surplus = surplus - extra
    return np.array(given)


def scatter_about(stream_key, extent, deviation, reach, split=(), kind=jnp.bfloat16):
    loudness = block_scale(stream_key, extent, split, -0.22, 0.18) if split else 1.0
    entries = jax.random.normal(stream_key, extent, jnp.float32) * deviation * loudness
    return jnp.minimum(jnp.maximum(entries, -reach), reach).astype(kind)


def setup_inputs(seed: int = 0) -> dict:
    arg_keys = jax.random.split(jax.random.key(seed), 13)
    velocity = scatter_about(arg_keys[0], (3, CZ, NX, NY), 1.0, 6.0, ((2, 16), (3, 16)), jnp.float32)
    stress = scatter_about(arg_keys[1], (6, CZ, NX, NY), 1.0, 6.0, ((2, 16), (3, 16)), jnp.float32)
    lame_first = jnp.clip(jnp.exp(math.log(1.0) - 1.2039728 * jax.random.uniform(arg_keys[2], (CZ, NX, NY), jnp.float32) ** block_scale(arg_keys[2], (CZ, NX, NY), ((1, 16), (2, 16)), -0.2, 0.2)), 0.3, 1.0)
    shear = jnp.clip(jnp.exp(math.log(0.6) - 1.0986123 * jax.random.uniform(arg_keys[3], (CZ, NX, NY), jnp.float32) ** block_scale(arg_keys[3], (CZ, NX, NY), ((1, 16), (2, 16)), -0.2, 0.2)), 0.2, 0.6)
    buoyancy = jnp.clip(jnp.exp(math.log(1.5) - 1.0986123 * jax.random.uniform(arg_keys[4], (CZ, NX, NY), jnp.float32) ** block_scale(arg_keys[4], (CZ, NX, NY), ((1, 16), (2, 16)), -0.2, 0.2)), 0.5, 1.5)
    fwd_strain = scatter_about(arg_keys[5], (6, CZ, NX, NY), 1.0, 6.0, ((2, 16), (3, 16)))
    fwd_accel = scatter_about(arg_keys[6], (3, CZ, NX, NY), 1.0, 6.0, ((2, 16), (3, 16)))
    kernels = scatter_about(arg_keys[7], (3, CZ, NX, NY), 1.0, 6.0, ((2, 16), (3, 16)), jnp.float32)
    station_trace = scatter_about(arg_keys[8], (STATIONS, 3 * STEPS), 1.0, 6.0, ((0, 256),), jnp.float32)
    station_tile_keys = jax.random.split(jax.random.fold_in(arg_keys[9], 1), STATIONS // STA_DEV)
    station_tile_turns = jax.random.permutation(jax.random.fold_in(arg_keys[9], 3), STATIONS // STA_DEV)
    station_tile = jax.vmap(lambda own, number: deal_out(jax.random.fold_in(arg_keys[9], 2), own, number, STA_DEV, N_GX * N_GY, 1, CAP, 2))(station_tile_keys, station_tile_turns).reshape((STATIONS, 1))
    station_cell = touch_ends(jax.random.randint(arg_keys[10], (STATIONS,), 0, CZ * CX * CY), jax.random.fold_in(arg_keys[10], 1), 0, (CZ * CX * CY) - 1).astype(jnp.int32)
    station_count = ragged_sizes(arg_keys[11], N_GX * N_GY, STATIONS * 3 // 4, STA_DEV, 1).astype(jnp.int32)
    return {"velocity": velocity, "stress": stress, "lame_first": lame_first, "shear": shear, "buoyancy": buoyancy, "fwd_strain": fwd_strain, "fwd_accel": fwd_accel, "kernels": kernels, "station_trace": station_trace, "station_tile": station_tile, "station_cell": station_cell, "station_count": station_count}


C_NEAR = 9.0 / 8.0
C_FAR = -1.0 / 24.0
STEP_DT = 0.25


def stencil(padded, axis, upward):
    count = padded.shape[axis] - 4

    def take(offset):
        return lax.slice_in_dim(padded, 2 + offset, 2 + offset + count, axis=axis)

    if upward:
        return C_NEAR * (take(1) - take(0)) + C_FAR * (take(2) - take(-1))
    return C_NEAR * (take(0) - take(-1)) + C_FAR * (take(1) - take(-2))


def derive(field, axis, upward):
    widths = [(0, 0)] * field.ndim
    widths[axis] = (2, 2)
    return stencil(jnp.pad(field, widths), axis, upward)


def reference(velocity, stress, lame_first, shear, buoyancy, fwd_strain, fwd_accel, kernels, station_trace, station_tile, station_cell, station_count):
    width_x = CX * N_GX
    width_y = CY * N_GY
    rows = jnp.arange(STA_DEV * N_GX * N_GY, dtype=jnp.int32)
    live = (rows % STA_DEV) < station_count[rows // STA_DEV]
    target = station_tile[:, 0]
    tile_x = target // N_GY
    tile_y = target % N_GY
    depth = station_cell // (CX * CY)
    local_x = (station_cell // CY) % CX
    local_y = station_cell % CY
    flat = (depth * (width_x * width_y) + (tile_x * CX + local_x) * width_y + tile_y * CY + local_y).astype(jnp.int32)
    values = jnp.where(live[:, None], station_trace, jnp.zeros_like(station_trace))
    vx, vy, vz = velocity[0], velocity[1], velocity[2]
    sxx, sxz, sxy, syy, syz, szz = stress[0], stress[1], stress[2], stress[3], stress[4], stress[5]
    for step in range(STEPS):
        source = jnp.zeros((3, CZ * width_x * width_y), station_trace.dtype)
        source = source.at[:, flat].add(values[:, 3 * step:3 * step + 3].T).reshape(3, CZ, width_x, width_y)
        rate_x = derive(sxx, 1, True) + derive(sxy, 2, False) + derive(sxz, 0, False)
        rate_y = derive(sxy, 1, False) + derive(syy, 2, True) + derive(syz, 0, False)
        rate_z = derive(sxz, 1, False) + derive(syz, 2, False) + derive(szz, 0, True)
        vx = vx + STEP_DT * buoyancy * (rate_x + source[0])
        vy = vy + STEP_DT * buoyancy * (rate_y + source[1])
        vz = vz + STEP_DT * buoyancy * (rate_z + source[2])
        exx = derive(vx, 1, False)
        eyy = derive(vy, 2, False)
        ezz = derive(vz, 0, False)
        gxy = derive(vx, 2, True) + derive(vy, 1, True)
        gxz = derive(vx, 0, True) + derive(vz, 1, True)
        gyz = derive(vy, 0, True) + derive(vz, 2, True)
        spread = exx + eyy + ezz
        sxx = sxx + STEP_DT * (lame_first * spread + 2.0 * shear * exx)
        syy = syy + STEP_DT * (lame_first * spread + 2.0 * shear * eyy)
        szz = szz + STEP_DT * (lame_first * spread + 2.0 * shear * ezz)
        sxy = sxy + STEP_DT * shear * gxy
        sxz = sxz + STEP_DT * shear * gxz
        syz = syz + STEP_DT * shear * gyz
    strain = fwd_strain.astype(jnp.float32)
    accel = fwd_accel.astype(jnp.float32)
    kernel_lame = kernels[0] - STEP_DT * (strain[0] + strain[3] + strain[5]) * spread
    kernel_shear = kernels[1] - 2.0 * STEP_DT * (strain[0] * exx + strain[3] * eyy + strain[5] * ezz + strain[2] * gxy + strain[1] * gxz + strain[4] * gyz)
    kernel_mass = kernels[2] - STEP_DT * (accel[0] * vx + accel[1] * vy + accel[2] * vz)
    return (jnp.stack([vx, vy, vz]), jnp.stack([sxx, sxz, sxy, syy, syz, szz]), jnp.stack([kernel_lame, kernel_shear, kernel_mass]))
```

```python
import functools

import jax
import jax.numpy as jnp
from jax import lax
from jax.experimental import pallas as pl
from jax.experimental.pallas import tpu as pltpu
from jax.sharding import PartitionSpec as P

STEPS = 2
CAP = 4
C_NEAR = 9.0 / 8.0
C_FAR = -1.0 / 24.0
STEP_DT = 0.25
MESH = pl.DeviceIdType.MESH

LANES = 128
FEATURES = 8
MARGIN = 8
ZPAD = 2
SXX, SXZ, SXY, SYY, SYZ, SZZ = range(6)
STRESS_X = (SXX, SXZ, SXY)
STRESS_Y = (SXY, SYY, SYZ)
SPEED_ALL = (0, 1, 2)
EXCHANGES = 2 * STEPS


def pieces(value):
    high = value.astype(jnp.bfloat16)
    rest = value - high.astype(jnp.float32)
    middle = rest.astype(jnp.bfloat16)
    low = (rest - middle.astype(jnp.float32)).astype(jnp.bfloat16)
    return high, middle, low


def dot_nt(left, right):
    return lax.dot_general(left, right, (((1,), (1,)), ((), ())), preferred_element_type=jnp.float32)


def kernel(
    n_x,
    n_y,
    vel_in,
    str_in,
    lame_in,
    shear_in,
    buoy_in,
    strain_in,
    accel_in,
    kern_in,
    trace_in,
    tile_in,
    cell_in,
    count,
    vel_out,
    str_out,
    kern_out,
    speed,
    tension,
    lame,
    shear,
    buoy,
    strain,
    accel,
    kern,
    trace,
    tile,
    cell,
    source,
    payload,
    packed,
    first_hop,
    second_hop,
    spot_rows,
    spot_cols,
    x_send,
    x_recv,
    y_send,
    y_recv,
    in_sem,
    out_sem,
    hop_send,
    hop_recv,
    face_send,
    face_recv,
):
    depth, width = buoy.shape[0], buoy.shape[1]
    rows = trace.shape[1]
    tiles = n_x * n_y
    gx, gy = lax.axis_index("gx"), lax.axis_index("gy")
    inner = pl.ds(MARGIN, width)
    planes = pl.ds(ZPAD, depth)

    loads = [
        pltpu.make_async_copy(src, dst, in_sem.at[i])
        for i, (src, dst) in enumerate(
            (
                (trace_in, trace),
                (tile_in, tile),
                (cell_in, cell),
                (str_in, tension.at[:, planes, inner, :]),
                (vel_in, speed.at[:, planes, inner, :]),
                (buoy_in, buoy),
                (lame_in, lame),
                (shear_in, shear),
                (strain_in, strain),
                (accel_in, accel),
                (kern_in, kern),
            )
        )
    ]
    for load in loads:
        load.start()

    barrier = pltpu.get_barrier_semaphore()

    def greet_x(i, _):
        pl.semaphore_signal(barrier, inc=1, device_id=(lax.rem(gx + i, n_x), gy), device_id_type=MESH)
        return 0

    def greet_y(i, _):
        pl.semaphore_signal(barrier, inc=1, device_id=(gx, lax.rem(gy + i, n_y)), device_id_type=MESH)
        return 0

    lax.fori_loop(1, n_x, greet_x, 0)
    lax.fori_loop(1, n_y, greet_y, 0)

    blank = jnp.zeros((ZPAD, width, LANES), jnp.float32)
    for ref, comps in ((speed, SPEED_ALL), (tension, (SXZ, SYZ, SZZ))):
        for comp in comps:
            ref[comp, pl.ds(0, ZPAD), inner, :] = blank
            ref[comp, pl.ds(ZPAD + depth, ZPAD), inner, :] = blank

    for load in loads[:3]:
        load.wait()
    names = tile[...]
    line = lax.broadcasted_iota(jnp.int32, (tiles, rows), 0)
    named = (line == names).astype(jnp.float32)
    named_16 = named.astype(jnp.bfloat16)
    earlier = (
        lax.broadcasted_iota(jnp.int32, (rows, rows), 0) < lax.broadcasted_iota(jnp.int32, (rows, rows), 1)
    ).astype(jnp.float32).astype(jnp.bfloat16)
    ahead = jnp.dot(named_16, earlier, preferred_element_type=jnp.float32)
    slot = jnp.sum(named * ahead, axis=0, keepdims=True)
    live = lax.broadcasted_iota(jnp.int32, (1, rows), 1) < count[0]
    cells = cell[...]
    samples = trace.shape[0]
    payload[pl.ds(0, samples), :] = jnp.where(live, trace[...], 0.0)
    payload[pl.ds(samples, 1), :] = (cells // LANES).astype(jnp.float32)
    payload[pl.ds(samples + 1, 1), :] = (cells % LANES).astype(jnp.float32)
    load_all = payload[...]
    parts = [jnp.where(slot == float(s), load_all, 0.0) for s in range(CAP)]
    parts.append(jnp.zeros((LANES - CAP * FEATURES, rows), jnp.float32))
    bundle = jnp.concatenate(parts, axis=0)
    outgoing = sum(dot_nt(named_16, piece) for piece in pieces(bundle))
    packed[...] = outgoing.reshape(n_x, n_y, 1, LANES)

    lane = lax.broadcasted_iota(jnp.int32, (width, LANES), 1)

    def face_copies(phase):
        up_x = (lax.rem(gx + 1, n_x), gy)
        down_x = (lax.rem(gx + n_x - 1, n_x), gy)
        up_y = (gx, lax.rem(gy + 1, n_y))
        down_y = (gx, lax.rem(gy + n_y - 1, n_y))
        return [
            pltpu.make_async_remote_copy(
                src_ref=send.at[phase, side],
                dst_ref=recv.at[phase, side],
                send_sem=face_send.at[phase, k],
                recv_sem=face_recv.at[phase, k],
                device_id=target,
                device_id_type=MESH,
            )
            for k, (send, recv, side, target) in enumerate(
                (
                    (y_send, y_recv, 0, down_y),
                    (y_send, y_recv, 1, up_y),
                    (x_send, x_recv, 0, down_x),
                    (x_send, x_recv, 1, up_x),
                )
            )
        ]

    def pack_faces(phase, ref, comps_x, comps_y):
        for k, comp in enumerate(comps_x):
            def rows_of(z, _, k=k, comp=comp):
                at = k * depth + z
                x_send[phase, 0, at] = ref[comp, z + ZPAD, pl.ds(MARGIN, 2), :]
                x_send[phase, 1, at] = ref[comp, z + ZPAD, pl.ds(MARGIN + width - 2, 2), :]
                return 0

            lax.fori_loop(0, depth, rows_of, 0, unroll=True)
        carried = (jnp.zeros((width, LANES), jnp.float32),) * 2
        for k, comp in enumerate(comps_y):
            def strip(z, carry, k=k, comp=comp):
                start = 2 * (k * depth + z)
                turned = pltpu.roll(ref[comp, z + ZPAD, inner, :], start + 2, 1)
                return (
                    jnp.where(lane >= start + 2, turned, carry[0]),
                    jnp.where(lane >= start, turned, carry[1]),
                )

            carried = lax.fori_loop(0, depth, strip, carried, unroll=True)
        y_send[phase, 0] = carried[0]
        y_send[phase, 1] = carried[1]

    def take_faces(phase, ref, comps_x):
        for copy in face_copies(phase):
            copy.wait_recv()

        @pl.when(gy == n_y - 1)
        def _():
            y_recv[phase, 0] = jnp.zeros((width, LANES), jnp.float32)

        @pl.when(gy == 0)
        def _():
            y_recv[phase, 1] = jnp.zeros((width, LANES), jnp.float32)

        @pl.when(gx == n_x - 1)
        def _():
            x_recv[phase, 0] = jnp.zeros(x_recv.shape[2:], jnp.float32)

        @pl.when(gx == 0)
        def _():
            x_recv[phase, 1] = jnp.zeros(x_recv.shape[2:], jnp.float32)

        for k, comp in enumerate(comps_x):
            def rows_of(z, _, k=k, comp=comp):
                at = k * depth + z
                ref[comp, z + ZPAD, pl.ds(MARGIN + width, 2), :] = x_recv[phase, 0, at]
                ref[comp, z + ZPAD, pl.ds(MARGIN - 2, 2), :] = x_recv[phase, 1, at]
                return 0

            lax.fori_loop(0, depth, rows_of, 0, unroll=True)

    def along_z(ref, comp, z, upward):
        def at(offset):
            return ref[comp, z + ZPAD + offset, inner, :]

        return difference(at, upward)

    def along_x(ref, comp, z, upward):
        def at(offset):
            return ref[comp, z + ZPAD, pl.ds(MARGIN + offset, width), :]

        return difference(at, upward)

    def along_y(phase, ref, comp, k, z, upward):
        start = 2 * (k * depth + z) + 2
        side = jnp.where(lane >= start, y_recv[phase, 0], y_recv[phase, 1])
        side = pltpu.roll(side, LANES - start, 1)
        centre = ref[comp, z + ZPAD, inner, :]

        def at(offset):
            if offset == 0:
                return centre
            if offset > 0:
                return pltpu.roll(jnp.where(lane < offset, side, centre), LANES - offset, 1)
            return pltpu.roll(jnp.where(lane >= LANES + offset, side, centre), -offset, 1)

        return difference(at, upward)

    def difference(at, upward):
        if upward:
            return C_NEAR * (at(1) - at(0)) + C_FAR * (at(2) - at(-1))
        return C_NEAR * (at(0) - at(-1)) + C_FAR * (at(1) - at(-2))

    def push_speed(phase):
        def plane(z, _):
            rate_x = (
                along_x(tension, SXX, z, True)
                + along_y(phase, tension, SXY, 0, z, False)
                + along_z(tension, SXZ, z, False)
            )
            rate_y = (
                along_x(tension, SXY, z, False)
                + along_y(phase, tension, SYY, 1, z, True)
                + along_z(tension, SYZ, z, False)
            )
            rate_z = (
                along_x(tension, SXZ, z, False)
                + along_y(phase, tension, SYZ, 2, z, False)
                + along_z(tension, SZZ, z, True)
            )
            factor = STEP_DT * buoy[z]
            for k, rate in enumerate((rate_x, rate_y, rate_z)):
                if phase > 0:
                    rate = rate + source[3 * (phase // 2) + k, z]
                speed[k, z + ZPAD, inner, :] = speed[k, z + ZPAD, inner, :] + factor * rate
            return 0

        lax.fori_loop(0, depth, plane, 0, unroll=True)

    def add_source(step):
        def plane(z, _):
            factor = STEP_DT * buoy[z]
            for k in range(3):
                speed[k, z + ZPAD, inner, :] = speed[k, z + ZPAD, inner, :] + factor * source[3 * step + k, z]
            return 0

        lax.fori_loop(0, depth, plane, 0, unroll=True)

    def push_stress(phase, last):
        def plane(z, _):
            exx = along_x(speed, 0, z, False)
            eyy = along_y(phase, speed, 1, 1, z, False)
            ezz = along_z(speed, 2, z, False)
            gxy = along_y(phase, speed, 0, 0, z, True) + along_x(speed, 1, z, True)
            gxz = along_z(speed, 0, z, True) + along_x(speed, 2, z, True)
            gyz = along_z(speed, 1, z, True) + along_y(phase, speed, 2, 2, z, True)
            spread = exx + eyy + ezz
            stiff = STEP_DT * shear[z]
            common = STEP_DT * lame[z] * spread
            for comp, change in (
                (SXX, common + 2.0 * stiff * exx),
                (SYY, common + 2.0 * stiff * eyy),
                (SZZ, common + 2.0 * stiff * ezz),
                (SXY, stiff * gxy),
                (SXZ, stiff * gxz),
                (SYZ, stiff * gyz),
            ):
                tension[comp, z + ZPAD, inner, :] = tension[comp, z + ZPAD, inner, :] + change
            if last:
                f = [strain[comp, z].astype(jnp.float32) for comp in range(6)]
                a = [accel[comp, z].astype(jnp.float32) for comp in range(3)]
                v = [speed[comp, z + ZPAD, inner, :] for comp in range(3)]
                kern[0, z] = kern[0, z] - STEP_DT * (f[SXX] + f[SYY] + f[SZZ]) * spread
                kern[1, z] = kern[1, z] - 2.0 * STEP_DT * (
                    f[SXX] * exx + f[SYY] * eyy + f[SZZ] * ezz + f[SXY] * gxy + f[SXZ] * gxz + f[SYZ] * gyz
                )
                kern[2, z] = kern[2, z] - STEP_DT * (a[0] * v[0] + a[1] * v[1] + a[2] * v[2])
            return 0

        lax.fori_loop(0, depth, plane, 0, unroll=True)

    loads[3].wait()
    pack_faces(0, tension, STRESS_X, STRESS_Y)
    pl.semaphore_wait(barrier, n_x + n_y - 2)

    def hop_x(i):
        to = lax.rem(gx + i, n_x)
        return pltpu.make_async_remote_copy(
            src_ref=packed.at[to],
            dst_ref=first_hop.at[:, gx],
            send_sem=hop_send.at[0, i],
            recv_sem=hop_recv.at[0, i],
            device_id=(to, gy),
            device_id_type=MESH,
        )

    def hop_y(i):
        to = lax.rem(gy + i, n_y)
        return pltpu.make_async_remote_copy(
            src_ref=first_hop.at[to],
            dst_ref=second_hop.at[gy],
            send_sem=hop_send.at[1, i],
            recv_sem=hop_recv.at[1, i],
            device_id=(gx, to),
            device_id_type=MESH,
        )

    def start(make):
        def run(i, _):
            make(i).start()
            return 0

        return run

    def landed(make):
        def run(i, _):
            make(i).wait_recv()
            return 0

        return run

    def sent(make):
        def run(i, _):
            make(i).wait_send()
            return 0

        return run

    own_x = pltpu.make_async_copy(packed.at[gx], first_hop.at[:, gx], hop_recv.at[0, 0])
    own_y = pltpu.make_async_copy(first_hop.at[gy], second_hop.at[gy], hop_recv.at[1, 0])
    lax.fori_loop(1, n_x, start(hop_x), 0)
    own_x.start()
    for copy in face_copies(0):
        copy.start()
    own_x.wait()
    lax.fori_loop(1, n_x, landed(hop_x), 0)
    lax.fori_loop(1, n_y, start(hop_y), 0)
    own_y.start()

    take_faces(0, tension, STRESS_X)
    loads[4].wait()
    loads[5].wait()
    push_speed(0)

    own_y.wait()
    lax.fori_loop(1, n_y, landed(hop_y), 0)
    arrived = second_hop[...].reshape(tiles, LANES).T
    row_of = lax.broadcasted_iota(jnp.int32, (depth * width, tiles), 0).astype(jnp.float32)
    col_of = lax.broadcasted_iota(jnp.int32, (LANES, tiles), 0).astype(jnp.float32)
    values = []
    for s in range(CAP):
        group = arrived[s * FEATURES : (s + 1) * FEATURES, :]
        span = pl.ds(s * tiles, tiles)
        spot_rows[:, span] = (row_of == group[samples : samples + 1]).astype(jnp.float32).astype(jnp.bfloat16)
        spot_cols[:, span] = (col_of == group[samples + 1 : samples + 2]).astype(jnp.float32).astype(jnp.bfloat16)
        values.append(group)
    amounts = pieces(jnp.concatenate(values, axis=1))

    def lay_sources(step):
        columns = spot_cols[...]
        total = jnp.zeros((depth * width, 3 * LANES), jnp.float32)
        for amount in amounts:
            spread = [columns * amount[3 * step + k : 3 * step + k + 1, :] for k in range(3)]
            total = total + dot_nt(spot_rows[...], jnp.concatenate(spread, axis=0))
        for k in range(3):
            source[3 * step + k] = total[:, k * LANES : (k + 1) * LANES].reshape(depth, width, LANES)

    lay_sources(0)
    add_source(0)
    for step in range(STEPS):
        phase = 2 * step + 1
        pack_faces(phase, speed, SPEED_ALL, SPEED_ALL)
        for copy in face_copies(phase):
            copy.start()
        if step + 1 < STEPS:
            lay_sources(step + 1)
            loads[6].wait()
            loads[7].wait()
        else:
            out_speed = pltpu.make_async_copy(speed.at[:, planes, inner, :], vel_out, out_sem.at[0])
            out_speed.start()
            for load in loads[8:]:
                load.wait()
        take_faces(phase, speed, SPEED_ALL)
        push_stress(phase, step + 1 == STEPS)
        if step + 1 < STEPS:
            phase = phase + 1
            pack_faces(phase, tension, STRESS_X, STRESS_Y)
            for copy in face_copies(phase):
                copy.start()
            take_faces(phase, tension, STRESS_X)
            push_speed(phase)
    out_rest = [
        pltpu.make_async_copy(tension.at[:, planes, inner, :], str_out, out_sem.at[1]),
        pltpu.make_async_copy(kern, kern_out, out_sem.at[2]),
    ]
    for copy in out_rest:
        copy.start()
    lax.fori_loop(1, n_x, sent(hop_x), 0)
    lax.fori_loop(1, n_y, sent(hop_y), 0)
    for phase in range(EXCHANGES):
        for copy in face_copies(phase):
            copy.wait_send()
    out_speed.wait()
    for copy in out_rest:
        copy.wait()


def body(
    velocity,
    stress,
    lame_first,
    shear,
    buoyancy,
    fwd_strain,
    fwd_accel,
    kernels,
    station_trace,
    station_tile,
    station_cell,
    station_count,
):
    n_x, n_y = lax.axis_size("gx"), lax.axis_size("gy")
    depth, width, lanes = buoyancy.shape
    rows = station_trace.shape[0]
    tiles = n_x * n_y
    strips = 3 * depth
    padded = (depth + 2 * ZPAD, width + 2 * MARGIN, lanes)
    f32, b16 = jnp.float32, jnp.bfloat16
    far = pl.BlockSpec(memory_space=pltpu.HBM)
    return pl.pallas_call(
        functools.partial(kernel, n_x, n_y),
        out_shape=[
            jax.ShapeDtypeStruct(velocity.shape, f32),
            jax.ShapeDtypeStruct(stress.shape, f32),
            jax.ShapeDtypeStruct(kernels.shape, f32),
        ],
        in_specs=[far] * 11 + [pl.BlockSpec(memory_space=pltpu.SMEM)],
        out_specs=[far] * 3,
        scratch_shapes=[
            pltpu.VMEM((3, *padded), f32),
            pltpu.VMEM((6, *padded), f32),
            pltpu.VMEM(buoyancy.shape, f32),
            pltpu.VMEM(buoyancy.shape, f32),
            pltpu.VMEM(buoyancy.shape, f32),
            pltpu.VMEM(fwd_strain.shape, b16),
            pltpu.VMEM(fwd_accel.shape, b16),
            pltpu.VMEM(kernels.shape, f32),
            pltpu.VMEM(station_trace.shape[::-1], f32),
            pltpu.VMEM((1, rows), jnp.int32),
            pltpu.VMEM((1, rows), jnp.int32),
            pltpu.VMEM((3 * STEPS, *buoyancy.shape), f32),
            pltpu.VMEM((FEATURES, rows), f32),
            pltpu.VMEM((n_x, n_y, 1, lanes), f32),
            pltpu.VMEM((n_y, n_x, 1, lanes), f32),
            pltpu.VMEM((n_y, n_x, 1, lanes), f32),
            pltpu.VMEM((depth * width, CAP * tiles), b16),
            pltpu.VMEM((lanes, CAP * tiles), b16),
            pltpu.VMEM((EXCHANGES, 2, strips, 2, lanes), f32),
            pltpu.VMEM((EXCHANGES, 2, strips, 2, lanes), f32),
            pltpu.VMEM((EXCHANGES, 2, width, lanes), f32),
            pltpu.VMEM((EXCHANGES, 2, width, lanes), f32),
            pltpu.SemaphoreType.DMA((11,)),
            pltpu.SemaphoreType.DMA((3,)),
            pltpu.SemaphoreType.DMA((2, max(n_x, n_y))),
            pltpu.SemaphoreType.DMA((2, max(n_x, n_y))),
            pltpu.SemaphoreType.DMA((EXCHANGES, 4)),
            pltpu.SemaphoreType.DMA((EXCHANGES, 4)),
        ],
        compiler_params=pltpu.CompilerParams(
            collective_id=0, has_side_effects=True, vmem_limit_bytes=60 * 1024 * 1024
        ),
    )(
        velocity,
        stress,
        lame_first,
        shear,
        buoyancy,
        fwd_strain,
        fwd_accel,
        kernels,
        station_trace.T,
        station_tile.reshape(1, rows),
        station_cell.reshape(1, rows),
        station_count,
    )


def solution(mesh):
    tiled = P(None, None, "gx", "gy")
    plane = P(None, "gx", "gy")
    listed = ("gx", "gy")
    return jax.shard_map(
        body,
        mesh=mesh,
        in_specs=(
            tiled,
            tiled,
            plane,
            plane,
            plane,
            tiled,
            tiled,
            tiled,
            P(listed, None),
            P(listed, None),
            P(listed),
            P(listed),
        ),
        out_specs=(tiled, tiled, tiled),
        check_vma=False,
    )
```

```python
import functools

import jax
import jax.numpy as jnp
from jax import lax
from jax.experimental import pallas as pl
from jax.experimental.pallas import tpu as pltpu
from jax.sharding import PartitionSpec as P

STEPS = 2
CAP = 4
C_NEAR = 9.0 / 8.0
C_FAR = -1.0 / 24.0
STEP_DT = 0.25
MESH = pl.DeviceIdType.MESH

LANES = 128
FEATURES = 8
MARGIN = 8
ZPAD = 2
SXX, SXZ, SXY, SYY, SYZ, SZZ = range(6)
STRESS_X = (SXX, SXZ, SXY)
STRESS_Y = (SXY, SYY, SYZ)
SPEED_ALL = (0, 1, 2)
EXCHANGES = 2 * STEPS


def pieces(value):
    high = value.astype(jnp.bfloat16)
    rest = value - high.astype(jnp.float32)
    middle = rest.astype(jnp.bfloat16)
    low = (rest - middle.astype(jnp.float32)).astype(jnp.bfloat16)
    return high, middle, low


def dot_nt(left, right):
    return lax.dot_general(left, right, (((1,), (1,)), ((), ())), preferred_element_type=jnp.float32)


def kernel(
    n_x,
    n_y,
    vel_in,
    str_in,
    lame_in,
    shear_in,
    buoy_in,
    strain_in,
    accel_in,
    kern_in,
    trace_in,
    tile_in,
    cell_in,
    count,
    vel_out,
    str_out,
    kern_out,
    speed,
    tension,
    lame,
    shear,
    buoy,
    strain,
    accel,
    kern,
    trace,
    tile,
    cell,
    source,
    payload,
    packed,
    first_hop,
    regrouped,
    second_hop,
    spot_rows,
    spot_cols,
    x_send,
    x_recv,
    y_send,
    y_recv,
    in_sem,
    hop_send,
    hop_recv,
    face_send,
    face_recv,
):
    depth, width = buoy.shape[0], buoy.shape[1]
    rows = trace.shape[1]
    tiles = n_x * n_y
    gx, gy = lax.axis_index("gx"), lax.axis_index("gy")
    inner = pl.ds(MARGIN, width)
    planes = pl.ds(ZPAD, depth)

    loads = [
        pltpu.make_async_copy(src, dst, in_sem.at[i])
        for i, (src, dst) in enumerate(
            (
                (trace_in, trace),
                (tile_in, tile),
                (cell_in, cell),
                (str_in, tension.at[:, planes, inner, :]),
                (vel_in, speed.at[:, planes, inner, :]),
                (buoy_in, buoy),
                (lame_in, lame),
                (shear_in, shear),
                (strain_in, strain),
                (accel_in, accel),
                (kern_in, kern),
            )
        )
    ]
    for load in loads:
        load.start()

    half_x, half_y = n_x // 2, n_y // 2
    my_a = lax.rem(gx, half_x) * 2 + lax.rem(gy, 2)
    my_b = (gx // half_x) * half_y + gy // 2
    size_a, size_b = n_x, n_y

    def at_a(a):
        return ((gx // half_x) * half_x + a // 2, (gy // 2) * 2 + lax.rem(a, 2))

    def at_b(b):
        return ((b // half_y) * half_x + lax.rem(gx, half_x), lax.rem(b, half_y) * 2 + lax.rem(gy, 2))

    up_x = (lax.rem(gx + 1, n_x), gy)
    down_x = (lax.rem(gx + n_x - 1, n_x), gy)
    up_y = (gx, lax.rem(gy + 1, n_y))
    down_y = (gx, lax.rem(gy + n_y - 1, n_y))
    around = (up_x, down_x, up_y, down_y)

    barrier = pltpu.get_barrier_semaphore()

    def greet(place, me, size):
        def run(i, _):
            pl.semaphore_signal(barrier, inc=1, device_id=place(lax.rem(me + i, size)), device_id_type=MESH)
            return 0

        lax.fori_loop(1, size, run, 0)

    greet(at_a, my_a, size_a)
    greet(at_b, my_b, size_b)
    for target in around:
        pl.semaphore_signal(barrier, inc=1, device_id=target, device_id_type=MESH)

    blank = jnp.zeros((ZPAD, width, LANES), jnp.float32)
    for ref, comps in ((speed, SPEED_ALL), (tension, (SXZ, SYZ, SZZ))):
        for comp in comps:
            ref[comp, pl.ds(0, ZPAD), inner, :] = blank
            ref[comp, pl.ds(ZPAD + depth, ZPAD), inner, :] = blank

    for load in loads[:3]:
        load.wait()
    names = tile[...]
    line = lax.broadcasted_iota(jnp.int32, (tiles, rows), 0)
    named = (line == names).astype(jnp.float32)
    named_16 = named.astype(jnp.bfloat16)
    earlier = (
        lax.broadcasted_iota(jnp.int32, (rows, rows), 0) < lax.broadcasted_iota(jnp.int32, (rows, rows), 1)
    ).astype(jnp.float32).astype(jnp.bfloat16)
    ahead = jnp.dot(named_16, earlier, preferred_element_type=jnp.float32)
    slot = jnp.sum(named * ahead, axis=0, keepdims=True)
    live = lax.broadcasted_iota(jnp.int32, (1, rows), 1) < count[0]
    cells = cell[...]
    samples = trace.shape[0]
    payload[pl.ds(0, samples), :] = jnp.where(live, trace[...], 0.0)
    payload[pl.ds(samples, 1), :] = (cells // LANES).astype(jnp.float32)
    payload[pl.ds(samples + 1, 1), :] = (cells % LANES).astype(jnp.float32)
    load_all = payload[...]
    at_x, at_y = names // n_y, lax.rem(names, n_y)
    to_a = lax.rem(at_x, half_x) * 2 + lax.rem(at_y, 2)
    to_b = (at_x // half_x) * half_y + at_y // 2
    row_to = to_a * (size_b // CAP) + to_b // CAP
    group = lax.rem(to_b, CAP).astype(jnp.float32) * CAP + slot
    spread = [jnp.where((group == float(g)) & (slot < CAP), load_all, 0.0) for g in range(CAP * CAP)]
    bundle = jnp.concatenate(spread, axis=0)
    lines = size_a * size_b // CAP
    aimed = (lax.broadcasted_iota(jnp.int32, (lines, rows), 0) == row_to).astype(jnp.float32).astype(jnp.bfloat16)
    outgoing = sum(dot_nt(aimed, piece) for piece in pieces(bundle))
    packed[...] = outgoing.reshape(size_a, size_b // CAP, 1, LANES)

    lane = lax.broadcasted_iota(jnp.int32, (width, LANES), 1)

    def face_copies(phase):
        return [
            pltpu.make_async_remote_copy(
                src_ref=send.at[phase, side],
                dst_ref=recv.at[phase, side],
                send_sem=face_send.at[phase, k],
                recv_sem=face_recv.at[phase, k],
                device_id=target,
                device_id_type=MESH,
            )
            for k, (send, recv, side, target) in enumerate(
                (
                    (y_send, y_recv, 0, down_y),
                    (y_send, y_recv, 1, up_y),
                    (x_send, x_recv, 0, down_x),
                    (x_send, x_recv, 1, up_x),
                )
            )
        ]

    def pack_faces(phase, ref, comps_x, comps_y):
        for k, comp in enumerate(comps_x):
            def rows_of(z, _, k=k, comp=comp):
                at = k * depth + z
                x_send[phase, 0, at] = ref[comp, z + ZPAD, pl.ds(MARGIN, 2), :]
                x_send[phase, 1, at] = ref[comp, z + ZPAD, pl.ds(MARGIN + width - 2, 2), :]
                return 0

            lax.fori_loop(0, depth, rows_of, 0, unroll=True)
        carried = (jnp.zeros((width, LANES), jnp.float32),) * 2
        for k, comp in enumerate(comps_y):
            def strip(z, carry, k=k, comp=comp):
                start = 2 * (k * depth + z)
                turned = pltpu.roll(ref[comp, z + ZPAD, inner, :], start + 2, 1)
                return (
                    jnp.where(lane >= start + 2, turned, carry[0]),
                    jnp.where(lane >= start, turned, carry[1]),
                )

            carried = lax.fori_loop(0, depth, strip, carried, unroll=True)
        y_send[phase, 0] = carried[0]
        y_send[phase, 1] = carried[1]

    def take_faces(phase, ref, comps_x):
        for copy in face_copies(phase):
            copy.wait_recv()

        @pl.when(gy == n_y - 1)
        def _():
            y_recv[phase, 0] = jnp.zeros((width, LANES), jnp.float32)

        @pl.when(gy == 0)
        def _():
            y_recv[phase, 1] = jnp.zeros((width, LANES), jnp.float32)

        @pl.when(gx == n_x - 1)
        def _():
            x_recv[phase, 0] = jnp.zeros(x_recv.shape[2:], jnp.float32)

        @pl.when(gx == 0)
        def _():
            x_recv[phase, 1] = jnp.zeros(x_recv.shape[2:], jnp.float32)

        for k, comp in enumerate(comps_x):
            def rows_of(z, _, k=k, comp=comp):
                at = k * depth + z
                ref[comp, z + ZPAD, pl.ds(MARGIN + width, 2), :] = x_recv[phase, 0, at]
                ref[comp, z + ZPAD, pl.ds(MARGIN - 2, 2), :] = x_recv[phase, 1, at]
                return 0

            lax.fori_loop(0, depth, rows_of, 0, unroll=True)

    def along_z(ref, comp, z, upward):
        def at(offset):
            return ref[comp, z + ZPAD + offset, inner, :]

        return difference(at, upward)

    def along_x(ref, comp, z, upward):
        def at(offset):
            return ref[comp, z + ZPAD, pl.ds(MARGIN + offset, width), :]

        return difference(at, upward)

    def along_y(phase, ref, comp, k, z, upward):
        start = 2 * (k * depth + z) + 2
        side = jnp.where(lane >= start, y_recv[phase, 0], y_recv[phase, 1])
        side = pltpu.roll(side, LANES - start, 1)
        centre = ref[comp, z + ZPAD, inner, :]

        def at(offset):
            if offset == 0:
                return centre
            if offset > 0:
                return pltpu.roll(jnp.where(lane < offset, side, centre), LANES - offset, 1)
            return pltpu.roll(jnp.where(lane >= LANES + offset, side, centre), -offset, 1)

        return difference(at, upward)

    def difference(at, upward):
        if upward:
            return C_NEAR * (at(1) - at(0)) + C_FAR * (at(2) - at(-1))
        return C_NEAR * (at(0) - at(-1)) + C_FAR * (at(1) - at(-2))

    def push_speed(phase):
        def plane(z, _):
            rate_x = (
                along_x(tension, SXX, z, True)
                + along_y(phase, tension, SXY, 0, z, False)
                + along_z(tension, SXZ, z, False)
            )
            rate_y = (
                along_x(tension, SXY, z, False)
                + along_y(phase, tension, SYY, 1, z, True)
                + along_z(tension, SYZ, z, False)
            )
            rate_z = (
                along_x(tension, SXZ, z, False)
                + along_y(phase, tension, SYZ, 2, z, False)
                + along_z(tension, SZZ, z, True)
            )
            factor = STEP_DT * buoy[z]
            for k, rate in enumerate((rate_x, rate_y, rate_z)):
                if phase > 0:
                    rate = rate + source[3 * (phase // 2) + k, z]
                value = speed[k, z + ZPAD, inner, :] + factor * rate
                speed[k, z + ZPAD, inner, :] = value
                if phase == EXCHANGES - 2:
                    vel_out[k, z] = value
            return 0

        lax.fori_loop(0, depth, plane, 0, unroll=True)

    def add_source(step):
        def plane(z, _):
            factor = STEP_DT * buoy[z]
            for k in range(3):
                speed[k, z + ZPAD, inner, :] = speed[k, z + ZPAD, inner, :] + factor * source[3 * step + k, z]
            return 0

        lax.fori_loop(0, depth, plane, 0, unroll=True)

    def push_stress(phase, last):
        def plane(z, _):
            exx = along_x(speed, 0, z, False)
            eyy = along_y(phase, speed, 1, 1, z, False)
            ezz = along_z(speed, 2, z, False)
            gxy = along_y(phase, speed, 0, 0, z, True) + along_x(speed, 1, z, True)
            gxz = along_z(speed, 0, z, True) + along_x(speed, 2, z, True)
            gyz = along_z(speed, 1, z, True) + along_y(phase, speed, 2, 2, z, True)
            spread = exx + eyy + ezz
            stiff = STEP_DT * shear[z]
            common = STEP_DT * lame[z] * spread
            for comp, change in (
                (SXX, common + 2.0 * stiff * exx),
                (SYY, common + 2.0 * stiff * eyy),
                (SZZ, common + 2.0 * stiff * ezz),
                (SXY, stiff * gxy),
                (SXZ, stiff * gxz),
                (SYZ, stiff * gyz),
            ):
                value = tension[comp, z + ZPAD, inner, :] + change
                if last:
                    str_out[comp, z] = value
                else:
                    tension[comp, z + ZPAD, inner, :] = value
            if last:
                f = [strain[comp, z].astype(jnp.float32) for comp in range(6)]
                a = [accel[comp, z].astype(jnp.float32) for comp in range(3)]
                v = [speed[comp, z + ZPAD, inner, :] for comp in range(3)]
                kern_out[0, z] = kern[0, z] - STEP_DT * (f[SXX] + f[SYY] + f[SZZ]) * spread
                kern_out[1, z] = kern[1, z] - 2.0 * STEP_DT * (
                    f[SXX] * exx + f[SYY] * eyy + f[SZZ] * ezz + f[SXY] * gxy + f[SXZ] * gxz + f[SYZ] * gyz
                )
                kern_out[2, z] = kern[2, z] - STEP_DT * (a[0] * v[0] + a[1] * v[1] + a[2] * v[2])
            return 0

        lax.fori_loop(0, depth, plane, 0, unroll=True)

    loads[3].wait()
    pack_faces(0, tension, STRESS_X, STRESS_Y)
    pl.semaphore_wait(barrier, size_a + size_b - 2 + len(around))

    def hop_a(i):
        to = lax.rem(my_a + i, size_a)
        return pltpu.make_async_remote_copy(
            src_ref=packed.at[to],
            dst_ref=first_hop.at[lax.rem(my_a, CAP), :, my_a // CAP],
            send_sem=hop_send.at[0, i],
            recv_sem=hop_recv.at[0, i],
            device_id=at_a(to),
            device_id_type=MESH,
        )

    def hop_b(i):
        to = lax.rem(my_b + i, size_b)
        return pltpu.make_async_remote_copy(
            src_ref=regrouped.at[to // CAP, lax.rem(to, CAP)],
            dst_ref=second_hop.at[my_b],
            send_sem=hop_send.at[1, i],
            recv_sem=hop_recv.at[1, i],
            device_id=at_b(to),
            device_id_type=MESH,
        )

    def start(make):
        def run(i, _):
            make(i).start()
            return 0

        return run

    def landed(make):
        def run(i, _):
            make(i).wait_recv()
            return 0

        return run

    def sent(make):
        def run(i, _):
            make(i).wait_send()
            return 0

        return run

    lax.fori_loop(1, size_a, start(hop_a), 0)
    own_a = pltpu.make_async_copy(
        packed.at[my_a], first_hop.at[lax.rem(my_a, CAP), :, my_a // CAP], hop_recv.at[0, 0]
    )
    own_a.start()
    for copy in face_copies(0):
        copy.start()
    own_a.wait()
    lax.fori_loop(1, size_a, landed(hop_a), 0)
    heaps = [first_hop[p].reshape(lines // CAP, LANES) for p in range(CAP)]
    span = CAP * FEATURES
    lane_hop = lax.broadcasted_iota(jnp.int32, (lines // CAP, LANES), 1)
    for low in range(CAP):
        merged = None
        for p in range(CAP):
            shift = (span * (p - low)) % LANES
            turned = heaps[p] if shift == 0 else pltpu.roll(heaps[p], shift, 1)
            merged = turned if p == 0 else jnp.where(lane_hop >= span * p, turned, merged)
        regrouped[:, low] = merged.reshape(size_b // CAP, size_a // CAP, 1, LANES)
    lax.fori_loop(1, size_b, start(hop_b), 0)
    own_b = pltpu.make_async_copy(
        regrouped.at[my_b // CAP, lax.rem(my_b, CAP)], second_hop.at[my_b], hop_recv.at[1, 0]
    )
    own_b.start()

    take_faces(0, tension, STRESS_X)
    loads[4].wait()
    loads[5].wait()
    push_speed(0)

    own_b.wait()
    lax.fori_loop(1, size_b, landed(hop_b), 0)
    arrived = second_hop[...].reshape(lines, LANES)
    arrived = jnp.concatenate([arrived, pltpu.roll(arrived, LANES // 2, 1)], axis=0).T
    heap = LANES // 2 // FEATURES
    values = jnp.concatenate([arrived[g * FEATURES : (g + 1) * FEATURES] for g in range(heap)], axis=1)
    entries = CAP * tiles
    row_of = lax.broadcasted_iota(jnp.int32, (depth * width, entries), 0).astype(jnp.float32)
    col_of = lax.broadcasted_iota(jnp.int32, (LANES, entries), 0).astype(jnp.float32)
    spot_rows[...] = (row_of == values[samples : samples + 1]).astype(jnp.float32).astype(jnp.bfloat16)
    spot_cols[...] = (col_of == values[samples + 1 : samples + 2]).astype(jnp.float32).astype(jnp.bfloat16)
    amounts = pieces(values)

    def lay_sources(step):
        columns = spot_cols[...]
        total = jnp.zeros((depth * width, 3 * LANES), jnp.float32)
        for amount in amounts:
            spread = [columns * amount[3 * step + k : 3 * step + k + 1, :] for k in range(3)]
            total = total + dot_nt(spot_rows[...], jnp.concatenate(spread, axis=0))
        for k in range(3):
            source[3 * step + k] = total[:, k * LANES : (k + 1) * LANES].reshape(depth, width, LANES)

    lay_sources(0)
    add_source(0)
    for step in range(STEPS):
        phase = 2 * step + 1
        pack_faces(phase, speed, SPEED_ALL, SPEED_ALL)
        for copy in face_copies(phase):
            copy.start()
        if step + 1 < STEPS:
            lay_sources(step + 1)
            loads[6].wait()
            loads[7].wait()
        else:
            for load in loads[8:]:
                load.wait()
        take_faces(phase, speed, SPEED_ALL)
        push_stress(phase, step + 1 == STEPS)
        if step + 1 < STEPS:
            phase = phase + 1
            pack_faces(phase, tension, STRESS_X, STRESS_Y)
            for copy in face_copies(phase):
                copy.start()
            take_faces(phase, tension, STRESS_X)
            push_speed(phase)
    lax.fori_loop(1, size_a, sent(hop_a), 0)
    lax.fori_loop(1, size_b, sent(hop_b), 0)
    for phase in range(EXCHANGES):
        for copy in face_copies(phase):
            copy.wait_send()


def deliver(*refs):
    sources, targets, sems = refs[:3], refs[3:6], refs[6]
    copies = [pltpu.make_async_copy(src, dst, sems.at[i]) for i, (src, dst) in enumerate(zip(sources, targets))]
    for copy in copies:
        copy.start()
    for copy in copies:
        copy.wait()


def body(
    velocity,
    stress,
    lame_first,
    shear,
    buoyancy,
    fwd_strain,
    fwd_accel,
    kernels,
    station_trace,
    station_tile,
    station_cell,
    station_count,
):
    n_x, n_y = lax.axis_size("gx"), lax.axis_size("gy")
    depth, width, lanes = buoyancy.shape
    rows = station_trace.shape[0]
    tiles = n_x * n_y
    strips = 3 * depth
    padded = (depth + 2 * ZPAD, width + 2 * MARGIN, lanes)
    f32, b16 = jnp.float32, jnp.bfloat16
    far = pl.BlockSpec(memory_space=pltpu.HBM)
    results = pl.pallas_call(
        functools.partial(kernel, n_x, n_y),
        out_shape=[
            pltpu.VMEM(velocity.shape, f32),
            pltpu.VMEM(stress.shape, f32),
            pltpu.VMEM(kernels.shape, f32),
        ],
        in_specs=[far] * 11 + [pl.BlockSpec(memory_space=pltpu.SMEM)],
        out_specs=[pl.BlockSpec(memory_space=pltpu.VMEM)] * 3,
        scratch_shapes=[
            pltpu.VMEM((3, *padded), f32),
            pltpu.VMEM((6, *padded), f32),
            pltpu.VMEM(buoyancy.shape, f32),
            pltpu.VMEM(buoyancy.shape, f32),
            pltpu.VMEM(buoyancy.shape, f32),
            pltpu.VMEM(fwd_strain.shape, b16),
            pltpu.VMEM(fwd_accel.shape, b16),
            pltpu.VMEM(kernels.shape, f32),
            pltpu.VMEM(station_trace.shape[::-1], f32),
            pltpu.VMEM((1, rows), jnp.int32),
            pltpu.VMEM((1, rows), jnp.int32),
            pltpu.VMEM((3 * STEPS, *buoyancy.shape), f32),
            pltpu.VMEM((FEATURES, rows), f32),
            pltpu.VMEM((n_x, n_y // CAP, 1, lanes), f32),
            pltpu.VMEM((CAP, n_y // CAP, n_x // CAP, 1, lanes), f32),
            pltpu.VMEM((n_y // CAP, CAP, n_x // CAP, 1, lanes), f32),
            pltpu.VMEM((n_y, n_x // CAP, 1, lanes), f32),
            pltpu.VMEM((depth * width, CAP * tiles), b16),
            pltpu.VMEM((lanes, CAP * tiles), b16),
            pltpu.VMEM((EXCHANGES, 2, strips, 2, lanes), f32),
            pltpu.VMEM((EXCHANGES, 2, strips, 2, lanes), f32),
            pltpu.VMEM((EXCHANGES, 2, width, lanes), f32),
            pltpu.VMEM((EXCHANGES, 2, width, lanes), f32),
            pltpu.SemaphoreType.DMA((11,)),
            pltpu.SemaphoreType.DMA((2, max(n_x, n_y))),
            pltpu.SemaphoreType.DMA((2, max(n_x, n_y))),
            pltpu.SemaphoreType.DMA((EXCHANGES, 4)),
            pltpu.SemaphoreType.DMA((EXCHANGES, 4)),
        ],
        compiler_params=pltpu.CompilerParams(
            collective_id=0, has_side_effects=True, vmem_limit_bytes=48 * 1024 * 1024
        ),
    )(
        *(
            pltpu.with_memory_space_constraint(array, pltpu.HBM)
            for array in (
                velocity,
                stress,
                lame_first,
                shear,
                buoyancy,
                fwd_strain,
                fwd_accel,
                kernels,
                station_trace.T,
                station_tile.reshape(1, rows),
                station_cell.reshape(1, rows),
            )
        ),
        station_count,
    )
    return pl.pallas_call(
        deliver,
        out_shape=[pltpu.HBM(array.shape, f32) for array in (velocity, stress, kernels)],
        in_specs=[pl.BlockSpec(memory_space=pltpu.VMEM)] * 3,
        out_specs=[far] * 3,
        scratch_shapes=[pltpu.SemaphoreType.DMA((3,))],
    )(*(pltpu.with_memory_space_constraint(array, pltpu.VMEM) for array in results))


def solution(mesh):
    tiled = P(None, None, "gx", "gy")
    plane = P(None, "gx", "gy")
    listed = ("gx", "gy")
    return jax.shard_map(
        body,
        mesh=mesh,
        in_specs=(
            tiled,
            tiled,
            plane,
            plane,
            plane,
            tiled,
            tiled,
            tiled,
            P(listed, None),
            P(listed, None),
            P(listed),
            P(listed),
        ),
        out_specs=(tiled, tiled, tiled),
        check_vma=False,
    )
```

```python
import functools

import jax
import jax.numpy as jnp
from jax import lax
from jax.experimental import pallas as pl
from jax.experimental.pallas import tpu as pltpu
from jax.sharding import PartitionSpec as P

STEPS = 2
CAP = 4
C_NEAR = 9.0 / 8.0
C_FAR = -1.0 / 24.0
STEP_DT = 0.25
MESH = pl.DeviceIdType.MESH

LANES = 128
FEATURES = 8
MARGIN = 8
ZPAD = 2
SXX, SXZ, SXY, SYY, SYZ, SZZ = range(6)
LAME, SHEAR, BUOY = range(3)
STRIP = 10
KEPT = 4
REACH = STRIP - KEPT
WINGS = LANES // 2 - 4


def pieces(value):
    high = value.astype(jnp.bfloat16)
    rest = value - high.astype(jnp.float32)
    middle = rest.astype(jnp.bfloat16)
    low = (rest - middle.astype(jnp.float32)).astype(jnp.bfloat16)
    return high, middle, low


def dot_nt(left, right):
    return lax.dot_general(left, right, (((1,), (1,)), ((), ())), preferred_element_type=jnp.float32)


def kernel(
    n_x,
    n_y,
    vel_in,
    str_in,
    lame_in,
    shear_in,
    buoy_in,
    strain_in,
    accel_in,
    kern_in,
    trace_in,
    tile_in,
    cell_in,
    count,
    vel_out,
    str_out,
    kern_out,
    speed,
    tension,
    solid,
    strain,
    accel,
    kern,
    trace,
    tile,
    cell,
    source,
    payload,
    packed,
    first_hop,
    regrouped,
    second_hop,
    spot_rows,
    spot_cols,
    speed_wing,
    tension_wing,
    solid_wing,
    source_wing,
    *rest,
):
    x_send, x_recv, wing_send, wing_recv, corner_recv = (rest[3 * i : 3 * i + 3] for i in range(5))
    in_sem, hop_send, hop_recv, face_send, face_recv = rest[15:]
    depth, width = buoy_in.shape[0], buoy_in.shape[1]
    rows = trace.shape[1]
    tiles = n_x * n_y
    gx, gy = lax.axis_index("gx"), lax.axis_index("gy")
    inner = pl.ds(MARGIN, width)
    planes = pl.ds(ZPAD, depth)

    loads = [
        pltpu.make_async_copy(src, dst, in_sem.at[i])
        for i, (src, dst) in enumerate(
            (
                (trace_in, trace),
                (tile_in, tile),
                (cell_in, cell),
                (str_in, tension.at[:, planes, inner, :]),
                (vel_in, speed.at[:, planes, inner, :]),
                (buoy_in, solid.at[BUOY, :, inner, :]),
                (lame_in, solid.at[LAME, :, inner, :]),
                (shear_in, solid.at[SHEAR, :, inner, :]),
                (strain_in, strain),
                (accel_in, accel),
                (kern_in, kern),
            )
        )
    ]
    for load in loads:
        load.start()

    half_x, half_y = n_x // 2, n_y // 2
    my_a = lax.rem(gx, half_x) * 2 + lax.rem(gy, 2)
    my_b = (gx // half_x) * half_y + gy // 2
    size_a, size_b = n_x, n_y

    def at_a(a):
        return ((gx // half_x) * half_x + a // 2, (gy // 2) * 2 + lax.rem(a, 2))

    def at_b(b):
        return ((b // half_y) * half_x + lax.rem(gx, half_x), lax.rem(b, half_y) * 2 + lax.rem(gy, 2))

    up_x = (lax.rem(gx + 1, n_x), gy)
    down_x = (lax.rem(gx + n_x - 1, n_x), gy)
    up_y = (gx, lax.rem(gy + 1, n_y))
    down_y = (gx, lax.rem(gy + n_y - 1, n_y))
    corners = tuple((x, y) for x in (down_x[0], up_x[0]) for y in (down_y[1], up_y[1]))
    around = (down_x, up_x, down_y, up_y) + corners

    barrier = pltpu.get_barrier_semaphore()

    def greet(place, me, size):
        def run(i, _):
            pl.semaphore_signal(barrier, inc=1, device_id=place(lax.rem(me + i, size)), device_id_type=MESH)
            return 0

        lax.fori_loop(1, size, run, 0)

    greet(at_a, my_a, size_a)
    greet(at_b, my_b, size_b)
    for target in around:
        pl.semaphore_signal(barrier, inc=1, device_id=target, device_id_type=MESH)

    blank = jnp.zeros((ZPAD, width + 2 * MARGIN, LANES), jnp.float32)
    for ref, comps in ((speed, (0, 1, 2)), (tension, (SXZ, SYZ, SZZ))):
        for comp in comps:
            ref[comp, pl.ds(0, ZPAD)] = blank
            ref[comp, pl.ds(ZPAD + depth, ZPAD)] = blank

    for load in loads[:3]:
        load.wait()
    names = tile[...]
    line = lax.broadcasted_iota(jnp.int32, (tiles, rows), 0)
    named = (line == names).astype(jnp.float32)
    named_16 = named.astype(jnp.bfloat16)
    earlier = (
        lax.broadcasted_iota(jnp.int32, (rows, rows), 0) < lax.broadcasted_iota(jnp.int32, (rows, rows), 1)
    ).astype(jnp.float32).astype(jnp.bfloat16)
    ahead = jnp.dot(named_16, earlier, preferred_element_type=jnp.float32)
    slot = jnp.sum(named * ahead, axis=0, keepdims=True)
    live = lax.broadcasted_iota(jnp.int32, (1, rows), 1) < count[0]
    cells = cell[...]
    samples = trace.shape[0]
    payload[pl.ds(0, samples), :] = jnp.where(live, trace[...], 0.0)
    payload[pl.ds(samples, 1), :] = (cells // LANES).astype(jnp.float32)
    payload[pl.ds(samples + 1, 1), :] = (cells % LANES).astype(jnp.float32)
    load_all = payload[...]
    at_x, at_y = names // n_y, lax.rem(names, n_y)
    to_a = lax.rem(at_x, half_x) * 2 + lax.rem(at_y, 2)
    to_b = (at_x // half_x) * half_y + at_y // 2
    row_to = to_a * (size_b // CAP) + to_b // CAP
    group = lax.rem(to_b, CAP).astype(jnp.float32) * CAP + slot
    spread = [jnp.where((group == float(g)) & (slot < CAP), load_all, 0.0) for g in range(CAP * CAP)]
    bundle = jnp.concatenate(spread, axis=0)
    lines = size_a * size_b // CAP
    aimed = (lax.broadcasted_iota(jnp.int32, (lines, rows), 0) == row_to).astype(jnp.float32).astype(jnp.bfloat16)
    outgoing = sum(dot_nt(aimed, piece) for piece in pieces(bundle))
    packed[...] = outgoing.reshape(size_a, size_b // CAP, 1, LANES)

    lane_row = lax.broadcasted_iota(jnp.int32, (1, LANES), 1)
    turn = lax.rem(lane_row, STRIP)
    level = lax.rem(lane_row // STRIP, depth)
    from_up = (lane_row < WINGS) & (turn >= KEPT)
    from_down = (lane_row >= WINGS) & (turn < REACH)
    below = MARGIN + width

    def face_copies(e):
        strips = x_send[e].shape[1]
        count = wing_send[e].shape[0]
        tail = pl.ds(strips - count, count)
        moves = [
            (x_send[e].at[0], x_recv[e].at[0], down_x),
            (x_send[e].at[1], x_recv[e].at[1], up_x),
            (wing_send[e], wing_recv[e].at[0], down_y),
            (wing_send[e], wing_recv[e].at[1], up_y),
        ]
        if e < 2:
            for k, target in enumerate(corners):
                moves.append((x_send[e].at[k // 2, tail], corner_recv[e].at[k // 2, k % 2], target))
        return [
            pltpu.make_async_remote_copy(
                src_ref=src,
                dst_ref=dst,
                send_sem=face_send.at[e, k],
                recv_sem=face_recv.at[e, k],
                device_id=target,
                device_id_type=MESH,
            )
            for k, (src, dst, target) in enumerate(moves)
        ]

    def pack_faces(e, fields):
        reach = x_send[e].shape[2]
        for i, (ref, comp, first) in enumerate(fields):
            def strip(z, heap, i=i, ref=ref, comp=comp, first=first):
                plane = ref[comp, z + first, inner, :]
                x_send[e][0, i * depth + z] = ref[comp, z + first, pl.ds(MARGIN, reach), :]
                x_send[e][1, i * depth + z] = ref[comp, z + first, pl.ds(below - reach, reach), :]
                start = z * STRIP
                low, high = heap
                low = jnp.where(lane_row >= start, pltpu.roll(plane, start + KEPT, 1), low)
                high = jnp.where(lane_row >= WINGS + start, pltpu.roll(plane, WINGS + start + REACH, 1), high)
                return low, high

            empty = jnp.zeros((width, LANES), jnp.float32)
            low, high = lax.fori_loop(0, depth, strip, (empty, empty), unroll=True)
            wing = jnp.where(lane_row >= WINGS, high, low)
            wing_send[e][i] = wing
            if e < 2:
                x_send[e][0, len(fields) * depth + i] = wing[:reach]
                x_send[e][1, len(fields) * depth + i] = wing[width - reach :]
        for copy in face_copies(e):
            copy.start()

    def take_faces(e, fields):
        reach = x_send[e].shape[2]
        for copy in face_copies(e):
            copy.wait_recv()

        def clear(at_edge, *refs):
            @pl.when(at_edge)
            def _():
                for ref in refs:
                    ref[...] = jnp.zeros(ref.shape, jnp.float32)

        corner = corner_recv[e]
        both = e < 2
        clear(gy == n_y - 1, wing_recv[e].at[0], *([corner.at[0, 0], corner.at[1, 0]] if both else []))
        clear(gy == 0, wing_recv[e].at[1], *([corner.at[0, 1], corner.at[1, 1]] if both else []))
        clear(gx == n_x - 1, x_recv[e].at[0], *([corner.at[0]] if both else []))
        clear(gx == 0, x_recv[e].at[1], *([corner.at[1]] if both else []))

        def mixed(up, down, own):
            return jnp.where(from_up, up, jnp.where(from_down, down, own))

        for i, (ref, comp, first, wing, at) in enumerate(fields):
            def rows_of(z, _, i=i, ref=ref, comp=comp, first=first):
                ref[comp, z + first, pl.ds(below, reach), :] = x_recv[e][0, i * depth + z]
                ref[comp, z + first, pl.ds(MARGIN - reach, reach), :] = x_recv[e][1, i * depth + z]
                return 0

            lax.fori_loop(0, depth, rows_of, 0, unroll=True)
            wing[at, inner, :] = mixed(wing_recv[e][0, i], wing_recv[e][1, i], wing_send[e][i])
            if both:
                for side, start in ((0, below), (1, MARGIN - reach)):
                    wing[at, pl.ds(start, reach), :] = mixed(
                        corner[side, 0, i], corner[side, 1, i], x_recv[e][side, len(fields) * depth + i]
                    )

    def difference(at, upward):
        if upward:
            return C_NEAR * (at(1) - at(0)) + C_FAR * (at(2) - at(-1))
        return C_NEAR * (at(0) - at(-1)) + C_FAR * (at(1) - at(-2))

    def tile_part(z, start, count):
        def along_z(ref, comp, upward):
            return difference(lambda o: ref[comp, z + ZPAD + o, pl.ds(start, count), :], upward)

        def along_x(ref, comp, upward):
            return difference(lambda o: ref[comp, z + ZPAD, pl.ds(start + o, count), :], upward)

        def along_y(ref, comp, upward):
            wing = (speed_wing if ref is speed else tension_wing)[comp, pl.ds(start, count), :]
            centre = ref[comp, z + ZPAD, pl.ds(start, count), :]
            side = jnp.where(
                lane_row < LANES // 2,
                pltpu.roll(wing, LANES - KEPT - z * STRIP, 1),
                pltpu.roll(wing, LANES - REACH - WINGS - z * STRIP, 1),
            )

            def at(o):
                if o == 0:
                    return centre
                if o > 0:
                    return pltpu.roll(jnp.where(lane_row < o, side, centre), LANES - o, 1)
                return pltpu.roll(jnp.where(lane_row >= LANES + o, side, centre), -o, 1)

            return difference(at, upward)

        return along_x, along_y, along_z

    def wing_part(start, count):
        def held(ref, comp, o=0):
            return (speed_wing if ref is speed else tension_wing)[comp, pl.ds(start + o, count), :]

        def along_z(ref, comp, upward):
            value = held(ref, comp)

            def at(o):
                if o == 0:
                    return value
                inside = (level + o >= 0) & (level + o < depth)
                return jnp.where(inside, pltpu.roll(value, (-o * STRIP) % LANES, 1), 0.0)

            return difference(at, upward)

        def along_x(ref, comp, upward):
            return difference(lambda o: held(ref, comp, o), upward)

        def along_y(ref, comp, upward):
            value = held(ref, comp)
            return difference(lambda o: value if o == 0 else pltpu.roll(value, -o % LANES, 1), upward)

        return along_x, along_y, along_z

    def rates(along_x, along_y, along_z):
        return (
            along_x(tension, SXX, True) + along_y(tension, SXY, False) + along_z(tension, SXZ, False),
            along_x(tension, SXY, False) + along_y(tension, SYY, True) + along_z(tension, SYZ, False),
            along_x(tension, SXZ, False) + along_y(tension, SYZ, False) + along_z(tension, SZZ, True),
        )

    def strains(along_x, along_y, along_z):
        exx = along_x(speed, 0, False)
        eyy = along_y(speed, 1, False)
        ezz = along_z(speed, 2, False)
        gxy = along_y(speed, 0, True) + along_x(speed, 1, True)
        gxz = along_z(speed, 0, True) + along_x(speed, 2, True)
        gyz = along_z(speed, 1, True) + along_y(speed, 2, True)
        return exx, eyy, ezz, gxy, gxz, gyz

    def changes(strained, lame, shear):
        exx, eyy, ezz, gxy, gxz, gyz = strained
        stiff = STEP_DT * shear
        common = STEP_DT * lame * (exx + eyy + ezz)
        return (
            (SXX, common + 2.0 * stiff * exx),
            (SYY, common + 2.0 * stiff * eyy),
            (SZZ, common + 2.0 * stiff * ezz),
            (SXY, stiff * gxy),
            (SXZ, stiff * gxz),
            (SYZ, stiff * gyz),
        )

    def push_speed(margin, step, final):
        start, count = MARGIN - margin, width + 2 * margin
        rows_at = pl.ds(start, count)

        def plane(z, _):
            factor = STEP_DT * solid[BUOY, z, rows_at, :]
            for k, rate in enumerate(rates(*tile_part(z, start, count))):
                if step > 0:
                    rate = rate + source[3 * step + k, z, rows_at, :]
                value = speed[k, z + ZPAD, rows_at, :] + factor * rate
                speed[k, z + ZPAD, rows_at, :] = value
                if final:
                    vel_out[k, z] = value[margin : margin + width]
            return 0

        lax.fori_loop(0, depth, plane, 0, unroll=True)
        if margin > 0:
            factor = STEP_DT * solid_wing[BUOY, inner, :]
            for k, rate in enumerate(rates(*wing_part(MARGIN, width))):
                change = factor * (rate + source_wing[k, inner, :])
                speed_wing[k, inner, :] = speed_wing[k, inner, :] + change

    def add_source(step):
        def plane(z, _):
            factor = STEP_DT * solid[BUOY, z, inner, :]
            for k in range(3):
                speed[k, z + ZPAD, inner, :] = (
                    speed[k, z + ZPAD, inner, :] + factor * source[3 * step + k, z, inner, :]
                )
            return 0

        lax.fori_loop(0, depth, plane, 0, unroll=True)

    def push_stress(margin, final):
        start, count = MARGIN - margin, width + 2 * margin
        rows_at = pl.ds(start, count)

        def plane(z, _):
            strained = strains(*tile_part(z, start, count))
            for comp, change in changes(strained, solid[LAME, z, rows_at, :], solid[SHEAR, z, rows_at, :]):
                value = tension[comp, z + ZPAD, rows_at, :] + change
                if final:
                    str_out[comp, z] = value
                else:
                    tension[comp, z + ZPAD, rows_at, :] = value
            if final:
                exx, eyy, ezz, gxy, gxz, gyz = strained
                f = [strain[comp, z].astype(jnp.float32) for comp in range(6)]
                a = [accel[comp, z].astype(jnp.float32) for comp in range(3)]
                v = [speed[comp, z + ZPAD, inner, :] for comp in range(3)]
                kern_out[0, z] = kern[0, z] - STEP_DT * (f[SXX] + f[SYY] + f[SZZ]) * (exx + eyy + ezz)
                kern_out[1, z] = kern[1, z] - 2.0 * STEP_DT * (
                    f[SXX] * exx + f[SYY] * eyy + f[SZZ] * ezz + f[SXY] * gxy + f[SXZ] * gxz + f[SYZ] * gyz
                )
                kern_out[2, z] = kern[2, z] - STEP_DT * (a[0] * v[0] + a[1] * v[1] + a[2] * v[2])
            return 0

        lax.fori_loop(0, depth, plane, 0, unroll=True)
        if margin > 0:
            near = margin // 2
            near_at = pl.ds(MARGIN - near, width + 2 * near)
            strained = strains(*wing_part(MARGIN - near, width + 2 * near))
            for comp, change in changes(strained, solid_wing[LAME, near_at, :], solid_wing[SHEAR, near_at, :]):
                tension_wing[comp, near_at, :] = tension_wing[comp, near_at, :] + change

    pl.semaphore_wait(barrier, size_a + size_b - 2 + len(around))

    def hop_a(i):
        to = lax.rem(my_a + i, size_a)
        return pltpu.make_async_remote_copy(
            src_ref=packed.at[to],
            dst_ref=first_hop.at[lax.rem(my_a, CAP), :, my_a // CAP],
            send_sem=hop_send.at[0, i],
            recv_sem=hop_recv.at[0, i],
            device_id=at_a(to),
            device_id_type=MESH,
        )

    def hop_b(i):
        to = lax.rem(my_b + i, size_b)
        return pltpu.make_async_remote_copy(
            src_ref=regrouped.at[to // CAP, lax.rem(to, CAP)],
            dst_ref=second_hop.at[my_b],
            send_sem=hop_send.at[1, i],
            recv_sem=hop_recv.at[1, i],
            device_id=at_b(to),
            device_id_type=MESH,
        )

    def start(make):
        def run(i, _):
            make(i).start()
            return 0

        return run

    def landed(make):
        def run(i, _):
            make(i).wait_recv()
            return 0

        return run

    def sent(make):
        def run(i, _):
            make(i).wait_send()
            return 0

        return run

    lax.fori_loop(1, size_a, start(hop_a), 0)
    own_a = pltpu.make_async_copy(
        packed.at[my_a], first_hop.at[lax.rem(my_a, CAP), :, my_a // CAP], hop_recv.at[0, 0]
    )
    own_a.start()
    start_fields = [(tension, comp, ZPAD, tension_wing, comp) for comp in range(6)]
    start_fields += [(solid, comp, 0, solid_wing, comp) for comp in range(3)]
    speed_fields = [(speed, comp, ZPAD, speed_wing, comp) for comp in range(3)]
    late_fields = [(source, 3 + comp, 0, source_wing, comp) for comp in range(3)]
    for load in (loads[3], *loads[5:8]):
        load.wait()
    pack_faces(0, [field[:3] for field in start_fields])
    own_a.wait()
    lax.fori_loop(1, size_a, landed(hop_a), 0)
    heaps = [first_hop[p].reshape(lines // CAP, LANES) for p in range(CAP)]
    span = CAP * FEATURES
    lane_hop = lax.broadcasted_iota(jnp.int32, (lines // CAP, LANES), 1)
    for low in range(CAP):
        merged = None
        for p in range(CAP):
            shift = (span * (p - low)) % LANES
            turned = heaps[p] if shift == 0 else pltpu.roll(heaps[p], shift, 1)
            merged = turned if p == 0 else jnp.where(lane_hop >= span * p, turned, merged)
        regrouped[:, low] = merged.reshape(size_b // CAP, size_a // CAP, 1, LANES)
    lax.fori_loop(1, size_b, start(hop_b), 0)
    own_b = pltpu.make_async_copy(
        regrouped.at[my_b // CAP, lax.rem(my_b, CAP)], second_hop.at[my_b], hop_recv.at[1, 0]
    )
    own_b.start()

    take_faces(0, start_fields)
    loads[4].wait()
    push_speed(0, 0, False)

    own_b.wait()
    lax.fori_loop(1, size_b, landed(hop_b), 0)
    arrived = second_hop[...].reshape(lines, LANES)
    arrived = jnp.concatenate([arrived, pltpu.roll(arrived, LANES // 2, 1)], axis=0).T
    heap = LANES // 2 // FEATURES
    values = jnp.concatenate([arrived[g * FEATURES : (g + 1) * FEATURES] for g in range(heap)], axis=1)
    entries = CAP * tiles
    row_of = lax.broadcasted_iota(jnp.int32, (depth * width, entries), 0).astype(jnp.float32)
    col_of = lax.broadcasted_iota(jnp.int32, (LANES, entries), 0).astype(jnp.float32)
    spot_rows[...] = (row_of == values[samples : samples + 1]).astype(jnp.float32).astype(jnp.bfloat16)
    spot_cols[...] = (col_of == values[samples + 1 : samples + 2]).astype(jnp.float32).astype(jnp.bfloat16)
    amounts = pieces(values)

    def lay_sources(step):
        columns = spot_cols[...]
        total = jnp.zeros((depth * width, 3 * LANES), jnp.float32)
        for amount in amounts:
            spread = [columns * amount[3 * step + k : 3 * step + k + 1, :] for k in range(3)]
            total = total + dot_nt(spot_rows[...], jnp.concatenate(spread, axis=0))
        for k in range(3):
            source[3 * step + k, :, inner, :] = total[:, k * LANES : (k + 1) * LANES].reshape(depth, width, LANES)

    lay_sources(0)
    add_source(0)
    pack_faces(1, [field[:3] for field in speed_fields])
    lay_sources(1)
    pack_faces(2, [field[:3] for field in late_fields])
    for load in loads[8:]:
        load.wait()
    take_faces(1, speed_fields)
    push_stress(4, False)
    take_faces(2, late_fields)
    push_speed(2, 1, True)
    push_stress(0, True)
    lax.fori_loop(1, size_a, sent(hop_a), 0)
    lax.fori_loop(1, size_b, sent(hop_b), 0)
    for e in range(3):
        for copy in face_copies(e):
            copy.wait_send()


def deliver(*refs):
    sources, targets, sems = refs[:3], refs[3:6], refs[6]
    copies = [pltpu.make_async_copy(src, dst, sems.at[i]) for i, (src, dst) in enumerate(zip(sources, targets))]
    for copy in copies:
        copy.start()
    for copy in copies:
        copy.wait()


def body(
    velocity,
    stress,
    lame_first,
    shear,
    buoyancy,
    fwd_strain,
    fwd_accel,
    kernels,
    station_trace,
    station_tile,
    station_cell,
    station_count,
):
    n_x, n_y = lax.axis_size("gx"), lax.axis_size("gy")
    depth, width, lanes = buoyancy.shape
    rows = station_trace.shape[0]
    tiles = n_x * n_y
    exchanges = ((9, 4, 1), (3, 6, 1), (3, 2, 0))
    padded = (depth + 2 * ZPAD, width + 2 * MARGIN, lanes)
    f32, b16 = jnp.float32, jnp.bfloat16
    far = pl.BlockSpec(memory_space=pltpu.HBM)
    results = pl.pallas_call(
        functools.partial(kernel, n_x, n_y),
        out_shape=[
            pltpu.VMEM(velocity.shape, f32),
            pltpu.VMEM(stress.shape, f32),
            pltpu.VMEM(kernels.shape, f32),
        ],
        in_specs=[far] * 11 + [pl.BlockSpec(memory_space=pltpu.SMEM)],
        out_specs=[pl.BlockSpec(memory_space=pltpu.VMEM)] * 3,
        scratch_shapes=[
            pltpu.VMEM((3, *padded), f32),
            pltpu.VMEM((6, *padded), f32),
            pltpu.VMEM((3, depth, *padded[1:]), f32),
            pltpu.VMEM(fwd_strain.shape, b16),
            pltpu.VMEM(fwd_accel.shape, b16),
            pltpu.VMEM(kernels.shape, f32),
            pltpu.VMEM(station_trace.shape[::-1], f32),
            pltpu.VMEM((1, rows), jnp.int32),
            pltpu.VMEM((1, rows), jnp.int32),
            pltpu.VMEM((3 * STEPS, depth, *padded[1:]), f32),
            pltpu.VMEM((FEATURES, rows), f32),
            pltpu.VMEM((n_x, n_y // CAP, 1, lanes), f32),
            pltpu.VMEM((CAP, n_y // CAP, n_x // CAP, 1, lanes), f32),
            pltpu.VMEM((n_y // CAP, CAP, n_x // CAP, 1, lanes), f32),
            pltpu.VMEM((n_y, n_x // CAP, 1, lanes), f32),
            pltpu.VMEM((depth * width, CAP * tiles), b16),
            pltpu.VMEM((lanes, CAP * tiles), b16),
            *[pltpu.VMEM((fields, *padded[1:]), f32) for fields in (3, 6, 3, 3)],
            *[pltpu.VMEM((2, fields * (depth + wings), reach, lanes), f32) for fields, reach, wings in exchanges],
            *[pltpu.VMEM((2, fields * (depth + wings), reach, lanes), f32) for fields, reach, wings in exchanges],
            *[pltpu.VMEM((fields, width, lanes), f32) for fields, reach, wings in exchanges],
            *[pltpu.VMEM((2, fields, width, lanes), f32) for fields, reach, wings in exchanges],
            *[pltpu.VMEM((2, 2, fields, reach, lanes), f32) for fields, reach, wings in exchanges],
            pltpu.SemaphoreType.DMA((11,)),
            pltpu.SemaphoreType.DMA((2, max(n_x, n_y))),
            pltpu.SemaphoreType.DMA((2, max(n_x, n_y))),
            pltpu.SemaphoreType.DMA((len(exchanges), 8)),
            pltpu.SemaphoreType.DMA((len(exchanges), 8)),
        ],
        compiler_params=pltpu.CompilerParams(
            collective_id=0, has_side_effects=True, vmem_limit_bytes=48 * 1024 * 1024
        ),
    )(
        *(
            pltpu.with_memory_space_constraint(array, pltpu.HBM)
            for array in (
                velocity,
                stress,
                lame_first,
                shear,
                buoyancy,
                fwd_strain,
                fwd_accel,
                kernels,
                station_trace.T,
                station_tile.reshape(1, rows),
                station_cell.reshape(1, rows),
            )
        ),
        station_count,
    )
    return pl.pallas_call(
        deliver,
        out_shape=[pltpu.HBM(array.shape, f32) for array in (velocity, stress, kernels)],
        in_specs=[pl.BlockSpec(memory_space=pltpu.VMEM)] * 3,
        out_specs=[far] * 3,
        scratch_shapes=[pltpu.SemaphoreType.DMA((3,))],
    )(*(pltpu.with_memory_space_constraint(array, pltpu.VMEM) for array in results))


def solution(mesh):
    tiled = P(None, None, "gx", "gy")
    plane = P(None, "gx", "gy")
    listed = ("gx", "gy")
    return jax.shard_map(
        body,
        mesh=mesh,
        in_specs=(
            tiled,
            tiled,
            plane,
            plane,
            plane,
            tiled,
            tiled,
            tiled,
            P(listed, None),
            P(listed, None),
            P(listed),
            P(listed),
        ),
        out_specs=(tiled, tiled, tiled),
        check_vma=False,
    )
```

```python
import functools

import jax
import jax.numpy as jnp
from jax import lax
from jax.experimental import pallas as pl
from jax.experimental.pallas import tpu as pltpu
from jax.sharding import PartitionSpec as P

STEPS = 2
CAP = 4
C_NEAR = 9.0 / 8.0
C_FAR = -1.0 / 24.0
STEP_DT = 0.25
MESH = pl.DeviceIdType.MESH

LANES = 128
FEATURES = 8
MARGIN = 8
ZPAD = 2
SXX, SXZ, SXY, SYY, SYZ, SZZ = range(6)
LAME, SHEAR, BUOY = range(3)
NEAR_START, WIDE_START, WIDE_SPEED, LATE_SOURCE = range(4)
STRIP = 10
KEPT = 4
REACH = STRIP - KEPT
WINGS = LANES // 2 - 4


def pieces(value):
    high = value.astype(jnp.bfloat16)
    rest = value - high.astype(jnp.float32)
    middle = rest.astype(jnp.bfloat16)
    low = (rest - middle.astype(jnp.float32)).astype(jnp.bfloat16)
    return high, middle, low


def dot_nt(left, right):
    return lax.dot_general(left, right, (((1,), (1,)), ((), ())), preferred_element_type=jnp.float32)


def kernel(
    n_x,
    n_y,
    vel_in,
    str_in,
    lame_in,
    shear_in,
    buoy_in,
    strain_in,
    accel_in,
    kern_in,
    trace_in,
    tile_in,
    cell_in,
    count,
    vel_out,
    str_out,
    kern_out,
    speed,
    tension,
    solid,
    strain,
    accel,
    kern,
    trace,
    tile,
    cell,
    source,
    payload,
    packed,
    first_hop,
    regrouped,
    second_hop,
    spot_rows,
    spot_cols,
    speed_wing,
    tension_wing,
    solid_wing,
    source_wing,
    *rest,
):
    x_send, x_recv, wing_send, wing_recv, corner_recv = (rest[4 * i : 4 * i + 4] for i in range(5))
    in_sem, hop_send, hop_recv, face_send, face_recv = rest[20:]
    depth, width = buoy_in.shape[0], buoy_in.shape[1]
    rows = trace.shape[1]
    tiles = n_x * n_y
    gx, gy = lax.axis_index("gx"), lax.axis_index("gy")
    inner = pl.ds(MARGIN, width)
    planes = pl.ds(ZPAD, depth)

    half_x, half_y = n_x // 2, n_y // 2
    my_a = lax.rem(gx, half_x) * 2 + lax.rem(gy, 2)
    my_b = (gx // half_x) * half_y + gy // 2
    size_a, size_b = n_x, n_y

    quarter_y = n_y // 4
    high_y, low_y = gx // half_x, gy // half_y

    def around_ring(size):
        return lambda step: -min(step, size - step)

    offsets_a = [(dz, dc) for dz in sorted(range(half_x), key=around_ring(half_x)) for dc in range(2)][:-2] + [(0, 1)]
    offsets_b = sorted(
        ((dy, dx) for dy in range(4) for dx in range(quarter_y) if dy + dx > 0),
        key=lambda step: around_ring(4)(step[0]) + around_ring(quarter_y)(step[1]),
    )

    def partner_a(i):
        dz, dc = offsets_a[i]
        near = lax.rem(lax.rem(gx, half_x) + dz, half_x)
        core = lax.rem(gy + dc, 2)
        return near * 2 + core, ((gx // half_x) * half_x + near, (gy // 2) * 2 + core)

    def partner_b(i):
        dy, dx = offsets_b[i]
        line = lax.rem(high_y * 2 + low_y + dy, 4)
        spot = lax.rem(lax.rem(gy, half_y) // 2 + dx, quarter_y)
        outer = lax.rem(line, 2) * quarter_y + spot
        return (line // 2) * half_y + outer, (
            (line // 2) * half_x + lax.rem(gx, half_x),
            outer * 2 + lax.rem(gy, 2),
        )

    up_x = (lax.rem(gx + 1, n_x), gy)
    down_x = (lax.rem(gx + n_x - 1, n_x), gy)
    up_y = (gx, lax.rem(gy + 1, n_y))
    down_y = (gx, lax.rem(gy + n_y - 1, n_y))
    corners = tuple((x, y) for x in (down_x[0], up_x[0]) for y in (down_y[1], up_y[1]))
    around = (down_x, up_x, down_y, up_y) + corners

    barrier = pltpu.get_barrier_semaphore()

    partners_a = [partner_a(i) for i in range(size_a - 1)]
    partners_b = [partner_b(i) for i in range(size_b - 1)]
    for _, target in partners_a + partners_b:
        pl.semaphore_signal(barrier, inc=1, device_id=target, device_id_type=MESH)
    for target in around:
        pl.semaphore_signal(barrier, inc=1, device_id=target, device_id_type=MESH)

    loads = [
        pltpu.make_async_copy(src, dst, in_sem.at[i])
        for i, (src, dst) in enumerate(
            (
                (trace_in, trace),
                (tile_in, tile),
                (cell_in, cell),
                (str_in, tension.at[:, planes, inner, :]),
                (vel_in, speed.at[:, planes, inner, :]),
                (buoy_in, solid.at[BUOY, :, inner, :]),
                (lame_in, solid.at[LAME, :, inner, :]),
                (shear_in, solid.at[SHEAR, :, inner, :]),
                (strain_in, strain),
                (accel_in, accel),
                (kern_in, kern),
            )
        )
    ]
    for load in loads:
        load.start()


    blank = jnp.zeros((ZPAD, width + 2 * MARGIN, LANES), jnp.float32)
    for ref, comps in ((speed, (0, 1, 2)), (tension, (SXZ, SYZ, SZZ))):
        for comp in comps:
            ref[comp, pl.ds(0, ZPAD)] = blank
            ref[comp, pl.ds(ZPAD + depth, ZPAD)] = blank

    for load in loads[:3]:
        load.wait()
    names = tile[...]
    line = lax.broadcasted_iota(jnp.int32, (tiles, rows), 0)
    named = (line == names).astype(jnp.float32)
    named_16 = named.astype(jnp.bfloat16)
    earlier = (
        lax.broadcasted_iota(jnp.int32, (rows, rows), 0) < lax.broadcasted_iota(jnp.int32, (rows, rows), 1)
    ).astype(jnp.float32).astype(jnp.bfloat16)
    ahead = jnp.dot(named_16, earlier, preferred_element_type=jnp.float32)
    slot = jnp.sum(named * ahead, axis=0, keepdims=True)
    live = lax.broadcasted_iota(jnp.int32, (1, rows), 1) < count[0]
    cells = cell[...]
    samples = trace.shape[0]
    payload[pl.ds(0, samples), :] = jnp.where(live, trace[...], 0.0)
    payload[pl.ds(samples, 1), :] = (cells // LANES).astype(jnp.float32)
    payload[pl.ds(samples + 1, 1), :] = (cells % LANES).astype(jnp.float32)
    load_all = payload[...]
    at_x, at_y = names // n_y, lax.rem(names, n_y)
    to_a = lax.rem(at_x, half_x) * 2 + lax.rem(at_y, 2)
    to_b = (at_x // half_x) * half_y + at_y // 2
    row_to = to_a * (size_b // CAP) + to_b // CAP
    group = lax.rem(to_b, CAP).astype(jnp.float32) * CAP + slot
    spread = [jnp.where((group == float(g)) & (slot < CAP), load_all, 0.0) for g in range(CAP * CAP)]
    bundle = jnp.concatenate(spread, axis=0)
    lines = size_a * size_b // CAP
    aimed = (lax.broadcasted_iota(jnp.int32, (lines, rows), 0) == row_to).astype(jnp.float32).astype(jnp.bfloat16)
    outgoing = sum(dot_nt(aimed, piece) for piece in pieces(bundle))
    packed[...] = outgoing.reshape(size_a, size_b // CAP, 1, LANES)

    lane_row = lax.broadcasted_iota(jnp.int32, (1, LANES), 1)
    turn = lax.rem(lane_row, STRIP)
    level = lax.rem(lane_row // STRIP, depth)
    from_up = (lane_row < WINGS) & (turn >= KEPT)
    from_down = (lane_row >= WINGS) & (turn < REACH)
    below = MARGIN + width

    def has_corners(e):
        return e in (WIDE_SPEED, WIDE_START)

    def face_copies(e):
        strips = x_send[e].shape[1]
        count = wing_send[e].shape[0]
        tail = pl.ds(strips - count, count)
        moves = [
            (x_send[e].at[0], x_recv[e].at[0], down_x),
            (x_send[e].at[1], x_recv[e].at[1], up_x),
            (wing_send[e], wing_recv[e].at[0], down_y),
            (wing_send[e], wing_recv[e].at[1], up_y),
        ]
        if has_corners(e):
            for k, target in enumerate(corners):
                moves.append((x_send[e].at[k // 2, tail], corner_recv[e].at[k // 2, k % 2], target))
        return [
            pltpu.make_async_remote_copy(
                src_ref=src,
                dst_ref=dst,
                send_sem=face_send.at[e, k],
                recv_sem=face_recv.at[e, k],
                device_id=target,
                device_id_type=MESH,
            )
            for k, (src, dst, target) in enumerate(moves)
        ]

    def pack_faces(e, x_fields, wing_fields):
        reach = x_send[e].shape[2]
        for i, (ref, comp, first) in enumerate(x_fields):
            def rows_of(z, _, i=i, ref=ref, comp=comp, first=first):
                x_send[e][0, i * depth + z] = ref[comp, z + first, pl.ds(MARGIN, reach), :]
                x_send[e][1, i * depth + z] = ref[comp, z + first, pl.ds(below - reach, reach), :]
                return 0

            lax.fori_loop(0, depth, rows_of, 0, unroll=True)
        for i, (ref, comp, first) in enumerate(wing_fields):
            def strip(z, heap, ref=ref, comp=comp, first=first):
                plane = ref[comp, z + first, inner, :]
                start = z * STRIP
                low, high = heap
                low = jnp.where(lane_row >= start, pltpu.roll(plane, start + KEPT, 1), low)
                high = jnp.where(lane_row >= WINGS + start, pltpu.roll(plane, WINGS + start + REACH, 1), high)
                return low, high

            empty = jnp.zeros((width, LANES), jnp.float32)
            low, high = lax.fori_loop(0, depth, strip, (empty, empty), unroll=True)
            wing = jnp.where(lane_row >= WINGS, high, low)
            wing_send[e][i] = wing
            if has_corners(e):
                x_send[e][0, len(x_fields) * depth + i] = wing[:reach]
                x_send[e][1, len(x_fields) * depth + i] = wing[width - reach :]

    def send_faces(e):
        for copy in face_copies(e):
            copy.start()

    def take_faces(e, x_fields, wing_fields):
        reach = x_send[e].shape[2]
        for copy in face_copies(e):
            copy.wait_recv()

        def clear(at_edge, *refs):
            @pl.when(at_edge)
            def _():
                for ref in refs:
                    ref[...] = jnp.zeros(ref.shape, jnp.float32)

        corner = corner_recv[e]
        both = has_corners(e)
        clear(gy == n_y - 1, wing_recv[e].at[0], *([corner.at[0, 0], corner.at[1, 0]] if both else []))
        clear(gy == 0, wing_recv[e].at[1], *([corner.at[0, 1], corner.at[1, 1]] if both else []))
        clear(gx == n_x - 1, x_recv[e].at[0], *([corner.at[0]] if both else []))
        clear(gx == 0, x_recv[e].at[1], *([corner.at[1]] if both else []))

        def mixed(up, down, own):
            return jnp.where(from_up, up, jnp.where(from_down, down, own))

        for i, (ref, comp, first) in enumerate(x_fields):
            def rows_of(z, _, i=i, ref=ref, comp=comp, first=first):
                ref[comp, z + first, pl.ds(below, reach), :] = x_recv[e][0, i * depth + z]
                ref[comp, z + first, pl.ds(MARGIN - reach, reach), :] = x_recv[e][1, i * depth + z]
                return 0

            lax.fori_loop(0, depth, rows_of, 0, unroll=True)
        for i, (wing, at) in enumerate(wing_fields):
            wing[at, inner, :] = mixed(wing_recv[e][0, i], wing_recv[e][1, i], wing_send[e][i])
            if both:
                for side, start in ((0, below), (1, MARGIN - reach)):
                    wing[at, pl.ds(start, reach), :] = mixed(
                        corner[side, 0, i], corner[side, 1, i], x_recv[e][side, len(x_fields) * depth + i]
                    )

    def difference(at, upward):
        if upward:
            return C_NEAR * (at(1) - at(0)) + C_FAR * (at(2) - at(-1))
        return C_NEAR * (at(0) - at(-1)) + C_FAR * (at(1) - at(-2))

    def tile_part(z, start, count):
        def along_z(ref, comp, upward):
            return difference(lambda o: ref[comp, z + ZPAD + o, pl.ds(start, count), :], upward)

        def along_x(ref, comp, upward):
            return difference(lambda o: ref[comp, z + ZPAD, pl.ds(start + o, count), :], upward)

        def along_y(ref, comp, upward):
            wing = (speed_wing if ref is speed else tension_wing)[comp, pl.ds(start, count), :]
            centre = ref[comp, z + ZPAD, pl.ds(start, count), :]
            side = jnp.where(
                lane_row < LANES // 2,
                pltpu.roll(wing, LANES - KEPT - z * STRIP, 1),
                pltpu.roll(wing, LANES - REACH - WINGS - z * STRIP, 1),
            )

            def at(o):
                if o == 0:
                    return centre
                if o > 0:
                    return pltpu.roll(jnp.where(lane_row < o, side, centre), LANES - o, 1)
                return pltpu.roll(jnp.where(lane_row >= LANES + o, side, centre), -o, 1)

            return difference(at, upward)

        return along_x, along_y, along_z

    def wing_part(start, count):
        def held(ref, comp, o=0):
            return (speed_wing if ref is speed else tension_wing)[comp, pl.ds(start + o, count), :]

        def along_z(ref, comp, upward):
            value = held(ref, comp)

            def at(o):
                if o == 0:
                    return value
                inside = (level + o >= 0) & (level + o < depth)
                return jnp.where(inside, pltpu.roll(value, (-o * STRIP) % LANES, 1), 0.0)

            return difference(at, upward)

        def along_x(ref, comp, upward):
            return difference(lambda o: held(ref, comp, o), upward)

        def along_y(ref, comp, upward):
            value = held(ref, comp)
            return difference(lambda o: value if o == 0 else pltpu.roll(value, -o % LANES, 1), upward)

        return along_x, along_y, along_z

    def rates(along_x, along_y, along_z):
        return (
            along_x(tension, SXX, True) + along_y(tension, SXY, False) + along_z(tension, SXZ, False),
            along_x(tension, SXY, False) + along_y(tension, SYY, True) + along_z(tension, SYZ, False),
            along_x(tension, SXZ, False) + along_y(tension, SYZ, False) + along_z(tension, SZZ, True),
        )

    def strains(along_x, along_y, along_z):
        exx = along_x(speed, 0, False)
        eyy = along_y(speed, 1, False)
        ezz = along_z(speed, 2, False)
        gxy = along_y(speed, 0, True) + along_x(speed, 1, True)
        gxz = along_z(speed, 0, True) + along_x(speed, 2, True)
        gyz = along_z(speed, 1, True) + along_y(speed, 2, True)
        return exx, eyy, ezz, gxy, gxz, gyz

    def changes(strained, lame, shear):
        exx, eyy, ezz, gxy, gxz, gyz = strained
        stiff = STEP_DT * shear
        common = STEP_DT * lame * (exx + eyy + ezz)
        return (
            (SXX, common + 2.0 * stiff * exx),
            (SYY, common + 2.0 * stiff * eyy),
            (SZZ, common + 2.0 * stiff * ezz),
            (SXY, stiff * gxy),
            (SXZ, stiff * gxz),
            (SYZ, stiff * gyz),
        )

    def push_speed(margin, step, final):
        start, count = MARGIN - margin, width + 2 * margin
        rows_at = pl.ds(start, count)

        def plane(z, _):
            factor = STEP_DT * solid[BUOY, z, rows_at, :]
            for k, rate in enumerate(rates(*tile_part(z, start, count))):
                if step > 0:
                    rate = rate + source[3 * step + k, z, rows_at, :]
                value = speed[k, z + ZPAD, rows_at, :] + factor * rate
                speed[k, z + ZPAD, rows_at, :] = value
                if final:
                    vel_out[k, z] = value[margin : margin + width]
            return 0

        lax.fori_loop(0, depth, plane, 0, unroll=True)
        if margin > 0:
            factor = STEP_DT * solid_wing[BUOY, inner, :]
            for k, rate in enumerate(rates(*wing_part(MARGIN, width))):
                change = factor * (rate + source_wing[k, inner, :])
                speed_wing[k, inner, :] = speed_wing[k, inner, :] + change

    def add_source(step):
        def plane(z, _):
            factor = STEP_DT * solid[BUOY, z, inner, :]
            for k in range(3):
                speed[k, z + ZPAD, inner, :] = (
                    speed[k, z + ZPAD, inner, :] + factor * source[3 * step + k, z, inner, :]
                )
            return 0

        lax.fori_loop(0, depth, plane, 0, unroll=True)

    def push_stress(margin, final):
        start, count = MARGIN - margin, width + 2 * margin
        rows_at = pl.ds(start, count)

        def plane(z, _):
            strained = strains(*tile_part(z, start, count))
            for comp, change in changes(strained, solid[LAME, z, rows_at, :], solid[SHEAR, z, rows_at, :]):
                value = tension[comp, z + ZPAD, rows_at, :] + change
                if final:
                    str_out[comp, z] = value
                else:
                    tension[comp, z + ZPAD, rows_at, :] = value
            if final:
                exx, eyy, ezz, gxy, gxz, gyz = strained
                f = [strain[comp, z].astype(jnp.float32) for comp in range(6)]
                a = [accel[comp, z].astype(jnp.float32) for comp in range(3)]
                v = [speed[comp, z + ZPAD, inner, :] for comp in range(3)]
                kern_out[0, z] = kern[0, z] - STEP_DT * (f[SXX] + f[SYY] + f[SZZ]) * (exx + eyy + ezz)
                kern_out[1, z] = kern[1, z] - 2.0 * STEP_DT * (
                    f[SXX] * exx + f[SYY] * eyy + f[SZZ] * ezz + f[SXY] * gxy + f[SXZ] * gxz + f[SYZ] * gyz
                )
                kern_out[2, z] = kern[2, z] - STEP_DT * (a[0] * v[0] + a[1] * v[1] + a[2] * v[2])
            return 0

        lax.fori_loop(0, depth, plane, 0, unroll=True)
        if margin > 0:
            near = margin // 2
            near_at = pl.ds(MARGIN - near, width + 2 * near)
            strained = strains(*wing_part(MARGIN - near, width + 2 * near))
            for comp, change in changes(strained, solid_wing[LAME, near_at, :], solid_wing[SHEAR, near_at, :]):
                tension_wing[comp, near_at, :] = tension_wing[comp, near_at, :] + change

    loads[3].wait()
    near_x, near_y = (SXX, SXZ, SXY), (SXY, SYY, SYZ)
    near_fields = [(tension, comp, ZPAD) for comp in near_x]
    near_wings = [(tension_wing, comp) for comp in near_y]
    pack_faces(NEAR_START, near_fields, [(tension, comp, ZPAD) for comp in near_y])
    pl.semaphore_wait(barrier, size_a + size_b - 2 + len(around))

    def hop_a(i):
        to, target = partners_a[i]
        return pltpu.make_async_remote_copy(
            src_ref=packed.at[to],
            dst_ref=first_hop.at[lax.rem(my_a, CAP), :, my_a // CAP],
            send_sem=hop_send.at[0, i + 1],
            recv_sem=hop_recv.at[0, i + 1],
            device_id=target,
            device_id_type=MESH,
        )

    def hop_b(i):
        to, target = partners_b[i]
        return pltpu.make_async_remote_copy(
            src_ref=regrouped.at[to // CAP, lax.rem(to, CAP)],
            dst_ref=second_hop.at[my_b],
            send_sem=hop_send.at[1, i + 1],
            recv_sem=hop_recv.at[1, i + 1],
            device_id=target,
            device_id_type=MESH,
        )

    hops_a = [hop_a(i) for i in range(size_a - 1)]
    hops_b = [hop_b(i) for i in range(size_b - 1)]
    for copy in hops_a:
        copy.start()
    own_a = pltpu.make_async_copy(
        packed.at[my_a], first_hop.at[lax.rem(my_a, CAP), :, my_a // CAP], hop_recv.at[0, 0]
    )
    own_a.start()
    send_faces(NEAR_START)
    for load in loads[5:8]:
        load.wait()
    wide_fields = [(tension, comp, ZPAD) for comp in range(6)] + [(solid, comp, 0) for comp in range(3)]
    wide_wings = [(tension_wing, comp) for comp in range(6)] + [(solid_wing, comp) for comp in range(3)]
    pack_faces(WIDE_START, wide_fields, wide_fields)
    own_a.wait()
    for copy in reversed(hops_a):
        copy.wait_recv()
    heaps = [first_hop[p].reshape(lines // CAP, LANES) for p in range(CAP)]
    span = CAP * FEATURES
    lane_hop = lax.broadcasted_iota(jnp.int32, (lines // CAP, LANES), 1)
    for low in range(CAP):
        merged = None
        for p in range(CAP):
            shift = (span * (p - low)) % LANES
            turned = heaps[p] if shift == 0 else pltpu.roll(heaps[p], shift, 1)
            merged = turned if p == 0 else jnp.where(lane_hop >= span * p, turned, merged)
        regrouped[:, low] = merged.reshape(size_b // CAP, size_a // CAP, 1, LANES)
    for copy in hops_b:
        copy.start()
    own_b = pltpu.make_async_copy(
        regrouped.at[my_b // CAP, lax.rem(my_b, CAP)], second_hop.at[my_b], hop_recv.at[1, 0]
    )
    own_b.start()

    send_faces(WIDE_START)
    take_faces(NEAR_START, near_fields, near_wings)
    loads[4].wait()
    push_speed(0, 0, False)

    own_b.wait()
    for copy in reversed(hops_b):
        copy.wait_recv()
    arrived = second_hop[...].reshape(lines, LANES)
    arrived = jnp.concatenate([arrived, pltpu.roll(arrived, LANES // 2, 1)], axis=0).T
    heap = LANES // 2 // FEATURES
    values = jnp.concatenate([arrived[g * FEATURES : (g + 1) * FEATURES] for g in range(heap)], axis=1)
    entries = CAP * tiles
    row_of = lax.broadcasted_iota(jnp.int32, (depth * width, entries), 0).astype(jnp.float32)
    col_of = lax.broadcasted_iota(jnp.int32, (LANES, entries), 0).astype(jnp.float32)
    spot_rows[...] = (row_of == values[samples : samples + 1]).astype(jnp.float32).astype(jnp.bfloat16)
    spot_cols[...] = (col_of == values[samples + 1 : samples + 2]).astype(jnp.float32).astype(jnp.bfloat16)
    amounts = pieces(values)

    def lay_sources(step):
        columns = spot_cols[...]
        total = jnp.zeros((depth * width, 3 * LANES), jnp.float32)
        for amount in amounts:
            spread = [columns * amount[3 * step + k : 3 * step + k + 1, :] for k in range(3)]
            total = total + dot_nt(spot_rows[...], jnp.concatenate(spread, axis=0))
        for k in range(3):
            source[3 * step + k, :, inner, :] = total[:, k * LANES : (k + 1) * LANES].reshape(depth, width, LANES)

    lay_sources(0)
    add_source(0)
    speed_fields = [(speed, comp, ZPAD) for comp in range(3)]
    pack_faces(WIDE_SPEED, speed_fields, speed_fields)
    send_faces(WIDE_SPEED)
    lay_sources(1)
    late_fields = [(source, 3 + comp, 0) for comp in range(3)]
    pack_faces(LATE_SOURCE, late_fields, late_fields)
    send_faces(LATE_SOURCE)
    for load in loads[8:]:
        load.wait()
    take_faces(WIDE_START, wide_fields, wide_wings)
    take_faces(WIDE_SPEED, speed_fields, [(speed_wing, comp) for comp in range(3)])
    push_stress(4, False)
    take_faces(LATE_SOURCE, late_fields, [(source_wing, comp) for comp in range(3)])
    push_speed(2, 1, True)
    push_stress(0, True)
    for copy in hops_a + hops_b:
        copy.wait_send()
    for e in range(4):
        for copy in face_copies(e):
            copy.wait_send()


def deliver(*refs):
    sources, targets, sems = refs[:3], refs[3:6], refs[6]
    copies = [pltpu.make_async_copy(src, dst, sems.at[i]) for i, (src, dst) in enumerate(zip(sources, targets))]
    for copy in copies:
        copy.start()
    for copy in copies:
        copy.wait()


def body(
    velocity,
    stress,
    lame_first,
    shear,
    buoyancy,
    fwd_strain,
    fwd_accel,
    kernels,
    station_trace,
    station_tile,
    station_cell,
    station_count,
):
    n_x, n_y = lax.axis_size("gx"), lax.axis_size("gy")
    depth, width, lanes = buoyancy.shape
    rows = station_trace.shape[0]
    tiles = n_x * n_y
    exchanges = ((3, 2, 0), (9, 4, 1), (3, 6, 1), (3, 2, 0))
    padded = (depth + 2 * ZPAD, width + 2 * MARGIN, lanes)
    f32, b16 = jnp.float32, jnp.bfloat16
    far = pl.BlockSpec(memory_space=pltpu.HBM)
    results = pl.pallas_call(
        functools.partial(kernel, n_x, n_y),
        out_shape=[
            pltpu.VMEM(velocity.shape, f32),
            pltpu.VMEM(stress.shape, f32),
            pltpu.VMEM(kernels.shape, f32),
        ],
        in_specs=[far] * 11 + [pl.BlockSpec(memory_space=pltpu.SMEM)],
        out_specs=[pl.BlockSpec(memory_space=pltpu.VMEM)] * 3,
        scratch_shapes=[
            pltpu.VMEM((3, *padded), f32),
            pltpu.VMEM((6, *padded), f32),
            pltpu.VMEM((3, depth, *padded[1:]), f32),
            pltpu.VMEM(fwd_strain.shape, b16),
            pltpu.VMEM(fwd_accel.shape, b16),
            pltpu.VMEM(kernels.shape, f32),
            pltpu.VMEM(station_trace.shape[::-1], f32),
            pltpu.VMEM((1, rows), jnp.int32),
            pltpu.VMEM((1, rows), jnp.int32),
            pltpu.VMEM((3 * STEPS, depth, *padded[1:]), f32),
            pltpu.VMEM((FEATURES, rows), f32),
            pltpu.VMEM((n_x, n_y // CAP, 1, lanes), f32),
            pltpu.VMEM((CAP, n_y // CAP, n_x // CAP, 1, lanes), f32),
            pltpu.VMEM((n_y // CAP, CAP, n_x // CAP, 1, lanes), f32),
            pltpu.VMEM((n_y, n_x // CAP, 1, lanes), f32),
            pltpu.VMEM((depth * width, CAP * tiles), b16),
            pltpu.VMEM((lanes, CAP * tiles), b16),
            *[pltpu.VMEM((fields, *padded[1:]), f32) for fields in (3, 6, 3, 3)],
            *[pltpu.VMEM((2, fields * (depth + wings), reach, lanes), f32) for fields, reach, wings in exchanges],
            *[pltpu.VMEM((2, fields * (depth + wings), reach, lanes), f32) for fields, reach, wings in exchanges],
            *[pltpu.VMEM((fields, width, lanes), f32) for fields, reach, wings in exchanges],
            *[pltpu.VMEM((2, fields, width, lanes), f32) for fields, reach, wings in exchanges],
            *[pltpu.VMEM((2, 2, fields, reach, lanes), f32) for fields, reach, wings in exchanges],
            pltpu.SemaphoreType.DMA((11,)),
            pltpu.SemaphoreType.DMA((2, max(n_x, n_y))),
            pltpu.SemaphoreType.DMA((2, max(n_x, n_y))),
            pltpu.SemaphoreType.DMA((len(exchanges), 8)),
            pltpu.SemaphoreType.DMA((len(exchanges), 8)),
        ],
        compiler_params=pltpu.CompilerParams(
            collective_id=0, has_side_effects=True, vmem_limit_bytes=48 * 1024 * 1024
        ),
    )(
        *(
            pltpu.with_memory_space_constraint(array, pltpu.HBM)
            for array in (
                velocity,
                stress,
                lame_first,
                shear,
                buoyancy,
                fwd_strain,
                fwd_accel,
                kernels,
                station_trace.T,
                station_tile.reshape(1, rows),
                station_cell.reshape(1, rows),
            )
        ),
        station_count,
    )
    return pl.pallas_call(
        deliver,
        out_shape=[pltpu.HBM(array.shape, f32) for array in (velocity, stress, kernels)],
        in_specs=[pl.BlockSpec(memory_space=pltpu.VMEM)] * 3,
        out_specs=[far] * 3,
        scratch_shapes=[pltpu.SemaphoreType.DMA((3,))],
    )(*(pltpu.with_memory_space_constraint(array, pltpu.VMEM) for array in results))


def solution(mesh):
    tiled = P(None, None, "gx", "gy")
    plane = P(None, "gx", "gy")
    listed = ("gx", "gy")
    return jax.shard_map(
        body,
        mesh=mesh,
        in_specs=(
            tiled,
            tiled,
            plane,
            plane,
            plane,
            tiled,
            tiled,
            tiled,
            P(listed, None),
            P(listed, None),
            P(listed),
            P(listed),
        ),
        out_specs=(tiled, tiled, tiled),
        check_vma=False,
    )
```

```python
import functools

import jax
import jax.numpy as jnp
from jax import lax
from jax.experimental import pallas as pl
from jax.experimental.pallas import tpu as pltpu
from jax.sharding import PartitionSpec as P

STEPS = 2
CAP = 4
C_NEAR = 9.0 / 8.0
C_FAR = -1.0 / 24.0
STEP_DT = 0.25
MESH = pl.DeviceIdType.MESH

LANES = 128
FEATURES = 8
MARGIN = 8
ZPAD = 2
SXX, SXZ, SXY, SYY, SYZ, SZZ = range(6)
LAME, SHEAR, BUOY = range(3)
NEAR_START, WIDE_START, WIDE_SPEED, LATE_SOURCE = range(4)
STRIP = 10
KEPT = 4
REACH = STRIP - KEPT
WINGS = LANES // 2 - 4


def pieces(value):
    high = value.astype(jnp.bfloat16)
    rest = value - high.astype(jnp.float32)
    middle = rest.astype(jnp.bfloat16)
    low = (rest - middle.astype(jnp.float32)).astype(jnp.bfloat16)
    return high, middle, low


def dot_nt(left, right):
    return lax.dot_general(left, right, (((1,), (1,)), ((), ())), preferred_element_type=jnp.float32)


def kernel(
    n_x,
    n_y,
    vel_in,
    str_in,
    lame_in,
    shear_in,
    buoy_in,
    strain_in,
    accel_in,
    kern_in,
    trace_in,
    tile_in,
    cell_in,
    count,
    vel_out,
    str_out,
    kern_out,
    speed,
    tension,
    solid,
    strain,
    accel,
    kern,
    trace,
    tile,
    cell,
    source,
    payload,
    packed,
    first_hop,
    regrouped,
    second_hop,
    spot_rows,
    spot_cols,
    speed_wing,
    tension_wing,
    solid_wing,
    source_wing,
    band,
    choice,
    slopes,
    *rest,
):
    x_send, x_recv, wing_send, wing_recv, corner_recv = (rest[4 * i : 4 * i + 4] for i in range(5))
    in_sem, hop_send, hop_recv, face_send, face_recv = rest[20:]
    depth, width = buoy_in.shape[0], buoy_in.shape[1]
    rows = trace.shape[1]
    tiles = n_x * n_y
    gx, gy = lax.axis_index("gx"), lax.axis_index("gy")
    inner = pl.ds(MARGIN, width)
    planes = pl.ds(ZPAD, depth)

    half_x, half_y = n_x // 2, n_y // 2
    my_a = lax.rem(gx, half_x) * 2 + lax.rem(gy, 2)
    my_b = (gx // half_x) * half_y + gy // 2
    size_a, size_b = n_x, n_y

    quarter_y = n_y // 4
    high_y, low_y = gx // half_x, gy // half_y

    def around_ring(size):
        return lambda step: -min(step, size - step)

    offsets_a = [(dz, dc) for dz in sorted(range(half_x), key=around_ring(half_x)) for dc in range(2)][:-2] + [(0, 1)]
    offsets_b = sorted(
        ((dy, dx) for dy in range(4) for dx in range(quarter_y) if dy + dx > 0),
        key=lambda step: around_ring(4)(step[0]) + around_ring(quarter_y)(step[1]),
    )

    def partner_a(i):
        dz, dc = offsets_a[i]
        near = lax.rem(lax.rem(gx, half_x) + dz, half_x)
        core = lax.rem(gy + dc, 2)
        return near * 2 + core, ((gx // half_x) * half_x + near, (gy // 2) * 2 + core)

    def partner_b(i):
        dy, dx = offsets_b[i]
        line = lax.rem(high_y * 2 + low_y + dy, 4)
        spot = lax.rem(lax.rem(gy, half_y) // 2 + dx, quarter_y)
        outer = lax.rem(line, 2) * quarter_y + spot
        return (line // 2) * half_y + outer, (
            (line // 2) * half_x + lax.rem(gx, half_x),
            outer * 2 + lax.rem(gy, 2),
        )

    up_x = (lax.rem(gx + 1, n_x), gy)
    down_x = (lax.rem(gx + n_x - 1, n_x), gy)
    up_y = (gx, lax.rem(gy + 1, n_y))
    down_y = (gx, lax.rem(gy + n_y - 1, n_y))
    corners = tuple((x, y) for x in (down_x[0], up_x[0]) for y in (down_y[1], up_y[1]))
    around = (down_x, up_x, down_y, up_y) + corners

    barrier = pltpu.get_barrier_semaphore()

    partners_a = [partner_a(i) for i in range(size_a - 1)]
    partners_b = [partner_b(i) for i in range(size_b - 1)]
    for _, target in partners_a + partners_b:
        pl.semaphore_signal(barrier, inc=1, device_id=target, device_id_type=MESH)
    for target in around:
        pl.semaphore_signal(barrier, inc=1, device_id=target, device_id_type=MESH)

    loads = [
        pltpu.make_async_copy(src, dst, in_sem.at[i])
        for i, (src, dst) in enumerate(
            (
                (trace_in, trace),
                (tile_in, tile),
                (cell_in, cell),
                (str_in, tension.at[:, planes, inner, :]),
                (vel_in, speed.at[:, planes, inner, :]),
                (buoy_in, solid.at[BUOY, :, inner, :]),
                (lame_in, solid.at[LAME, :, inner, :]),
                (shear_in, solid.at[SHEAR, :, inner, :]),
                (strain_in, strain),
                (accel_in, accel),
                (kern_in, kern),
            )
        )
    ]
    for load in loads:
        load.start()


    blank = jnp.zeros((ZPAD, width + 2 * MARGIN, LANES), jnp.float32)
    for ref, comps in ((speed, (0, 1, 2)), (tension, (SXZ, SYZ, SZZ))):
        for comp in comps:
            ref[comp, pl.ds(0, ZPAD)] = blank
            ref[comp, pl.ds(ZPAD + depth, ZPAD)] = blank

    for load in loads[:3]:
        load.wait()
    names = tile[...]
    line = lax.broadcasted_iota(jnp.int32, (tiles, rows), 0)
    named = (line == names).astype(jnp.float32)
    named_16 = named.astype(jnp.bfloat16)
    earlier = (
        lax.broadcasted_iota(jnp.int32, (rows, rows), 0) < lax.broadcasted_iota(jnp.int32, (rows, rows), 1)
    ).astype(jnp.float32).astype(jnp.bfloat16)
    ahead = jnp.dot(named_16, earlier, preferred_element_type=jnp.float32)
    slot = jnp.sum(named * ahead, axis=0, keepdims=True)
    live = lax.broadcasted_iota(jnp.int32, (1, rows), 1) < count[0]
    cells = cell[...]
    samples = trace.shape[0]
    payload[pl.ds(0, samples), :] = jnp.where(live, trace[...], 0.0)
    payload[pl.ds(samples, 1), :] = (cells // LANES).astype(jnp.float32)
    payload[pl.ds(samples + 1, 1), :] = (cells % LANES).astype(jnp.float32)
    load_all = payload[...]
    at_x, at_y = names // n_y, lax.rem(names, n_y)
    to_a = lax.rem(at_x, half_x) * 2 + lax.rem(at_y, 2)
    to_b = (at_x // half_x) * half_y + at_y // 2
    row_to = to_a * (size_b // CAP) + to_b // CAP
    group = lax.rem(to_b, CAP).astype(jnp.float32) * CAP + slot
    spread = [jnp.where((group == float(g)) & (slot < CAP), load_all, 0.0) for g in range(CAP * CAP)]
    bundle = jnp.concatenate(spread, axis=0)
    lines = size_a * size_b // CAP
    aimed = (lax.broadcasted_iota(jnp.int32, (lines, rows), 0) == row_to).astype(jnp.float32).astype(jnp.bfloat16)
    outgoing = sum(dot_nt(aimed, piece) for piece in pieces(bundle))
    packed[...] = outgoing.reshape(size_a, size_b // CAP, 1, LANES)

    lane_row = lax.broadcasted_iota(jnp.int32, (1, LANES), 1)
    turn = lax.rem(lane_row, STRIP)
    level = lax.rem(lane_row // STRIP, depth)
    from_up = (lane_row < WINGS) & (turn >= KEPT)
    from_down = (lane_row >= WINGS) & (turn < REACH)
    below = MARGIN + width

    def by_pieces(parts, matrix):
        count = parts[0].shape[0]
        total = jnp.dot(jnp.concatenate(parts, axis=0), matrix, preferred_element_type=jnp.float32)
        return (total[2 * count :] + total[count : 2 * count]) + total[:count]

    def build_choice():
        row = lax.broadcasted_iota(jnp.int32, (LANES, LANES), 0)
        column = lax.broadcasted_iota(jnp.int32, (LANES, LANES), 1)
        high, low = lax.rem(row + KEPT, LANES), lax.rem(row + REACH, LANES)

        def block(z, _):
            first = (high < STRIP) & (column == z * STRIP + high)
            second = (low < STRIP) & (column == WINGS + z * STRIP + low)
            choice[pl.ds(z * LANES, LANES), :] = (first | second).astype(jnp.float32).astype(jnp.bfloat16)
            return 0

        lax.fori_loop(0, depth, block, 0, unroll=True)

    def build_band():
        row = lax.broadcasted_iota(jnp.int32, (LANES, LANES), 0)
        column = lax.broadcasted_iota(jnp.int32, (LANES, LANES), 1)

        def weights(away, upward):
            near, far = 24.0 * C_NEAR, -24.0 * C_FAR
            ahead = away if upward else away + 1
            value = jnp.where(ahead == 1, near, 0.0) + jnp.where(ahead == 0, -near, 0.0)
            value = value + jnp.where(ahead == 2, -far, 0.0) + jnp.where(ahead == -1, far, 0.0)
            return value.astype(jnp.bfloat16)

        for side, upward in enumerate((False, True)):
            centre = weights(row - column, upward)

            def block(z, _, side=side, upward=upward, centre=centre):
                band[side, z, pl.ds(0, LANES), :] = centre
                high = row - z * STRIP
                low = row - WINGS - z * STRIP
                place = jnp.where(
                    (high >= KEPT) & (high < STRIP),
                    high + LANES - KEPT,
                    jnp.where((low >= 0) & (low < REACH), low - REACH, 4 * LANES),
                )
                band[side, z, pl.ds(LANES, LANES), :] = weights(place - column, upward)
                return 0

            lax.fori_loop(0, depth, block, 0, unroll=True)

    def take_slopes(ref, wing, fields, start, count):
        rows_at = pl.ds(start, count)
        for k, (comp, upward) in enumerate(fields):
            edge = pieces(wing[comp, rows_at, :])

            def plane(z, _, k=k, comp=comp, upward=upward, edge=edge):
                core = pieces(ref[comp, z + ZPAD, rows_at, :])
                both = [jnp.concatenate([a, b], axis=1) for a, b in zip(core, edge)]
                slopes[k, z, rows_at, :] = by_pieces(both, band[int(upward), z]) * (1.0 / 24.0)
                return 0

            lax.fori_loop(0, depth, plane, 0, unroll=True)

    def has_corners(e):
        return e in (WIDE_SPEED, WIDE_START)

    def face_copies(e):
        strips = x_send[e].shape[1]
        count = wing_send[e].shape[0]
        tail = pl.ds(strips - count, count)
        moves = [
            (x_send[e].at[0], x_recv[e].at[0], down_x),
            (x_send[e].at[1], x_recv[e].at[1], up_x),
            (wing_send[e], wing_recv[e].at[0], down_y),
            (wing_send[e], wing_recv[e].at[1], up_y),
        ]
        if has_corners(e):
            for k, target in enumerate(corners):
                moves.append((x_send[e].at[k // 2, tail], corner_recv[e].at[k // 2, k % 2], target))
        return [
            pltpu.make_async_remote_copy(
                src_ref=src,
                dst_ref=dst,
                send_sem=face_send.at[e, k],
                recv_sem=face_recv.at[e, k],
                device_id=target,
                device_id_type=MESH,
            )
            for k, (src, dst, target) in enumerate(moves)
        ]

    def pack_faces(e, x_fields, wing_fields):
        reach = x_send[e].shape[2]
        for i, (ref, comp, first) in enumerate(x_fields):
            def rows_of(z, _, i=i, ref=ref, comp=comp, first=first):
                x_send[e][0, i * depth + z] = ref[comp, z + first, pl.ds(MARGIN, reach), :]
                x_send[e][1, i * depth + z] = ref[comp, z + first, pl.ds(below - reach, reach), :]
                return 0

            lax.fori_loop(0, depth, rows_of, 0, unroll=True)
        for i, (ref, comp, first) in enumerate(wing_fields):
            planes_of = [pieces(ref[comp, z + first, inner, :]) for z in range(depth)]
            wing = by_pieces([jnp.concatenate([parts[k] for parts in planes_of], axis=1) for k in range(3)], choice[...])
            wing_send[e][i] = wing
            if has_corners(e):
                x_send[e][0, len(x_fields) * depth + i] = wing[:reach]
                x_send[e][1, len(x_fields) * depth + i] = wing[width - reach :]

    def send_faces(e):
        for copy in face_copies(e):
            copy.start()

    def take_faces(e, x_fields, wing_fields):
        reach = x_send[e].shape[2]
        for copy in face_copies(e):
            copy.wait_recv()

        def clear(at_edge, *refs):
            @pl.when(at_edge)
            def _():
                for ref in refs:
                    ref[...] = jnp.zeros(ref.shape, jnp.float32)

        corner = corner_recv[e]
        both = has_corners(e)
        clear(gy == n_y - 1, wing_recv[e].at[0], *([corner.at[0, 0], corner.at[1, 0]] if both else []))
        clear(gy == 0, wing_recv[e].at[1], *([corner.at[0, 1], corner.at[1, 1]] if both else []))
        clear(gx == n_x - 1, x_recv[e].at[0], *([corner.at[0]] if both else []))
        clear(gx == 0, x_recv[e].at[1], *([corner.at[1]] if both else []))

        def mixed(up, down, own):
            return jnp.where(from_up, up, jnp.where(from_down, down, own))

        for i, (ref, comp, first) in enumerate(x_fields):
            def rows_of(z, _, i=i, ref=ref, comp=comp, first=first):
                ref[comp, z + first, pl.ds(below, reach), :] = x_recv[e][0, i * depth + z]
                ref[comp, z + first, pl.ds(MARGIN - reach, reach), :] = x_recv[e][1, i * depth + z]
                return 0

            lax.fori_loop(0, depth, rows_of, 0, unroll=True)
        for i, (wing, at) in enumerate(wing_fields):
            wing[at, inner, :] = mixed(wing_recv[e][0, i], wing_recv[e][1, i], wing_send[e][i])
            if both:
                for side, start in ((0, below), (1, MARGIN - reach)):
                    wing[at, pl.ds(start, reach), :] = mixed(
                        corner[side, 0, i], corner[side, 1, i], x_recv[e][side, len(x_fields) * depth + i]
                    )

    def difference(at, upward):
        if upward:
            return C_NEAR * (at(1) - at(0)) + C_FAR * (at(2) - at(-1))
        return C_NEAR * (at(0) - at(-1)) + C_FAR * (at(1) - at(-2))

    def tile_part(z, start, count):
        def along_z(ref, comp, upward):
            return difference(lambda o: ref[comp, z + ZPAD + o, pl.ds(start, count), :], upward)

        def along_x(ref, comp, upward):
            return difference(lambda o: ref[comp, z + ZPAD, pl.ds(start + o, count), :], upward)

        def along_y(ref, comp, upward):
            del upward
            return slopes[comp if ref is speed else comp - SXY, z, pl.ds(start, count), :]

        return along_x, along_y, along_z

    def wing_part(start, count):
        def held(ref, comp, o=0):
            return (speed_wing if ref is speed else tension_wing)[comp, pl.ds(start + o, count), :]

        def along_z(ref, comp, upward):
            value = held(ref, comp)

            def at(o):
                if o == 0:
                    return value
                inside = (level + o >= 0) & (level + o < depth)
                return jnp.where(inside, pltpu.roll(value, (-o * STRIP) % LANES, 1), 0.0)

            return difference(at, upward)

        def along_x(ref, comp, upward):
            return difference(lambda o: held(ref, comp, o), upward)

        def along_y(ref, comp, upward):
            value = held(ref, comp)
            return difference(lambda o: value if o == 0 else pltpu.roll(value, -o % LANES, 1), upward)

        return along_x, along_y, along_z

    def rates(along_x, along_y, along_z):
        return (
            along_x(tension, SXX, True) + along_y(tension, SXY, False) + along_z(tension, SXZ, False),
            along_x(tension, SXY, False) + along_y(tension, SYY, True) + along_z(tension, SYZ, False),
            along_x(tension, SXZ, False) + along_y(tension, SYZ, False) + along_z(tension, SZZ, True),
        )

    def strains(along_x, along_y, along_z):
        exx = along_x(speed, 0, False)
        eyy = along_y(speed, 1, False)
        ezz = along_z(speed, 2, False)
        gxy = along_y(speed, 0, True) + along_x(speed, 1, True)
        gxz = along_z(speed, 0, True) + along_x(speed, 2, True)
        gyz = along_z(speed, 1, True) + along_y(speed, 2, True)
        return exx, eyy, ezz, gxy, gxz, gyz

    def changes(strained, lame, shear):
        exx, eyy, ezz, gxy, gxz, gyz = strained
        stiff = STEP_DT * shear
        common = STEP_DT * lame * (exx + eyy + ezz)
        return (
            (SXX, common + 2.0 * stiff * exx),
            (SYY, common + 2.0 * stiff * eyy),
            (SZZ, common + 2.0 * stiff * ezz),
            (SXY, stiff * gxy),
            (SXZ, stiff * gxz),
            (SYZ, stiff * gyz),
        )

    def matrix_rows(margin):
        return (0, width + 2 * MARGIN) if margin > 0 else (MARGIN, width)

    def push_speed(margin, step, final):
        start, count = MARGIN - margin, width + 2 * margin
        take_slopes(tension, tension_wing, ((SXY, False), (SYY, True), (SYZ, False)), *matrix_rows(margin))
        rows_at = pl.ds(start, count)

        def plane(z, _):
            factor = STEP_DT * solid[BUOY, z, rows_at, :]
            for k, rate in enumerate(rates(*tile_part(z, start, count))):
                if step > 0:
                    rate = rate + source[3 * step + k, z, rows_at, :]
                value = speed[k, z + ZPAD, rows_at, :] + factor * rate
                speed[k, z + ZPAD, rows_at, :] = value
                if final:
                    vel_out[k, z] = value[margin : margin + width]
            return 0

        lax.fori_loop(0, depth, plane, 0, unroll=True)
        if margin > 0:
            factor = STEP_DT * solid_wing[BUOY, inner, :]
            for k, rate in enumerate(rates(*wing_part(MARGIN, width))):
                change = factor * (rate + source_wing[k, inner, :])
                speed_wing[k, inner, :] = speed_wing[k, inner, :] + change

    def add_source(step):
        def plane(z, _):
            factor = STEP_DT * solid[BUOY, z, inner, :]
            for k in range(3):
                speed[k, z + ZPAD, inner, :] = (
                    speed[k, z + ZPAD, inner, :] + factor * source[3 * step + k, z, inner, :]
                )
            return 0

        lax.fori_loop(0, depth, plane, 0, unroll=True)

    def push_stress(margin, final):
        start, count = MARGIN - margin, width + 2 * margin
        take_slopes(speed, speed_wing, ((0, True), (1, False), (2, True)), *matrix_rows(margin))
        rows_at = pl.ds(start, count)

        def plane(z, _):
            strained = strains(*tile_part(z, start, count))
            for comp, change in changes(strained, solid[LAME, z, rows_at, :], solid[SHEAR, z, rows_at, :]):
                value = tension[comp, z + ZPAD, rows_at, :] + change
                if final:
                    str_out[comp, z] = value
                else:
                    tension[comp, z + ZPAD, rows_at, :] = value
            if final:
                exx, eyy, ezz, gxy, gxz, gyz = strained
                f = [strain[comp, z].astype(jnp.float32) for comp in range(6)]
                a = [accel[comp, z].astype(jnp.float32) for comp in range(3)]
                v = [speed[comp, z + ZPAD, inner, :] for comp in range(3)]
                kern_out[0, z] = kern[0, z] - STEP_DT * (f[SXX] + f[SYY] + f[SZZ]) * (exx + eyy + ezz)
                kern_out[1, z] = kern[1, z] - 2.0 * STEP_DT * (
                    f[SXX] * exx + f[SYY] * eyy + f[SZZ] * ezz + f[SXY] * gxy + f[SXZ] * gxz + f[SYZ] * gyz
                )
                kern_out[2, z] = kern[2, z] - STEP_DT * (a[0] * v[0] + a[1] * v[1] + a[2] * v[2])
            return 0

        lax.fori_loop(0, depth, plane, 0, unroll=True)
        if margin > 0:
            near = margin // 2
            near_at = pl.ds(MARGIN - near, width + 2 * near)
            strained = strains(*wing_part(MARGIN - near, width + 2 * near))
            for comp, change in changes(strained, solid_wing[LAME, near_at, :], solid_wing[SHEAR, near_at, :]):
                tension_wing[comp, near_at, :] = tension_wing[comp, near_at, :] + change

    pl.semaphore_wait(barrier, size_a + size_b - 2 + len(around))

    def hop_a(i):
        to, target = partners_a[i]
        return pltpu.make_async_remote_copy(
            src_ref=packed.at[to],
            dst_ref=first_hop.at[lax.rem(my_a, CAP), :, my_a // CAP],
            send_sem=hop_send.at[0, i + 1],
            recv_sem=hop_recv.at[0, i + 1],
            device_id=target,
            device_id_type=MESH,
        )

    def hop_b(i):
        to, target = partners_b[i]
        return pltpu.make_async_remote_copy(
            src_ref=regrouped.at[to // CAP, lax.rem(to, CAP)],
            dst_ref=second_hop.at[my_b],
            send_sem=hop_send.at[1, i + 1],
            recv_sem=hop_recv.at[1, i + 1],
            device_id=target,
            device_id_type=MESH,
        )

    hops_a = [hop_a(i) for i in range(size_a - 1)]
    hops_b = [hop_b(i) for i in range(size_b - 1)]
    for copy in hops_a:
        copy.start()
    own_a = pltpu.make_async_copy(
        packed.at[my_a], first_hop.at[lax.rem(my_a, CAP), :, my_a // CAP], hop_recv.at[0, 0]
    )
    own_a.start()
    build_choice()
    loads[3].wait()
    near_x, near_y = (SXX, SXZ, SXY), (SXY, SYY, SYZ)
    near_fields = [(tension, comp, ZPAD) for comp in near_x]
    near_wings = [(tension_wing, comp) for comp in near_y]
    pack_faces(NEAR_START, near_fields, [(tension, comp, ZPAD) for comp in near_y])
    send_faces(NEAR_START)
    build_band()
    for load in loads[5:8]:
        load.wait()
    wide_fields = [(tension, comp, ZPAD) for comp in range(6)] + [(solid, comp, 0) for comp in range(3)]
    wide_wings = [(tension_wing, comp) for comp in range(6)] + [(solid_wing, comp) for comp in range(3)]
    pack_faces(WIDE_START, wide_fields, wide_fields)
    own_a.wait()
    for copy in reversed(hops_a):
        copy.wait_recv()
    heaps = [first_hop[p].reshape(lines // CAP, LANES) for p in range(CAP)]
    span = CAP * FEATURES
    lane_hop = lax.broadcasted_iota(jnp.int32, (lines // CAP, LANES), 1)
    for low in range(CAP):
        merged = None
        for p in range(CAP):
            shift = (span * (p - low)) % LANES
            turned = heaps[p] if shift == 0 else pltpu.roll(heaps[p], shift, 1)
            merged = turned if p == 0 else jnp.where(lane_hop >= span * p, turned, merged)
        regrouped[:, low] = merged.reshape(size_b // CAP, size_a // CAP, 1, LANES)
    for copy in hops_b:
        copy.start()
    own_b = pltpu.make_async_copy(
        regrouped.at[my_b // CAP, lax.rem(my_b, CAP)], second_hop.at[my_b], hop_recv.at[1, 0]
    )
    own_b.start()

    send_faces(WIDE_START)
    take_faces(NEAR_START, near_fields, near_wings)
    loads[4].wait()
    push_speed(0, 0, False)

    own_b.wait()
    for copy in reversed(hops_b):
        copy.wait_recv()
    arrived = second_hop[...].reshape(lines, LANES)
    arrived = jnp.concatenate([arrived, pltpu.roll(arrived, LANES // 2, 1)], axis=0).T
    heap = LANES // 2 // FEATURES
    values = jnp.concatenate([arrived[g * FEATURES : (g + 1) * FEATURES] for g in range(heap)], axis=1)
    entries = CAP * tiles
    row_of = lax.broadcasted_iota(jnp.int32, (depth * width, entries), 0).astype(jnp.float32)
    col_of = lax.broadcasted_iota(jnp.int32, (LANES, entries), 0).astype(jnp.float32)
    spot_rows[...] = (row_of == values[samples : samples + 1]).astype(jnp.float32).astype(jnp.bfloat16)
    spot_cols[...] = (col_of == values[samples + 1 : samples + 2]).astype(jnp.float32).astype(jnp.bfloat16)
    amounts = pieces(values)

    def lay_sources(step):
        columns = spot_cols[...]
        total = jnp.zeros((depth * width, 3 * LANES), jnp.float32)
        for amount in amounts:
            spread = [columns * amount[3 * step + k : 3 * step + k + 1, :] for k in range(3)]
            total = total + dot_nt(spot_rows[...], jnp.concatenate(spread, axis=0))
        for k in range(3):
            source[3 * step + k, :, inner, :] = total[:, k * LANES : (k + 1) * LANES].reshape(depth, width, LANES)

    lay_sources(0)
    add_source(0)
    speed_fields = [(speed, comp, ZPAD) for comp in range(3)]
    pack_faces(WIDE_SPEED, speed_fields, speed_fields)
    send_faces(WIDE_SPEED)
    lay_sources(1)
    late_fields = [(source, 3 + comp, 0) for comp in range(3)]
    pack_faces(LATE_SOURCE, late_fields, late_fields)
    send_faces(LATE_SOURCE)
    for load in loads[8:]:
        load.wait()
    take_faces(WIDE_START, wide_fields, wide_wings)
    take_faces(WIDE_SPEED, speed_fields, [(speed_wing, comp) for comp in range(3)])
    push_stress(4, False)
    take_faces(LATE_SOURCE, late_fields, [(source_wing, comp) for comp in range(3)])
    push_speed(2, 1, True)
    push_stress(0, True)
    for copy in hops_a + hops_b:
        copy.wait_send()
    for e in range(4):
        for copy in face_copies(e):
            copy.wait_send()


def deliver(*refs):
    sources, targets, sems = refs[:3], refs[3:6], refs[6]
    copies = [pltpu.make_async_copy(src, dst, sems.at[i]) for i, (src, dst) in enumerate(zip(sources, targets))]
    for copy in copies:
        copy.start()
    for copy in copies:
        copy.wait()


def body(
    velocity,
    stress,
    lame_first,
    shear,
    buoyancy,
    fwd_strain,
    fwd_accel,
    kernels,
    station_trace,
    station_tile,
    station_cell,
    station_count,
):
    n_x, n_y = lax.axis_size("gx"), lax.axis_size("gy")
    depth, width, lanes = buoyancy.shape
    rows = station_trace.shape[0]
    tiles = n_x * n_y
    exchanges = ((3, 2, 0), (9, 4, 1), (3, 6, 1), (3, 2, 0))
    padded = (depth + 2 * ZPAD, width + 2 * MARGIN, lanes)
    f32, b16 = jnp.float32, jnp.bfloat16
    far = pl.BlockSpec(memory_space=pltpu.HBM)
    results = pl.pallas_call(
        functools.partial(kernel, n_x, n_y),
        out_shape=[
            pltpu.VMEM(velocity.shape, f32),
            pltpu.VMEM(stress.shape, f32),
            pltpu.VMEM(kernels.shape, f32),
        ],
        in_specs=[far] * 11 + [pl.BlockSpec(memory_space=pltpu.SMEM)],
        out_specs=[pl.BlockSpec(memory_space=pltpu.VMEM)] * 3,
        scratch_shapes=[
            pltpu.VMEM((3, *padded), f32),
            pltpu.VMEM((6, *padded), f32),
            pltpu.VMEM((3, depth, *padded[1:]), f32),
            pltpu.VMEM(fwd_strain.shape, b16),
            pltpu.VMEM(fwd_accel.shape, b16),
            pltpu.VMEM(kernels.shape, f32),
            pltpu.VMEM(station_trace.shape[::-1], f32),
            pltpu.VMEM((1, rows), jnp.int32),
            pltpu.VMEM((1, rows), jnp.int32),
            pltpu.VMEM((3 * STEPS, depth, *padded[1:]), f32),
            pltpu.VMEM((FEATURES, rows), f32),
            pltpu.VMEM((n_x, n_y // CAP, 1, lanes), f32),
            pltpu.VMEM((CAP, n_y // CAP, n_x // CAP, 1, lanes), f32),
            pltpu.VMEM((n_y // CAP, CAP, n_x // CAP, 1, lanes), f32),
            pltpu.VMEM((n_y, n_x // CAP, 1, lanes), f32),
            pltpu.VMEM((depth * width, CAP * tiles), b16),
            pltpu.VMEM((lanes, CAP * tiles), b16),
            *[pltpu.VMEM((fields, *padded[1:]), f32) for fields in (3, 6, 3, 3)],
            pltpu.VMEM((2, depth, 2 * lanes, lanes), b16),
            pltpu.VMEM((depth * lanes, lanes), b16),
            pltpu.VMEM((3, depth, *padded[1:]), f32),
            *[pltpu.VMEM((2, fields * (depth + wings), reach, lanes), f32) for fields, reach, wings in exchanges],
            *[pltpu.VMEM((2, fields * (depth + wings), reach, lanes), f32) for fields, reach, wings in exchanges],
            *[pltpu.VMEM((fields, width, lanes), f32) for fields, reach, wings in exchanges],
            *[pltpu.VMEM((2, fields, width, lanes), f32) for fields, reach, wings in exchanges],
            *[pltpu.VMEM((2, 2, fields, reach, lanes), f32) for fields, reach, wings in exchanges],
            pltpu.SemaphoreType.DMA((11,)),
            pltpu.SemaphoreType.DMA((2, max(n_x, n_y))),
            pltpu.SemaphoreType.DMA((2, max(n_x, n_y))),
            pltpu.SemaphoreType.DMA((len(exchanges), 8)),
            pltpu.SemaphoreType.DMA((len(exchanges), 8)),
        ],
        compiler_params=pltpu.CompilerParams(
            collective_id=0, has_side_effects=True, vmem_limit_bytes=48 * 1024 * 1024
        ),
    )(
        *(
            pltpu.with_memory_space_constraint(array, pltpu.HBM)
            for array in (
                velocity,
                stress,
                lame_first,
                shear,
                buoyancy,
                fwd_strain,
                fwd_accel,
                kernels,
                station_trace.T,
                station_tile.reshape(1, rows),
                station_cell.reshape(1, rows),
            )
        ),
        station_count,
    )
    return pl.pallas_call(
        deliver,
        out_shape=[pltpu.HBM(array.shape, f32) for array in (velocity, stress, kernels)],
        in_specs=[pl.BlockSpec(memory_space=pltpu.VMEM)] * 3,
        out_specs=[far] * 3,
        scratch_shapes=[pltpu.SemaphoreType.DMA((3,))],
    )(*(pltpu.with_memory_space_constraint(array, pltpu.VMEM) for array in results))


def solution(mesh):
    tiled = P(None, None, "gx", "gy")
    plane = P(None, "gx", "gy")
    listed = ("gx", "gy")
    return jax.shard_map(
        body,
        mesh=mesh,
        in_specs=(
            tiled,
            tiled,
            plane,
            plane,
            plane,
            tiled,
            tiled,
            tiled,
            P(listed, None),
            P(listed, None),
            P(listed),
            P(listed),
        ),
        out_specs=(tiled, tiled, tiled),
        check_vma=False,
    )
```

```python
import functools

import jax
import jax.numpy as jnp
from jax import lax
from jax.experimental import pallas as pl
from jax.experimental.pallas import tpu as pltpu
from jax.sharding import PartitionSpec as P

STEPS = 2
CAP = 4
C_NEAR = 9.0 / 8.0
C_FAR = -1.0 / 24.0
STEP_DT = 0.25
MESH = pl.DeviceIdType.MESH

LANES = 128
FEATURES = 8
MARGIN = 8
ZPAD = 2
SXX, SXZ, SXY, SYY, SYZ, SZZ = range(6)
LAME, SHEAR, BUOY = range(3)
NEAR_START, WIDE_START, WIDE_SPEED, LATE_SOURCE = range(4)
STRIP = 10
KEPT = 4
REACH = STRIP - KEPT
WINGS = LANES // 2 - 4


def pieces(value):
    high = value.astype(jnp.bfloat16)
    rest = value - high.astype(jnp.float32)
    middle = rest.astype(jnp.bfloat16)
    low = (rest - middle.astype(jnp.float32)).astype(jnp.bfloat16)
    return high, middle, low


def dot_nt(left, right):
    return lax.dot_general(left, right, (((1,), (1,)), ((), ())), preferred_element_type=jnp.float32)


def kernel(
    n_x,
    n_y,
    vel_in,
    str_in,
    lame_in,
    shear_in,
    buoy_in,
    strain_in,
    accel_in,
    kern_in,
    trace_in,
    tile_in,
    cell_in,
    count,
    vel_out,
    str_out,
    kern_out,
    speed,
    tension,
    solid,
    strain,
    accel,
    kern,
    trace,
    tile,
    cell,
    source,
    payload,
    packed,
    first_hop,
    regrouped,
    second_hop,
    spot_rows,
    spot_cols,
    speed_wing,
    tension_wing,
    solid_wing,
    source_wing,
    band,
    choice,
    slopes,
    *rest,
):
    x_send, x_recv, wing_send, wing_recv, corner_recv = (rest[4 * i : 4 * i + 4] for i in range(5))
    in_sem, hop_send, hop_recv, face_send, face_recv = rest[20:]
    depth, width = buoy_in.shape[0], buoy_in.shape[1]
    rows = trace.shape[1]
    tiles = n_x * n_y
    gx, gy = lax.axis_index("gx"), lax.axis_index("gy")
    inner = pl.ds(MARGIN, width)
    planes = pl.ds(ZPAD, depth)

    half_x, half_y = n_x // 2, n_y // 2
    my_a = lax.rem(gx, half_x) * 2 + lax.rem(gy, 2)
    my_b = (gx // half_x) * half_y + gy // 2
    size_a, size_b = n_x, n_y

    quarter_y = n_y // 4
    high_y, low_y = gx // half_x, gy // half_y

    def around_ring(size):
        return lambda step: -min(step, size - step)

    offsets_a = [(dz, dc) for dz in sorted(range(half_x), key=around_ring(half_x)) for dc in range(2)][:-2] + [(0, 1)]
    offsets_b = sorted(
        ((dy, dx) for dy in range(4) for dx in range(quarter_y) if dy + dx > 0),
        key=lambda step: around_ring(4)(step[0]) + around_ring(quarter_y)(step[1]),
    )

    def partner_a(i):
        dz, dc = offsets_a[i]
        near = lax.rem(lax.rem(gx, half_x) + dz, half_x)
        core = lax.rem(gy + dc, 2)
        return near * 2 + core, ((gx // half_x) * half_x + near, (gy // 2) * 2 + core)

    def partner_b(i):
        dy, dx = offsets_b[i]
        line = lax.rem(high_y * 2 + low_y + dy, 4)
        spot = lax.rem(lax.rem(gy, half_y) // 2 + dx, quarter_y)
        outer = lax.rem(line, 2) * quarter_y + spot
        return (line // 2) * half_y + outer, (
            (line // 2) * half_x + lax.rem(gx, half_x),
            outer * 2 + lax.rem(gy, 2),
        )

    up_x = (lax.rem(gx + 1, n_x), gy)
    down_x = (lax.rem(gx + n_x - 1, n_x), gy)
    up_y = (gx, lax.rem(gy + 1, n_y))
    down_y = (gx, lax.rem(gy + n_y - 1, n_y))
    corners = tuple((x, y) for x in (down_x[0], up_x[0]) for y in (down_y[1], up_y[1]))
    can_down_x, can_up_x = gx > 0, gx < n_x - 1
    can_down_y, can_up_y = gy > 0, gy < n_y - 1
    around = (down_x, up_x, down_y, up_y) + corners

    barrier = pltpu.get_barrier_semaphore()

    partners_a = [partner_a(i) for i in range(size_a - 1)]
    partners_b = [partner_b(i) for i in range(size_b - 1)]
    for _, target in partners_a + partners_b:
        pl.semaphore_signal(barrier, inc=1, device_id=target, device_id_type=MESH)
    for target in around:
        pl.semaphore_signal(barrier, inc=1, device_id=target, device_id_type=MESH)

    loads = [
        pltpu.make_async_copy(src, dst, in_sem.at[i])
        for i, (src, dst) in enumerate(
            (
                (trace_in, trace),
                (tile_in, tile),
                (cell_in, cell),
                (str_in, tension.at[:, planes, inner, :]),
                (vel_in, speed.at[:, planes, inner, :]),
                (buoy_in, solid.at[BUOY, :, inner, :]),
                (lame_in, solid.at[LAME, :, inner, :]),
                (shear_in, solid.at[SHEAR, :, inner, :]),
                (strain_in, strain),
                (accel_in, accel),
                (kern_in, kern),
            )
        )
    ]
    for load in loads:
        load.start()


    blank = jnp.zeros((ZPAD, width + 2 * MARGIN, LANES), jnp.float32)
    for ref, comps in ((speed, (0, 1, 2)), (tension, (SXZ, SYZ, SZZ))):
        for comp in comps:
            ref[comp, pl.ds(0, ZPAD)] = blank
            ref[comp, pl.ds(ZPAD + depth, ZPAD)] = blank

    for load in loads[:3]:
        load.wait()
    names = tile[...]
    line = lax.broadcasted_iota(jnp.int32, (tiles, rows), 0)
    named = (line == names).astype(jnp.float32)
    named_16 = named.astype(jnp.bfloat16)
    earlier = (
        lax.broadcasted_iota(jnp.int32, (rows, rows), 0) < lax.broadcasted_iota(jnp.int32, (rows, rows), 1)
    ).astype(jnp.float32).astype(jnp.bfloat16)
    ahead = jnp.dot(named_16, earlier, preferred_element_type=jnp.float32)
    slot = jnp.sum(named * ahead, axis=0, keepdims=True)
    live = lax.broadcasted_iota(jnp.int32, (1, rows), 1) < count[0]
    cells = cell[...]
    samples = trace.shape[0]
    payload[pl.ds(0, samples), :] = jnp.where(live, trace[...], 0.0)
    payload[pl.ds(samples, 1), :] = (cells // LANES).astype(jnp.float32)
    payload[pl.ds(samples + 1, 1), :] = (cells % LANES).astype(jnp.float32)
    load_all = payload[...]
    at_x, at_y = names // n_y, lax.rem(names, n_y)
    to_a = lax.rem(at_x, half_x) * 2 + lax.rem(at_y, 2)
    to_b = (at_x // half_x) * half_y + at_y // 2
    row_to = to_a * (size_b // CAP) + to_b // CAP
    group = lax.rem(to_b, CAP).astype(jnp.float32) * CAP + slot
    spread = [jnp.where((group == float(g)) & (slot < CAP), load_all, 0.0) for g in range(CAP * CAP)]
    bundle = jnp.concatenate(spread, axis=0)
    lines = size_a * size_b // CAP
    aimed = (lax.broadcasted_iota(jnp.int32, (lines, rows), 0) == row_to).astype(jnp.float32).astype(jnp.bfloat16)
    outgoing = sum(dot_nt(aimed, piece) for piece in pieces(bundle))
    packed[...] = outgoing.reshape(size_a, size_b // CAP, 1, LANES)

    lane_row = lax.broadcasted_iota(jnp.int32, (1, LANES), 1)
    turn = lax.rem(lane_row, STRIP)
    level = lax.rem(lane_row // STRIP, depth)
    from_up = (lane_row < WINGS) & (turn >= KEPT)
    from_down = (lane_row >= WINGS) & (turn < REACH)
    below = MARGIN + width

    def by_pieces(parts, matrix):
        count = parts[0].shape[0]
        total = jnp.dot(jnp.concatenate(parts, axis=0), matrix, preferred_element_type=jnp.float32)
        return (total[2 * count :] + total[count : 2 * count]) + total[:count]

    def build_choice():
        row = lax.broadcasted_iota(jnp.int32, (LANES, LANES), 0)
        column = lax.broadcasted_iota(jnp.int32, (LANES, LANES), 1)
        high, low = lax.rem(row + KEPT, LANES), lax.rem(row + REACH, LANES)

        def block(z, _):
            first = (high < STRIP) & (column == z * STRIP + high)
            second = (low < STRIP) & (column == WINGS + z * STRIP + low)
            choice[pl.ds(z * LANES, LANES), :] = (first | second).astype(jnp.float32).astype(jnp.bfloat16)
            return 0

        lax.fori_loop(0, depth, block, 0, unroll=True)

    def build_band():
        row = lax.broadcasted_iota(jnp.int32, (LANES, LANES), 0)
        column = lax.broadcasted_iota(jnp.int32, (LANES, LANES), 1)

        def weights(away, upward):
            near, far = 24.0 * C_NEAR, -24.0 * C_FAR
            ahead = away if upward else away + 1
            value = jnp.where(ahead == 1, near, 0.0) + jnp.where(ahead == 0, -near, 0.0)
            value = value + jnp.where(ahead == 2, -far, 0.0) + jnp.where(ahead == -1, far, 0.0)
            return value.astype(jnp.bfloat16)

        for side, upward in enumerate((False, True)):
            centre = weights(row - column, upward)

            def block(z, _, side=side, upward=upward, centre=centre):
                band[side, z, pl.ds(0, LANES), :] = centre
                high = row - z * STRIP
                low = row - WINGS - z * STRIP
                place = jnp.where(
                    (high >= KEPT) & (high < STRIP),
                    high + LANES - KEPT,
                    jnp.where((low >= 0) & (low < REACH), low - REACH, 4 * LANES),
                )
                band[side, z, pl.ds(LANES, LANES), :] = weights(place - column, upward)
                return 0

            lax.fori_loop(0, depth, block, 0, unroll=True)

    def take_slopes(ref, wing, fields, start, count):
        rows_at = pl.ds(start, count)
        for k, (comp, upward) in enumerate(fields):
            edge = pieces(wing[comp, rows_at, :])

            def plane(z, _, k=k, comp=comp, upward=upward, edge=edge):
                core = pieces(ref[comp, z + ZPAD, rows_at, :])
                both = [jnp.concatenate([a, b], axis=1) for a, b in zip(core, edge)]
                slopes[k, z, rows_at, :] = by_pieces(both, band[int(upward), z]) * (1.0 / 24.0)
                return 0

            lax.fori_loop(0, depth, plane, 0, unroll=True)

    def has_corners(e):
        return e in (WIDE_SPEED, WIDE_START)

    def face_copies(e):
        strips = x_send[e].shape[1]
        count = wing_send[e].shape[0]
        tail = pl.ds(strips - count, count)
        moves = [
            (x_send[e].at[0], x_recv[e].at[0], down_x, can_down_x, can_up_x),
            (x_send[e].at[1], x_recv[e].at[1], up_x, can_up_x, can_down_x),
            (wing_send[e], wing_recv[e].at[0], down_y, can_down_y, can_up_y),
            (wing_send[e], wing_recv[e].at[1], up_y, can_up_y, can_down_y),
        ]
        if has_corners(e):
            for k, target in enumerate(corners):
                to_x, from_x = ((can_down_x, can_up_x), (can_up_x, can_down_x))[k // 2]
                to_y, from_y = ((can_down_y, can_up_y), (can_up_y, can_down_y))[k % 2]
                moves.append(
                    (x_send[e].at[k // 2, tail], corner_recv[e].at[k // 2, k % 2], target, to_x & to_y, from_x & from_y)
                )
        return [
            (
                pltpu.make_async_remote_copy(
                    src_ref=src,
                    dst_ref=dst,
                    send_sem=face_send.at[e, k],
                    recv_sem=face_recv.at[e, k],
                    device_id=target,
                    device_id_type=MESH,
                ),
                sends,
                takes,
            )
            for k, (src, dst, target, sends, takes) in enumerate(moves)
        ]

    def sent_faces(e):
        for copy, sends, _ in face_copies(e):
            pl.when(sends)(copy.wait_send)

    def pack_faces(e, x_fields, wing_fields):
        reach = x_send[e].shape[2]
        for i, (ref, comp, first) in enumerate(x_fields):
            def rows_of(z, _, i=i, ref=ref, comp=comp, first=first):
                x_send[e][0, i * depth + z] = ref[comp, z + first, pl.ds(MARGIN, reach), :]
                x_send[e][1, i * depth + z] = ref[comp, z + first, pl.ds(below - reach, reach), :]
                return 0

            lax.fori_loop(0, depth, rows_of, 0, unroll=True)
        for i, (ref, comp, first) in enumerate(wing_fields):
            planes_of = [pieces(ref[comp, z + first, inner, :]) for z in range(depth)]
            wing = by_pieces([jnp.concatenate([parts[k] for parts in planes_of], axis=1) for k in range(3)], choice[...])
            wing_send[e][i] = wing
            if has_corners(e):
                x_send[e][0, len(x_fields) * depth + i] = wing[:reach]
                x_send[e][1, len(x_fields) * depth + i] = wing[width - reach :]

    def send_faces(e):
        for copy, sends, _ in face_copies(e):
            pl.when(sends)(copy.start)

    def take_faces(e, x_fields, wing_fields):
        reach = x_send[e].shape[2]
        for copy, _, takes in face_copies(e):
            pl.when(takes)(copy.wait_recv)

        def clear(at_edge, *refs):
            @pl.when(at_edge)
            def _():
                for ref in refs:
                    ref[...] = jnp.zeros(ref.shape, jnp.float32)

        corner = corner_recv[e]
        both = has_corners(e)
        clear(gy == n_y - 1, wing_recv[e].at[0], *([corner.at[0, 0], corner.at[1, 0]] if both else []))
        clear(gy == 0, wing_recv[e].at[1], *([corner.at[0, 1], corner.at[1, 1]] if both else []))
        clear(gx == n_x - 1, x_recv[e].at[0], *([corner.at[0]] if both else []))
        clear(gx == 0, x_recv[e].at[1], *([corner.at[1]] if both else []))

        def mixed(up, down, own):
            return jnp.where(from_up, up, jnp.where(from_down, down, own))

        for i, (ref, comp, first) in enumerate(x_fields):
            def rows_of(z, _, i=i, ref=ref, comp=comp, first=first):
                ref[comp, z + first, pl.ds(below, reach), :] = x_recv[e][0, i * depth + z]
                ref[comp, z + first, pl.ds(MARGIN - reach, reach), :] = x_recv[e][1, i * depth + z]
                return 0

            lax.fori_loop(0, depth, rows_of, 0, unroll=True)
        for i, (wing, at) in enumerate(wing_fields):
            wing[at, inner, :] = mixed(wing_recv[e][0, i], wing_recv[e][1, i], wing_send[e][i])
            if both:
                for side, start in ((0, below), (1, MARGIN - reach)):
                    wing[at, pl.ds(start, reach), :] = mixed(
                        corner[side, 0, i], corner[side, 1, i], x_recv[e][side, len(x_fields) * depth + i]
                    )

    def difference(at, upward):
        if upward:
            return C_NEAR * (at(1) - at(0)) + C_FAR * (at(2) - at(-1))
        return C_NEAR * (at(0) - at(-1)) + C_FAR * (at(1) - at(-2))

    def tile_part(z, start, count):
        def along_z(ref, comp, upward):
            return difference(lambda o: ref[comp, z + ZPAD + o, pl.ds(start, count), :], upward)

        def along_x(ref, comp, upward):
            return difference(lambda o: ref[comp, z + ZPAD, pl.ds(start + o, count), :], upward)

        def along_y(ref, comp, upward):
            del upward
            return slopes[comp if ref is speed else comp - SXY, z, pl.ds(start, count), :]

        return along_x, along_y, along_z

    def wing_part(start, count):
        def held(ref, comp, o=0):
            return (speed_wing if ref is speed else tension_wing)[comp, pl.ds(start + o, count), :]

        def along_z(ref, comp, upward):
            value = held(ref, comp)

            def at(o):
                if o == 0:
                    return value
                inside = (level + o >= 0) & (level + o < depth)
                return jnp.where(inside, pltpu.roll(value, (-o * STRIP) % LANES, 1), 0.0)

            return difference(at, upward)

        def along_x(ref, comp, upward):
            return difference(lambda o: held(ref, comp, o), upward)

        def along_y(ref, comp, upward):
            value = held(ref, comp)
            return difference(lambda o: value if o == 0 else pltpu.roll(value, -o % LANES, 1), upward)

        return along_x, along_y, along_z

    def rates(along_x, along_y, along_z):
        return (
            along_x(tension, SXX, True) + along_y(tension, SXY, False) + along_z(tension, SXZ, False),
            along_x(tension, SXY, False) + along_y(tension, SYY, True) + along_z(tension, SYZ, False),
            along_x(tension, SXZ, False) + along_y(tension, SYZ, False) + along_z(tension, SZZ, True),
        )

    def strains(along_x, along_y, along_z):
        exx = along_x(speed, 0, False)
        eyy = along_y(speed, 1, False)
        ezz = along_z(speed, 2, False)
        gxy = along_y(speed, 0, True) + along_x(speed, 1, True)
        gxz = along_z(speed, 0, True) + along_x(speed, 2, True)
        gyz = along_z(speed, 1, True) + along_y(speed, 2, True)
        return exx, eyy, ezz, gxy, gxz, gyz

    def changes(strained, lame, shear):
        exx, eyy, ezz, gxy, gxz, gyz = strained
        stiff = STEP_DT * shear
        common = STEP_DT * lame * (exx + eyy + ezz)
        return (
            (SXX, common + 2.0 * stiff * exx),
            (SYY, common + 2.0 * stiff * eyy),
            (SZZ, common + 2.0 * stiff * ezz),
            (SXY, stiff * gxy),
            (SXZ, stiff * gxz),
            (SYZ, stiff * gyz),
        )

    def matrix_rows(margin):
        return (0, width + 2 * MARGIN) if margin > 0 else (MARGIN, width)

    def push_speed(margin, step, final):
        start, count = MARGIN - margin, width + 2 * margin
        take_slopes(tension, tension_wing, ((SXY, False), (SYY, True), (SYZ, False)), *matrix_rows(margin))
        rows_at = pl.ds(start, count)

        def plane(z, _):
            factor = STEP_DT * solid[BUOY, z, rows_at, :]
            for k, rate in enumerate(rates(*tile_part(z, start, count))):
                if step > 0:
                    rate = rate + source[3 * step + k, z, rows_at, :]
                value = speed[k, z + ZPAD, rows_at, :] + factor * rate
                speed[k, z + ZPAD, rows_at, :] = value
                if final:
                    vel_out[k, z] = value[margin : margin + width]
            return 0

        lax.fori_loop(0, depth, plane, 0, unroll=True)
        if margin > 0:
            factor = STEP_DT * solid_wing[BUOY, inner, :]
            for k, rate in enumerate(rates(*wing_part(MARGIN, width))):
                change = factor * (rate + source_wing[k, inner, :])
                speed_wing[k, inner, :] = speed_wing[k, inner, :] + change

    def add_source(step):
        def plane(z, _):
            factor = STEP_DT * solid[BUOY, z, inner, :]
            for k in range(3):
                speed[k, z + ZPAD, inner, :] = (
                    speed[k, z + ZPAD, inner, :] + factor * source[3 * step + k, z, inner, :]
                )
            return 0

        lax.fori_loop(0, depth, plane, 0, unroll=True)

    def push_stress(margin, final):
        start, count = MARGIN - margin, width + 2 * margin
        take_slopes(speed, speed_wing, ((0, True), (1, False), (2, True)), *matrix_rows(margin))
        rows_at = pl.ds(start, count)

        def plane(z, _):
            strained = strains(*tile_part(z, start, count))
            for comp, change in changes(strained, solid[LAME, z, rows_at, :], solid[SHEAR, z, rows_at, :]):
                value = tension[comp, z + ZPAD, rows_at, :] + change
                if final:
                    str_out[comp, z] = value
                else:
                    tension[comp, z + ZPAD, rows_at, :] = value
            if final:
                exx, eyy, ezz, gxy, gxz, gyz = strained
                f = [strain[comp, z].astype(jnp.float32) for comp in range(6)]
                a = [accel[comp, z].astype(jnp.float32) for comp in range(3)]
                v = [speed[comp, z + ZPAD, inner, :] for comp in range(3)]
                kern_out[0, z] = kern[0, z] - STEP_DT * (f[SXX] + f[SYY] + f[SZZ]) * (exx + eyy + ezz)
                kern_out[1, z] = kern[1, z] - 2.0 * STEP_DT * (
                    f[SXX] * exx + f[SYY] * eyy + f[SZZ] * ezz + f[SXY] * gxy + f[SXZ] * gxz + f[SYZ] * gyz
                )
                kern_out[2, z] = kern[2, z] - STEP_DT * (a[0] * v[0] + a[1] * v[1] + a[2] * v[2])
            return 0

        lax.fori_loop(0, depth, plane, 0, unroll=True)
        if margin > 0:
            near = margin // 2
            near_at = pl.ds(MARGIN - near, width + 2 * near)
            strained = strains(*wing_part(MARGIN - near, width + 2 * near))
            for comp, change in changes(strained, solid_wing[LAME, near_at, :], solid_wing[SHEAR, near_at, :]):
                tension_wing[comp, near_at, :] = tension_wing[comp, near_at, :] + change

    pl.semaphore_wait(barrier, size_a + size_b - 2 + len(around))

    def hop_a(i):
        to, target = partners_a[i]
        return pltpu.make_async_remote_copy(
            src_ref=packed.at[to],
            dst_ref=first_hop.at[lax.rem(my_a, CAP), :, my_a // CAP],
            send_sem=hop_send.at[0, i + 1],
            recv_sem=hop_recv.at[0, i + 1],
            device_id=target,
            device_id_type=MESH,
        )

    def hop_b(i):
        to, target = partners_b[i]
        return pltpu.make_async_remote_copy(
            src_ref=regrouped.at[to // CAP, lax.rem(to, CAP)],
            dst_ref=second_hop.at[my_b],
            send_sem=hop_send.at[1, i + 1],
            recv_sem=hop_recv.at[1, i + 1],
            device_id=target,
            device_id_type=MESH,
        )

    hops_a = [hop_a(i) for i in range(size_a - 1)]
    hops_b = [hop_b(i) for i in range(size_b - 1)]
    for copy in hops_a:
        copy.start()
    own_a = pltpu.make_async_copy(
        packed.at[my_a], first_hop.at[lax.rem(my_a, CAP), :, my_a // CAP], hop_recv.at[0, 0]
    )
    own_a.start()
    build_choice()
    loads[3].wait()
    near_x, near_y = (SXX, SXZ, SXY), (SXY, SYY, SYZ)
    near_fields = [(tension, comp, ZPAD) for comp in near_x]
    near_wings = [(tension_wing, comp) for comp in near_y]
    pack_faces(NEAR_START, near_fields, [(tension, comp, ZPAD) for comp in near_y])
    send_faces(NEAR_START)
    build_band()
    for load in loads[5:8]:
        load.wait()
    wide_fields = [(tension, comp, ZPAD) for comp in range(6)] + [(solid, comp, 0) for comp in range(3)]
    wide_wings = [(tension_wing, comp) for comp in range(6)] + [(solid_wing, comp) for comp in range(3)]
    pack_faces(WIDE_START, wide_fields, wide_fields)
    own_a.wait()
    for copy in reversed(hops_a):
        copy.wait_recv()
    heaps = [first_hop[p].reshape(lines // CAP, LANES) for p in range(CAP)]
    span = CAP * FEATURES
    lane_hop = lax.broadcasted_iota(jnp.int32, (lines // CAP, LANES), 1)
    for low in range(CAP):
        merged = None
        for p in range(CAP):
            shift = (span * (p - low)) % LANES
            turned = heaps[p] if shift == 0 else pltpu.roll(heaps[p], shift, 1)
            merged = turned if p == 0 else jnp.where(lane_hop >= span * p, turned, merged)
        regrouped[:, low] = merged.reshape(size_b // CAP, size_a // CAP, 1, LANES)
    for copy in hops_b:
        copy.start()
    own_b = pltpu.make_async_copy(
        regrouped.at[my_b // CAP, lax.rem(my_b, CAP)], second_hop.at[my_b], hop_recv.at[1, 0]
    )
    own_b.start()

    send_faces(WIDE_START)
    take_faces(NEAR_START, near_fields, near_wings)
    loads[4].wait()
    push_speed(0, 0, False)

    own_b.wait()
    for copy in reversed(hops_b):
        copy.wait_recv()
    arrived = second_hop[...].reshape(lines, LANES)
    arrived = jnp.concatenate([arrived, pltpu.roll(arrived, LANES // 2, 1)], axis=0).T
    heap = LANES // 2 // FEATURES
    values = jnp.concatenate([arrived[g * FEATURES : (g + 1) * FEATURES] for g in range(heap)], axis=1)
    entries = CAP * tiles
    row_of = lax.broadcasted_iota(jnp.int32, (depth * width, entries), 0).astype(jnp.float32)
    col_of = lax.broadcasted_iota(jnp.int32, (LANES, entries), 0).astype(jnp.float32)
    spot_rows[...] = (row_of == values[samples : samples + 1]).astype(jnp.float32).astype(jnp.bfloat16)
    spot_cols[...] = (col_of == values[samples + 1 : samples + 2]).astype(jnp.float32).astype(jnp.bfloat16)
    amounts = pieces(values)

    def lay_sources(step):
        columns = spot_cols[...]
        total = jnp.zeros((depth * width, 3 * LANES), jnp.float32)
        for amount in amounts:
            spread = [columns * amount[3 * step + k : 3 * step + k + 1, :] for k in range(3)]
            total = total + dot_nt(spot_rows[...], jnp.concatenate(spread, axis=0))
        for k in range(3):
            source[3 * step + k, :, inner, :] = total[:, k * LANES : (k + 1) * LANES].reshape(depth, width, LANES)

    lay_sources(0)
    add_source(0)
    speed_fields = [(speed, comp, ZPAD) for comp in range(3)]
    pack_faces(WIDE_SPEED, speed_fields, speed_fields)
    send_faces(WIDE_SPEED)
    lay_sources(1)
    late_fields = [(source, 3 + comp, 0) for comp in range(3)]
    pack_faces(LATE_SOURCE, late_fields, late_fields)
    send_faces(LATE_SOURCE)
    for load in loads[8:]:
        load.wait()
    take_faces(WIDE_START, wide_fields, wide_wings)
    for copy in hops_a + hops_b:
        copy.wait_send()
    for e in (NEAR_START, WIDE_START, WIDE_SPEED):
        sent_faces(e)
    take_faces(WIDE_SPEED, speed_fields, [(speed_wing, comp) for comp in range(3)])
    push_stress(4, False)
    sent_faces(LATE_SOURCE)
    take_faces(LATE_SOURCE, late_fields, [(source_wing, comp) for comp in range(3)])
    push_speed(2, 1, True)
    push_stress(0, True)


def deliver(*refs):
    sources, targets, sems = refs[:3], refs[3:6], refs[6]
    copies = [pltpu.make_async_copy(src, dst, sems.at[i]) for i, (src, dst) in enumerate(zip(sources, targets))]
    for copy in copies:
        copy.start()
    for copy in copies:
        copy.wait()


def body(
    velocity,
    stress,
    lame_first,
    shear,
    buoyancy,
    fwd_strain,
    fwd_accel,
    kernels,
    station_trace,
    station_tile,
    station_cell,
    station_count,
):
    n_x, n_y = lax.axis_size("gx"), lax.axis_size("gy")
    depth, width, lanes = buoyancy.shape
    rows = station_trace.shape[0]
    tiles = n_x * n_y
    exchanges = ((3, 2, 0), (9, 4, 1), (3, 6, 1), (3, 2, 0))
    padded = (depth + 2 * ZPAD, width + 2 * MARGIN, lanes)
    f32, b16 = jnp.float32, jnp.bfloat16
    far = pl.BlockSpec(memory_space=pltpu.HBM)
    results = pl.pallas_call(
        functools.partial(kernel, n_x, n_y),
        out_shape=[
            pltpu.VMEM(velocity.shape, f32),
            pltpu.VMEM(stress.shape, f32),
            pltpu.VMEM(kernels.shape, f32),
        ],
        in_specs=[far] * 11 + [pl.BlockSpec(memory_space=pltpu.SMEM)],
        out_specs=[pl.BlockSpec(memory_space=pltpu.VMEM)] * 3,
        scratch_shapes=[
            pltpu.VMEM((3, *padded), f32),
            pltpu.VMEM((6, *padded), f32),
            pltpu.VMEM((3, depth, *padded[1:]), f32),
            pltpu.VMEM(fwd_strain.shape, b16),
            pltpu.VMEM(fwd_accel.shape, b16),
            pltpu.VMEM(kernels.shape, f32),
            pltpu.VMEM(station_trace.shape[::-1], f32),
            pltpu.VMEM((1, rows), jnp.int32),
            pltpu.VMEM((1, rows), jnp.int32),
            pltpu.VMEM((3 * STEPS, depth, *padded[1:]), f32),
            pltpu.VMEM((FEATURES, rows), f32),
            pltpu.VMEM((n_x, n_y // CAP, 1, lanes), f32),
            pltpu.VMEM((CAP, n_y // CAP, n_x // CAP, 1, lanes), f32),
            pltpu.VMEM((n_y // CAP, CAP, n_x // CAP, 1, lanes), f32),
            pltpu.VMEM((n_y, n_x // CAP, 1, lanes), f32),
            pltpu.VMEM((depth * width, CAP * tiles), b16),
            pltpu.VMEM((lanes, CAP * tiles), b16),
            *[pltpu.VMEM((fields, *padded[1:]), f32) for fields in (3, 6, 3, 3)],
            pltpu.VMEM((2, depth, 2 * lanes, lanes), b16),
            pltpu.VMEM((depth * lanes, lanes), b16),
            pltpu.VMEM((3, depth, *padded[1:]), f32),
            *[pltpu.VMEM((2, fields * (depth + wings), reach, lanes), f32) for fields, reach, wings in exchanges],
            *[pltpu.VMEM((2, fields * (depth + wings), reach, lanes), f32) for fields, reach, wings in exchanges],
            *[pltpu.VMEM((fields, width, lanes), f32) for fields, reach, wings in exchanges],
            *[pltpu.VMEM((2, fields, width, lanes), f32) for fields, reach, wings in exchanges],
            *[pltpu.VMEM((2, 2, fields, reach, lanes), f32) for fields, reach, wings in exchanges],
            pltpu.SemaphoreType.DMA((11,)),
            pltpu.SemaphoreType.DMA((2, max(n_x, n_y))),
            pltpu.SemaphoreType.DMA((2, max(n_x, n_y))),
            pltpu.SemaphoreType.DMA((len(exchanges), 8)),
            pltpu.SemaphoreType.DMA((len(exchanges), 8)),
        ],
        compiler_params=pltpu.CompilerParams(
            collective_id=0, has_side_effects=True, vmem_limit_bytes=48 * 1024 * 1024
        ),
    )(
        *(
            pltpu.with_memory_space_constraint(array, pltpu.HBM)
            for array in (
                velocity,
                stress,
                lame_first,
                shear,
                buoyancy,
                fwd_strain,
                fwd_accel,
                kernels,
                station_trace.T,
                station_tile.reshape(1, rows),
                station_cell.reshape(1, rows),
            )
        ),
        station_count,
    )
    return pl.pallas_call(
        deliver,
        out_shape=[pltpu.HBM(array.shape, f32) for array in (velocity, stress, kernels)],
        in_specs=[pl.BlockSpec(memory_space=pltpu.VMEM)] * 3,
        out_specs=[far] * 3,
        scratch_shapes=[pltpu.SemaphoreType.DMA((3,))],
    )(*(pltpu.with_memory_space_constraint(array, pltpu.VMEM) for array in results))


def solution(mesh):
    tiled = P(None, None, "gx", "gy")
    plane = P(None, "gx", "gy")
    listed = ("gx", "gy")
    return jax.shard_map(
        body,
        mesh=mesh,
        in_specs=(
            tiled,
            tiled,
            plane,
            plane,
            plane,
            tiled,
            tiled,
            tiled,
            P(listed, None),
            P(listed, None),
            P(listed),
            P(listed),
        ),
        out_specs=(tiled, tiled, tiled),
        check_vma=False,
    )
```

```python
import functools

import jax
import jax.numpy as jnp
from jax import lax
from jax.experimental import pallas as pl
from jax.experimental.pallas import tpu as pltpu
from jax.sharding import PartitionSpec as P

STEPS = 2
CAP = 4
C_NEAR = 9.0 / 8.0
C_FAR = -1.0 / 24.0
STEP_DT = 0.25
MESH = pl.DeviceIdType.MESH

LANES = 128
FEATURES = 8
MARGIN = 8
ZPAD = 2
SXX, SXZ, SXY, SYY, SYZ, SZZ = range(6)
LAME, SHEAR, BUOY = range(3)
NEAR_START, WIDE_START, WIDE_SPEED, LATE_SOURCE = range(4)
STRIP = 10
KEPT = 4
REACH = STRIP - KEPT
WINGS = LANES // 2 - 4


def pieces(value):
    high = value.astype(jnp.bfloat16)
    rest = value - high.astype(jnp.float32)
    middle = rest.astype(jnp.bfloat16)
    low = (rest - middle.astype(jnp.float32)).astype(jnp.bfloat16)
    return high, middle, low


def dot_nt(left, right):
    return lax.dot_general(left, right, (((1,), (1,)), ((), ())), preferred_element_type=jnp.float32)


def difference(at, upward):
    if upward:
        return C_NEAR * (at(1) - at(0)) + C_FAR * (at(2) - at(-1))
    return C_NEAR * (at(0) - at(-1)) + C_FAR * (at(1) - at(-2))


def changes(strained, lame, shear):
    exx, eyy, ezz, gxy, gxz, gyz = strained
    stiff = STEP_DT * shear
    common = STEP_DT * lame * (exx + eyy + ezz)
    return (
        (SXX, common + 2.0 * stiff * exx),
        (SYY, common + 2.0 * stiff * eyy),
        (SZZ, common + 2.0 * stiff * ezz),
        (SXY, stiff * gxy),
        (SXZ, stiff * gxz),
        (SYZ, stiff * gyz),
    )


def kernel(
    n_x,
    n_y,
    vel_in,
    str_in,
    lame_in,
    shear_in,
    buoy_in,
    strain_in,
    accel_in,
    kern_in,
    trace_in,
    tile_in,
    cell_in,
    count,
    speed,
    tension,
    solid,
    strain,
    accel,
    kern,
    slopes,
    trace,
    tile,
    cell,
    source,
    payload,
    packed,
    first_hop,
    regrouped,
    second_hop,
    spot_rows,
    spot_cols,
    speed_wing,
    tension_wing,
    solid_wing,
    source_wing,
    band,
    choice,
    *rest,
):
    x_send, x_recv, wing_send, wing_recv, corner_recv = (rest[4 * i : 4 * i + 4] for i in range(5))
    in_sem, hop_send, hop_recv, face_send, face_recv = rest[20:]
    depth, width = buoy_in.shape[0], buoy_in.shape[1]
    rows = trace.shape[1]
    tiles = n_x * n_y
    gx, gy = lax.axis_index("gx"), lax.axis_index("gy")
    inner = pl.ds(MARGIN, width)
    planes = pl.ds(ZPAD, depth)

    half_x, half_y = n_x // 2, n_y // 2
    my_a = lax.rem(gx, half_x) * 2 + lax.rem(gy, 2)
    my_b = (gx // half_x) * half_y + gy // 2
    size_a, size_b = n_x, n_y

    quarter_y = n_y // 4
    high_y, low_y = gx // half_x, gy // half_y

    def around_ring(size):
        return lambda step: -min(step, size - step)

    offsets_a = [(dz, dc) for dz in sorted(range(half_x), key=around_ring(half_x)) for dc in range(2)][:-2] + [(0, 1)]
    offsets_b = sorted(
        ((dy, dx) for dy in range(4) for dx in range(quarter_y) if dy + dx > 0),
        key=lambda step: around_ring(4)(step[0]) + around_ring(quarter_y)(step[1]),
    )

    def partner_a(i):
        dz, dc = offsets_a[i]
        near = lax.rem(lax.rem(gx, half_x) + dz, half_x)
        core = lax.rem(gy + dc, 2)
        return near * 2 + core, ((gx // half_x) * half_x + near, (gy // 2) * 2 + core)

    def partner_b(i):
        dy, dx = offsets_b[i]
        line = lax.rem(high_y * 2 + low_y + dy, 4)
        spot = lax.rem(lax.rem(gy, half_y) // 2 + dx, quarter_y)
        outer = lax.rem(line, 2) * quarter_y + spot
        return (line // 2) * half_y + outer, (
            (line // 2) * half_x + lax.rem(gx, half_x),
            outer * 2 + lax.rem(gy, 2),
        )

    up_x = (lax.rem(gx + 1, n_x), gy)
    down_x = (lax.rem(gx + n_x - 1, n_x), gy)
    up_y = (gx, lax.rem(gy + 1, n_y))
    down_y = (gx, lax.rem(gy + n_y - 1, n_y))
    corners = tuple((x, y) for x in (down_x[0], up_x[0]) for y in (down_y[1], up_y[1]))
    can_down_x, can_up_x = gx > 0, gx < n_x - 1
    can_down_y, can_up_y = gy > 0, gy < n_y - 1
    around = (down_x, up_x, down_y, up_y) + corners

    barrier = pltpu.get_barrier_semaphore()

    partners_a = [partner_a(i) for i in range(size_a - 1)]
    partners_b = [partner_b(i) for i in range(size_b - 1)]
    for _, target in partners_a + partners_b:
        pl.semaphore_signal(barrier, inc=1, device_id=target, device_id_type=MESH)
    for target in around:
        pl.semaphore_signal(barrier, inc=1, device_id=target, device_id_type=MESH)

    loads = [
        pltpu.make_async_copy(src, dst, in_sem.at[i])
        for i, (src, dst) in enumerate(
            (
                (trace_in, trace),
                (tile_in, tile),
                (cell_in, cell),
                (str_in, tension.at[:, planes, inner, :]),
                (vel_in, speed.at[:, planes, inner, :]),
                (buoy_in, solid.at[BUOY, :, inner, :]),
                (lame_in, solid.at[LAME, :, inner, :]),
                (shear_in, solid.at[SHEAR, :, inner, :]),
                (strain_in, strain),
                (accel_in, accel),
                (kern_in, kern),
            )
        )
    ]
    for load in loads:
        load.start()


    blank = jnp.zeros((ZPAD, width + 2 * MARGIN, LANES), jnp.float32)
    for ref, comps in ((speed, (0, 1, 2)), (tension, (SXZ, SYZ, SZZ))):
        for comp in comps:
            ref[comp, pl.ds(0, ZPAD)] = blank
            ref[comp, pl.ds(ZPAD + depth, ZPAD)] = blank

    for load in loads[:3]:
        load.wait()
    names = tile[...]
    line = lax.broadcasted_iota(jnp.int32, (tiles, rows), 0)
    named = (line == names).astype(jnp.float32)
    named_16 = named.astype(jnp.bfloat16)
    earlier = (
        lax.broadcasted_iota(jnp.int32, (rows, rows), 0) < lax.broadcasted_iota(jnp.int32, (rows, rows), 1)
    ).astype(jnp.float32).astype(jnp.bfloat16)
    ahead = jnp.dot(named_16, earlier, preferred_element_type=jnp.float32)
    slot = jnp.sum(named * ahead, axis=0, keepdims=True)
    live = lax.broadcasted_iota(jnp.int32, (1, rows), 1) < count[0]
    cells = cell[...]
    samples = trace.shape[0]
    payload[pl.ds(0, samples), :] = jnp.where(live, trace[...], 0.0)
    payload[pl.ds(samples, 1), :] = (cells // LANES).astype(jnp.float32)
    payload[pl.ds(samples + 1, 1), :] = (cells % LANES).astype(jnp.float32)
    load_all = payload[...]
    at_x, at_y = names // n_y, lax.rem(names, n_y)
    to_a = lax.rem(at_x, half_x) * 2 + lax.rem(at_y, 2)
    to_b = (at_x // half_x) * half_y + at_y // 2
    row_to = to_a * (size_b // CAP) + to_b // CAP
    group = lax.rem(to_b, CAP).astype(jnp.float32) * CAP + slot
    spread = [jnp.where((group == float(g)) & (slot < CAP), load_all, 0.0) for g in range(CAP * CAP)]
    bundle = jnp.concatenate(spread, axis=0)
    lines = size_a * size_b // CAP
    aimed = (lax.broadcasted_iota(jnp.int32, (lines, rows), 0) == row_to).astype(jnp.float32).astype(jnp.bfloat16)
    outgoing = sum(dot_nt(aimed, piece) for piece in pieces(bundle))
    packed[...] = outgoing.reshape(size_a, size_b // CAP, 1, LANES)

    lane_row = lax.broadcasted_iota(jnp.int32, (1, LANES), 1)
    turn = lax.rem(lane_row, STRIP)
    level = lax.rem(lane_row // STRIP, depth)
    from_up = (lane_row < WINGS) & (turn >= KEPT)
    from_down = (lane_row >= WINGS) & (turn < REACH)
    below = MARGIN + width

    def by_pieces(parts, matrix):
        count = parts[0].shape[0]
        total = jnp.dot(jnp.concatenate(parts, axis=0), matrix, preferred_element_type=jnp.float32)
        return (total[2 * count :] + total[count : 2 * count]) + total[:count]

    def build_choice():
        row = lax.broadcasted_iota(jnp.int32, (LANES, LANES), 0)
        column = lax.broadcasted_iota(jnp.int32, (LANES, LANES), 1)
        high, low = lax.rem(row + KEPT, LANES), lax.rem(row + REACH, LANES)

        def block(z, _):
            first = (high < STRIP) & (column == z * STRIP + high)
            second = (low < STRIP) & (column == WINGS + z * STRIP + low)
            choice[pl.ds(z * LANES, LANES), :] = (first | second).astype(jnp.float32).astype(jnp.bfloat16)
            return 0

        lax.fori_loop(0, depth, block, 0, unroll=True)

    def build_band():
        row = lax.broadcasted_iota(jnp.int32, (LANES, LANES), 0)
        column = lax.broadcasted_iota(jnp.int32, (LANES, LANES), 1)

        def weights(away, upward):
            near, far = 24.0 * C_NEAR, -24.0 * C_FAR
            ahead = away if upward else away + 1
            value = jnp.where(ahead == 1, near, 0.0) + jnp.where(ahead == 0, -near, 0.0)
            value = value + jnp.where(ahead == 2, -far, 0.0) + jnp.where(ahead == -1, far, 0.0)
            return value.astype(jnp.bfloat16)

        for side, upward in enumerate((False, True)):
            centre = weights(row - column, upward)

            def block(z, _, side=side, upward=upward, centre=centre):
                band[side, z, pl.ds(0, LANES), :] = centre
                high = row - z * STRIP
                low = row - WINGS - z * STRIP
                place = jnp.where(
                    (high >= KEPT) & (high < STRIP),
                    high + LANES - KEPT,
                    jnp.where((low >= 0) & (low < REACH), low - REACH, 4 * LANES),
                )
                band[side, z, pl.ds(LANES, LANES), :] = weights(place - column, upward)
                return 0

            lax.fori_loop(0, depth, block, 0, unroll=True)

    def take_slopes(ref, wing, fields, start, count):
        rows_at = pl.ds(start, count)
        for k, (comp, upward) in enumerate(fields):
            edge = pieces(wing[comp, rows_at, :])

            def plane(z, _, k=k, comp=comp, upward=upward, edge=edge):
                core = pieces(ref[comp, z + ZPAD, rows_at, :])
                both = [jnp.concatenate([a, b], axis=1) for a, b in zip(core, edge)]
                slopes[k, z, rows_at, :] = by_pieces(both, band[int(upward), z]) * (1.0 / 24.0)
                return 0

            lax.fori_loop(0, depth, plane, 0, unroll=True)

    def has_corners(e):
        return e in (WIDE_SPEED, WIDE_START)

    def face_copies(e):
        strips = x_send[e].shape[1]
        count = wing_send[e].shape[0]
        tail = pl.ds(strips - count, count)
        moves = [
            (x_send[e].at[0], x_recv[e].at[0], down_x, can_down_x, can_up_x),
            (x_send[e].at[1], x_recv[e].at[1], up_x, can_up_x, can_down_x),
            (wing_send[e], wing_recv[e].at[0], down_y, can_down_y, can_up_y),
            (wing_send[e], wing_recv[e].at[1], up_y, can_up_y, can_down_y),
        ]
        if has_corners(e):
            for k, target in enumerate(corners):
                to_x, from_x = ((can_down_x, can_up_x), (can_up_x, can_down_x))[k // 2]
                to_y, from_y = ((can_down_y, can_up_y), (can_up_y, can_down_y))[k % 2]
                moves.append(
                    (x_send[e].at[k // 2, tail], corner_recv[e].at[k // 2, k % 2], target, to_x & to_y, from_x & from_y)
                )
        return [
            (
                pltpu.make_async_remote_copy(
                    src_ref=src,
                    dst_ref=dst,
                    send_sem=face_send.at[e, k],
                    recv_sem=face_recv.at[e, k],
                    device_id=target,
                    device_id_type=MESH,
                ),
                sends,
                takes,
            )
            for k, (src, dst, target, sends, takes) in enumerate(moves)
        ]

    def sent_faces(e):
        for copy, sends, _ in face_copies(e):
            pl.when(sends)(copy.wait_send)

    def pack_faces(e, x_fields, wing_fields):
        reach = x_send[e].shape[2]
        for i, (ref, comp, first) in enumerate(x_fields):
            def rows_of(z, _, i=i, ref=ref, comp=comp, first=first):
                x_send[e][0, i * depth + z] = ref[comp, z + first, pl.ds(MARGIN, reach), :]
                x_send[e][1, i * depth + z] = ref[comp, z + first, pl.ds(below - reach, reach), :]
                return 0

            lax.fori_loop(0, depth, rows_of, 0, unroll=True)
        for i, (ref, comp, first) in enumerate(wing_fields):
            planes_of = [pieces(ref[comp, z + first, inner, :]) for z in range(depth)]
            wing = by_pieces([jnp.concatenate([parts[k] for parts in planes_of], axis=1) for k in range(3)], choice[...])
            wing_send[e][i] = wing
            if has_corners(e):
                x_send[e][0, len(x_fields) * depth + i] = wing[:reach]
                x_send[e][1, len(x_fields) * depth + i] = wing[width - reach :]

    def send_faces(e):
        for copy, sends, _ in face_copies(e):
            pl.when(sends)(copy.start)

    def take_faces(e, x_fields, wing_fields):
        reach = x_send[e].shape[2]
        for copy, _, takes in face_copies(e):
            pl.when(takes)(copy.wait_recv)

        def clear(at_edge, *refs):
            @pl.when(at_edge)
            def _():
                for ref in refs:
                    ref[...] = jnp.zeros(ref.shape, jnp.float32)

        corner = corner_recv[e]
        both = has_corners(e)
        clear(gy == n_y - 1, wing_recv[e].at[0], *([corner.at[0, 0], corner.at[1, 0]] if both else []))
        clear(gy == 0, wing_recv[e].at[1], *([corner.at[0, 1], corner.at[1, 1]] if both else []))
        clear(gx == n_x - 1, x_recv[e].at[0], *([corner.at[0]] if both else []))
        clear(gx == 0, x_recv[e].at[1], *([corner.at[1]] if both else []))

        def mixed(up, down, own):
            return jnp.where(from_up, up, jnp.where(from_down, down, own))

        for i, (ref, comp, first) in enumerate(x_fields):
            def rows_of(z, _, i=i, ref=ref, comp=comp, first=first):
                ref[comp, z + first, pl.ds(below, reach), :] = x_recv[e][0, i * depth + z]
                ref[comp, z + first, pl.ds(MARGIN - reach, reach), :] = x_recv[e][1, i * depth + z]
                return 0

            lax.fori_loop(0, depth, rows_of, 0, unroll=True)
        for i, (wing, at) in enumerate(wing_fields):
            wing[at, inner, :] = mixed(wing_recv[e][0, i], wing_recv[e][1, i], wing_send[e][i])
            if both:
                for side, start in ((0, below), (1, MARGIN - reach)):
                    wing[at, pl.ds(start, reach), :] = mixed(
                        corner[side, 0, i], corner[side, 1, i], x_recv[e][side, len(x_fields) * depth + i]
                    )

    def tile_part(z, start, count):
        def along_z(ref, comp, upward):
            return difference(lambda o: ref[comp, z + ZPAD + o, pl.ds(start, count), :], upward)

        def along_x(ref, comp, upward):
            return difference(lambda o: ref[comp, z + ZPAD, pl.ds(start + o, count), :], upward)

        def along_y(ref, comp, upward):
            del upward
            return slopes[comp if ref is speed else comp - SXY, z, pl.ds(start, count), :]

        return along_x, along_y, along_z

    def wing_part(start, count):
        def held(ref, comp, o=0):
            return (speed_wing if ref is speed else tension_wing)[comp, pl.ds(start + o, count), :]

        def along_z(ref, comp, upward):
            value = held(ref, comp)

            def at(o):
                if o == 0:
                    return value
                inside = (level + o >= 0) & (level + o < depth)
                return jnp.where(inside, pltpu.roll(value, (-o * STRIP) % LANES, 1), 0.0)

            return difference(at, upward)

        def along_x(ref, comp, upward):
            return difference(lambda o: held(ref, comp, o), upward)

        def along_y(ref, comp, upward):
            value = held(ref, comp)
            return difference(lambda o: value if o == 0 else pltpu.roll(value, -o % LANES, 1), upward)

        return along_x, along_y, along_z

    def rates(along_x, along_y, along_z):
        return (
            along_x(tension, SXX, True) + along_y(tension, SXY, False) + along_z(tension, SXZ, False),
            along_x(tension, SXY, False) + along_y(tension, SYY, True) + along_z(tension, SYZ, False),
            along_x(tension, SXZ, False) + along_y(tension, SYZ, False) + along_z(tension, SZZ, True),
        )

    def strains(along_x, along_y, along_z):
        exx = along_x(speed, 0, False)
        eyy = along_y(speed, 1, False)
        ezz = along_z(speed, 2, False)
        gxy = along_y(speed, 0, True) + along_x(speed, 1, True)
        gxz = along_z(speed, 0, True) + along_x(speed, 2, True)
        gyz = along_z(speed, 1, True) + along_y(speed, 2, True)
        return exx, eyy, ezz, gxy, gxz, gyz

    def matrix_rows(margin):
        return (0, width + 2 * MARGIN) if margin > 0 else (MARGIN, width)

    def push_speed(margin, step):
        start, count = MARGIN - margin, width + 2 * margin
        take_slopes(tension, tension_wing, ((SXY, False), (SYY, True), (SYZ, False)), *matrix_rows(margin))
        rows_at = pl.ds(start, count)

        def plane(z, _):
            factor = STEP_DT * solid[BUOY, z, rows_at, :]
            for k, rate in enumerate(rates(*tile_part(z, start, count))):
                if step > 0:
                    rate = rate + source[3 * step + k, z, rows_at, :]
                value = speed[k, z + ZPAD, rows_at, :] + factor * rate
                speed[k, z + ZPAD, rows_at, :] = value
            return 0

        lax.fori_loop(0, depth, plane, 0, unroll=True)
        if margin > 0:
            factor = STEP_DT * solid_wing[BUOY, inner, :]
            for k, rate in enumerate(rates(*wing_part(MARGIN, width))):
                change = factor * (rate + source_wing[k, inner, :])
                speed_wing[k, inner, :] = speed_wing[k, inner, :] + change

    def add_source(step):
        def plane(z, _):
            factor = STEP_DT * solid[BUOY, z, inner, :]
            for k in range(3):
                speed[k, z + ZPAD, inner, :] = (
                    speed[k, z + ZPAD, inner, :] + factor * source[3 * step + k, z, inner, :]
                )
            return 0

        lax.fori_loop(0, depth, plane, 0, unroll=True)

    def push_stress(margin):
        start, count = MARGIN - margin, width + 2 * margin
        take_slopes(speed, speed_wing, ((0, True), (1, False), (2, True)), *matrix_rows(margin))
        rows_at = pl.ds(start, count)

        def plane(z, _):
            strained = strains(*tile_part(z, start, count))
            for comp, change in changes(strained, solid[LAME, z, rows_at, :], solid[SHEAR, z, rows_at, :]):
                value = tension[comp, z + ZPAD, rows_at, :] + change
                tension[comp, z + ZPAD, rows_at, :] = value
            return 0

        lax.fori_loop(0, depth, plane, 0, unroll=True)
        if margin > 0:
            near = margin // 2
            near_at = pl.ds(MARGIN - near, width + 2 * near)
            strained = strains(*wing_part(MARGIN - near, width + 2 * near))
            for comp, change in changes(strained, solid_wing[LAME, near_at, :], solid_wing[SHEAR, near_at, :]):
                tension_wing[comp, near_at, :] = tension_wing[comp, near_at, :] + change

    pl.semaphore_wait(barrier, size_a + size_b - 2 + len(around))

    def hop_a(i):
        to, target = partners_a[i]
        return pltpu.make_async_remote_copy(
            src_ref=packed.at[to],
            dst_ref=first_hop.at[lax.rem(my_a, CAP), :, my_a // CAP],
            send_sem=hop_send.at[0, i + 1],
            recv_sem=hop_recv.at[0, i + 1],
            device_id=target,
            device_id_type=MESH,
        )

    def hop_b(i):
        to, target = partners_b[i]
        return pltpu.make_async_remote_copy(
            src_ref=regrouped.at[to // CAP, lax.rem(to, CAP)],
            dst_ref=second_hop.at[my_b],
            send_sem=hop_send.at[1, i + 1],
            recv_sem=hop_recv.at[1, i + 1],
            device_id=target,
            device_id_type=MESH,
        )

    hops_a = [hop_a(i) for i in range(size_a - 1)]
    hops_b = [hop_b(i) for i in range(size_b - 1)]
    for copy in hops_a:
        copy.start()
    own_a = pltpu.make_async_copy(
        packed.at[my_a], first_hop.at[lax.rem(my_a, CAP), :, my_a // CAP], hop_recv.at[0, 0]
    )
    own_a.start()
    build_choice()
    loads[3].wait()
    near_x, near_y = (SXX, SXZ, SXY), (SXY, SYY, SYZ)
    near_fields = [(tension, comp, ZPAD) for comp in near_x]
    near_wings = [(tension_wing, comp) for comp in near_y]
    pack_faces(NEAR_START, near_fields, [(tension, comp, ZPAD) for comp in near_y])
    send_faces(NEAR_START)
    build_band()
    for load in loads[5:8]:
        load.wait()
    wide_fields = [(tension, comp, ZPAD) for comp in range(6)] + [(solid, comp, 0) for comp in range(3)]
    wide_wings = [(tension_wing, comp) for comp in range(6)] + [(solid_wing, comp) for comp in range(3)]
    pack_faces(WIDE_START, wide_fields, wide_fields)
    own_a.wait()
    for copy in reversed(hops_a):
        copy.wait_recv()
    heaps = [first_hop[p].reshape(lines // CAP, LANES) for p in range(CAP)]
    span = CAP * FEATURES
    lane_hop = lax.broadcasted_iota(jnp.int32, (lines // CAP, LANES), 1)
    for low in range(CAP):
        merged = None
        for p in range(CAP):
            shift = (span * (p - low)) % LANES
            turned = heaps[p] if shift == 0 else pltpu.roll(heaps[p], shift, 1)
            merged = turned if p == 0 else jnp.where(lane_hop >= span * p, turned, merged)
        regrouped[:, low] = merged.reshape(size_b // CAP, size_a // CAP, 1, LANES)
    for copy in hops_b:
        copy.start()
    own_b = pltpu.make_async_copy(
        regrouped.at[my_b // CAP, lax.rem(my_b, CAP)], second_hop.at[my_b], hop_recv.at[1, 0]
    )
    own_b.start()

    send_faces(WIDE_START)
    take_faces(NEAR_START, near_fields, near_wings)
    loads[4].wait()
    push_speed(0, 0)

    own_b.wait()
    for copy in reversed(hops_b):
        copy.wait_recv()
    arrived = second_hop[...].reshape(lines, LANES)
    arrived = jnp.concatenate([arrived, pltpu.roll(arrived, LANES // 2, 1)], axis=0).T
    heap = LANES // 2 // FEATURES
    values = jnp.concatenate([arrived[g * FEATURES : (g + 1) * FEATURES] for g in range(heap)], axis=1)
    entries = CAP * tiles
    row_of = lax.broadcasted_iota(jnp.int32, (depth * width, entries), 0).astype(jnp.float32)
    col_of = lax.broadcasted_iota(jnp.int32, (LANES, entries), 0).astype(jnp.float32)
    spot_rows[...] = (row_of == values[samples : samples + 1]).astype(jnp.float32).astype(jnp.bfloat16)
    spot_cols[...] = (col_of == values[samples + 1 : samples + 2]).astype(jnp.float32).astype(jnp.bfloat16)
    amounts = pieces(values)

    def lay_sources(step):
        columns = spot_cols[...]
        total = jnp.zeros((depth * width, 3 * LANES), jnp.float32)
        for amount in amounts:
            spread = [columns * amount[3 * step + k : 3 * step + k + 1, :] for k in range(3)]
            total = total + dot_nt(spot_rows[...], jnp.concatenate(spread, axis=0))
        for k in range(3):
            source[3 * step + k, :, inner, :] = total[:, k * LANES : (k + 1) * LANES].reshape(depth, width, LANES)

    lay_sources(0)
    add_source(0)
    speed_fields = [(speed, comp, ZPAD) for comp in range(3)]
    pack_faces(WIDE_SPEED, speed_fields, speed_fields)
    send_faces(WIDE_SPEED)
    lay_sources(1)
    late_fields = [(source, 3 + comp, 0) for comp in range(3)]
    pack_faces(LATE_SOURCE, late_fields, late_fields)
    send_faces(LATE_SOURCE)
    for load in loads[8:]:
        load.wait()
    take_faces(WIDE_START, wide_fields, wide_wings)
    for copy in hops_a + hops_b:
        copy.wait_send()
    for e in (NEAR_START, WIDE_START, WIDE_SPEED):
        sent_faces(e)
    take_faces(WIDE_SPEED, speed_fields, [(speed_wing, comp) for comp in range(3)])
    push_stress(4)
    sent_faces(LATE_SOURCE)
    take_faces(LATE_SOURCE, late_fields, [(source_wing, comp) for comp in range(3)])
    push_speed(2, 1)
    take_slopes(speed, speed_wing, ((0, True), (1, False), (2, True)), *matrix_rows(0))


def finish(speed, tension, solid, strain, accel, kern, slopes, vel_out, str_out, kern_out, str_new, kern_new, vel_sem, plane_sem):
    depth, width = kern.shape[1], kern.shape[2]
    inner = pl.ds(MARGIN, width)
    speed_copy = pltpu.make_async_copy(speed.at[:, pl.ds(ZPAD, depth), inner, :], vel_out, vel_sem.at[0])
    speed_copy.start()
    copies = []
    for z in range(depth):

        def along_z(comp, upward, z=z):
            return difference(lambda o: speed[comp, z + ZPAD + o, inner, :], upward)

        def along_x(comp, upward, z=z):
            return difference(lambda o: speed[comp, z + ZPAD, pl.ds(MARGIN + o, width), :], upward)

        exx, eyy, ezz = along_x(0, False), slopes[1, z, inner, :], along_z(2, False)
        gxy = slopes[0, z, inner, :] + along_x(1, True)
        gxz = along_z(0, True) + along_x(2, True)
        gyz = along_z(1, True) + slopes[2, z, inner, :]
        strained = (exx, eyy, ezz, gxy, gxz, gyz)
        for comp, change in changes(strained, solid[LAME, z, inner, :], solid[SHEAR, z, inner, :]):
            str_new[comp, z] = tension[comp, z + ZPAD, inner, :] + change
        f = [strain[comp, z].astype(jnp.float32) for comp in range(6)]
        a = [accel[comp, z].astype(jnp.float32) for comp in range(3)]
        v = [speed[comp, z + ZPAD, inner, :] for comp in range(3)]
        kern_new[0, z] = kern[0, z] - STEP_DT * (f[SXX] + f[SYY] + f[SZZ]) * (exx + eyy + ezz)
        kern_new[1, z] = kern[1, z] - 2.0 * STEP_DT * (
            f[SXX] * exx + f[SYY] * eyy + f[SZZ] * ezz + f[SXY] * gxy + f[SXZ] * gxz + f[SYZ] * gyz
        )
        kern_new[2, z] = kern[2, z] - STEP_DT * (a[0] * v[0] + a[1] * v[1] + a[2] * v[2])
        copies.append(pltpu.make_async_copy(str_new.at[:, z], str_out.at[:, z], plane_sem.at[0, z]))
        copies.append(pltpu.make_async_copy(kern_new.at[:, z], kern_out.at[:, z], plane_sem.at[1, z]))
        for copy in copies[-2:]:
            copy.start()
    speed_copy.wait()
    for copy in copies:
        copy.wait()


def body(
    velocity,
    stress,
    lame_first,
    shear,
    buoyancy,
    fwd_strain,
    fwd_accel,
    kernels,
    station_trace,
    station_tile,
    station_cell,
    station_count,
):
    n_x, n_y = lax.axis_size("gx"), lax.axis_size("gy")
    depth, width, lanes = buoyancy.shape
    rows = station_trace.shape[0]
    tiles = n_x * n_y
    exchanges = ((3, 2, 0), (9, 4, 1), (3, 6, 1), (3, 2, 0))
    padded = (depth + 2 * ZPAD, width + 2 * MARGIN, lanes)
    f32, b16 = jnp.float32, jnp.bfloat16
    far = pl.BlockSpec(memory_space=pltpu.HBM)
    results = pl.pallas_call(
        functools.partial(kernel, n_x, n_y),
        out_shape=[
            pltpu.VMEM((3, *padded), f32),
            pltpu.VMEM((6, *padded), f32),
            pltpu.VMEM((3, depth, *padded[1:]), f32),
            pltpu.VMEM(fwd_strain.shape, b16),
            pltpu.VMEM(fwd_accel.shape, b16),
            pltpu.VMEM(kernels.shape, f32),
            pltpu.VMEM((3, depth, *padded[1:]), f32),
        ],
        in_specs=[far] * 11 + [pl.BlockSpec(memory_space=pltpu.SMEM)],
        out_specs=[pl.BlockSpec(memory_space=pltpu.VMEM)] * 7,
        scratch_shapes=[
            pltpu.VMEM(station_trace.shape[::-1], f32),
            pltpu.VMEM((1, rows), jnp.int32),
            pltpu.VMEM((1, rows), jnp.int32),
            pltpu.VMEM((3 * STEPS, depth, *padded[1:]), f32),
            pltpu.VMEM((FEATURES, rows), f32),
            pltpu.VMEM((n_x, n_y // CAP, 1, lanes), f32),
            pltpu.VMEM((CAP, n_y // CAP, n_x // CAP, 1, lanes), f32),
            pltpu.VMEM((n_y // CAP, CAP, n_x // CAP, 1, lanes), f32),
            pltpu.VMEM((n_y, n_x // CAP, 1, lanes), f32),
            pltpu.VMEM((depth * width, CAP * tiles), b16),
            pltpu.VMEM((lanes, CAP * tiles), b16),
            *[pltpu.VMEM((fields, *padded[1:]), f32) for fields in (3, 6, 3, 3)],
            pltpu.VMEM((2, depth, 2 * lanes, lanes), b16),
            pltpu.VMEM((depth * lanes, lanes), b16),
            *[pltpu.VMEM((2, fields * (depth + wings), reach, lanes), f32) for fields, reach, wings in exchanges],
            *[pltpu.VMEM((2, fields * (depth + wings), reach, lanes), f32) for fields, reach, wings in exchanges],
            *[pltpu.VMEM((fields, width, lanes), f32) for fields, reach, wings in exchanges],
            *[pltpu.VMEM((2, fields, width, lanes), f32) for fields, reach, wings in exchanges],
            *[pltpu.VMEM((2, 2, fields, reach, lanes), f32) for fields, reach, wings in exchanges],
            pltpu.SemaphoreType.DMA((11,)),
            pltpu.SemaphoreType.DMA((2, max(n_x, n_y))),
            pltpu.SemaphoreType.DMA((2, max(n_x, n_y))),
            pltpu.SemaphoreType.DMA((len(exchanges), 8)),
            pltpu.SemaphoreType.DMA((len(exchanges), 8)),
        ],
        compiler_params=pltpu.CompilerParams(
            collective_id=0, has_side_effects=True, vmem_limit_bytes=32 * 1024 * 1024
        ),
    )(
        *(
            pltpu.with_memory_space_constraint(array, pltpu.HBM)
            for array in (
                velocity,
                stress,
                lame_first,
                shear,
                buoyancy,
                fwd_strain,
                fwd_accel,
                kernels,
                station_trace.T,
                station_tile.reshape(1, rows),
                station_cell.reshape(1, rows),
            )
        ),
        station_count,
    )
    return pl.pallas_call(
        finish,
        out_shape=[pltpu.HBM(array.shape, f32) for array in (velocity, stress, kernels)],
        in_specs=[pl.BlockSpec(memory_space=pltpu.VMEM)] * 7,
        out_specs=[far] * 3,
        scratch_shapes=[
            pltpu.VMEM(stress.shape, f32),
            pltpu.VMEM(kernels.shape, f32),
            pltpu.SemaphoreType.DMA((1,)),
            pltpu.SemaphoreType.DMA((2, depth)),
        ],
        compiler_params=pltpu.CompilerParams(vmem_limit_bytes=16 * 1024 * 1024),
    )(*(pltpu.with_memory_space_constraint(array, pltpu.VMEM) for array in results))


def solution(mesh):
    tiled = P(None, None, "gx", "gy")
    plane = P(None, "gx", "gy")
    listed = ("gx", "gy")
    return jax.shard_map(
        body,
        mesh=mesh,
        in_specs=(
            tiled,
            tiled,
            plane,
            plane,
            plane,
            tiled,
            tiled,
            tiled,
            P(listed, None),
            P(listed, None),
            P(listed),
            P(listed),
        ),
        out_specs=(tiled, tiled, tiled),
        check_vma=False,
    )
```
